32 devices in a mesh: page: 4 (over x, core), blk: 8 (over z, y).
Axes of the slice: x: 2, y: 2, z: 4, core: 2. Of those that a mesh axis runs over, the one named last changes fastest.
Arguments:
- visual_in: bfloat16 [4608, 768], P(('page', 'blk')), may hold values from -6 to 6
- question_in: bfloat16 [4096, 768], P('page'), may hold values from -6 to 6
- segment_ids: int32 [4, 1024], P('page'), may hold values from 0 to 5, never falling along the last dimension, each value on 1 to 512 neighbouring positions
- regions: int32 [4608], P(('page', 'blk')), may hold values from 0 to 3
- rel_index: int32 [144, 144], replicated, may hold values from 0 to 528
- rel_table: float32 [12, 529], replicated, may hold values from -3 to 3
- window_project: bfloat16 [1769472], P(('page', 'blk')), may hold values from -0.21875 to 0.21875
- window_output: bfloat16 [589824], P(('page', 'blk')), may hold values from -0.875 to 0.875
- causal_project: bfloat16 [1769472], P(('page', 'blk')), may hold values from -0.21875 to 0.21875
- causal_output: bfloat16 [589824], P(('page', 'blk')), may hold values from -1.25 to 1.25
- reader_query: bfloat16 [589824], P(('page', 'blk')), may hold values from -0.4375 to 0.4375
- reader_pair: bfloat16 [1179648], P(('page', 'blk')), may hold values from -0.21875 to 0.21875
- reader_output: bfloat16 [589824], P(('page', 'blk')), may hold values from -1.75 to 1.75
- viewer_query: bfloat16 [589824], P(('page', 'blk')), may hold values from -0.3125 to 0.3125
- viewer_pair: bfloat16 [1179648], P(('page', 'blk')), may hold values from -0.21875 to 0.21875
- viewer_output: bfloat16 [589824], P(('page', 'blk')), may hold values from -1.75 to 1.75
- visual_up: bfloat16 [2359296], P(('page', 'blk')), may hold values from -0.21875 to 0.21875
- visual_down: bfloat16 [2359296], P(('page', 'blk')), may hold values from -0.15625 to 0.15625
- question_up: bfloat16 [2359296], P(('page', 'blk')), may hold values from -0.21875 to 0.21875
- question_down: bfloat16 [2359296], P(('page', 'blk')), may hold values from -0.15625 to 0.15625
- norm_gains: bfloat16 [4608], P(('page', 'blk')), may hold values from 0.5 to 1.5
- norm_shifts: bfloat16 [4608], P(('page', 'blk')), may hold values from -1 to 1
- visual_cot: bfloat16 [4608, 768], P(('page', 'blk')), may hold values from -6 to 6
- question_cot: bfloat16 [4096, 768], P('page'), may hold values from -6 to 6
Outputs:
- visual_out: bfloat16 [4608, 768], P(('page', 'blk'))
- question_out: bfloat16 [4096, 768], P('page')
- visual_delta: float32 [4608, 768], P(('page', 'blk'))
- question_delta: float32 [4096, 768], P('page')
- table_delta: float32 [12, 529], replicated
- delta_window_project: float32 [1769472], P(('page', 'blk'))
- delta_window_output: float32 [589824], P(('page', 'blk'))
- delta_causal_project: float32 [1769472], P(('page', 'blk'))
- delta_causal_output: float32 [589824], P(('page', 'blk'))
- delta_reader_query: float32 [589824], P(('page', 'blk'))
- delta_reader_pair: float32 [1179648], P(('page', 'blk'))
- delta_reader_output: float32 [589824], P(('page', 'blk'))
- delta_viewer_query: float32 [589824], P(('page', 'blk'))
- delta_viewer_pair: float32 [1179648], P(('page', 'blk'))
- delta_viewer_output: float32 [589824], P(('page', 'blk'))
- delta_visual_up: float32 [2359296], P(('page', 'blk'))
- delta_visual_down: float32 [2359296], P(('page', 'blk'))
- delta_question_up: float32 [2359296], P(('page', 'blk'))
- delta_question_down: float32 [2359296], P(('page', 'blk'))
- delta_norm_gains: float32 [4608], P(('page', 'blk'))
- delta_norm_shifts: float32 [4608], P(('page', 'blk'))
- delta_question_shift: float32 [768], replicated
The draws below stay inside these ranges and needn't reach their ends.
Inputs may be any that keep to these rules, and one draw needn't show every extreme that they name: `segment_ids`: within a page question numbers never fall along the tokens, each question has 1 to 512 tokens and one has exactly that many.
All inputs are finite; a program needn't handle non-finite values.
Results may differ from the reference program's by a relative error of at most 0.025.
Values may be sent and summed in bfloat16 or wider, within the bound.
No kernel may reach another device: no remote copies, remote signals or barrier semaphores. Data moves between devices by JAX's collectives and lax.ppermute only.
A program may use at most 384 MiB of HBM per device.

```python
import math
import jax
import jax.numpy as jnp
import numpy as np
from jax import lax

D = 768
HEADS = 12
HEAD_DIM = 64
FF = 3072
Q_LEN = 1024
QUESTIONS = 6
WIN = 144
RELS = 529
NV = 4608
QUERIES = 4096
N_PAGE = 4
N_BLK = 8


def plant(values, own_key, low, high):
    shape = values.shape
    spot = [jax.random.randint(jax.random.fold_in(own_key, axis), (), 0, shape[axis]) for axis in range(len(shape))]
    values = values.at[tuple(spot)].set(low)
    longest = shape.index(max(shape))
    spot[longest] = (spot[longest] + 1) % shape[longest]
    return values.at[tuple(spot)].set(high)


def block_levels(rng, extent, cuts, low, largest):
    def one(dim, blocks):
        steps = jax.random.uniform(jax.random.fold_in(jax.random.fold_in(rng, 6), dim), (blocks,), jnp.float32, low / len(cuts), largest / len(cuts))
        return jnp.repeat(jnp.exp(steps), extent[dim] // blocks).reshape((-1,) + (1,) * (len(extent) - dim - 1))

    level = one(*cuts[0])
    for cut in cuts[1:]:
        level = level * one(*cut)
    return level


def split_up(amount, total, most, lean):
    loads = [(1 << 20) // math.isqrt(standing ** lean) + 1 for standing in range(2, amount + 1)]
    spare, given = total - most - (amount - 1), [1] * (amount - 1)
    while spare > 0:
        free = [i for i in range(amount - 1) if given[i] < most]
        whole, remaining = sum([loads[i] for i in free]), spare
        for i in free:
            more = min(most - given[i], max(1, remaining * loads[i] // whole), spare)
            given[i] = given[i] + more
            spare = spare - more
    return np.array([most] + given)


def ragged_sizes(rng, number_of, total, most, lean):
    if number_of == 2:
        one = jax.random.randint(rng, (), max(1, total - most), min(most, total - 1) + 1)
        return jnp.stack([one, total - one])
    lengths = jnp.asarray(split_up(number_of, total, most, lean), jnp.int32)
    couples = (number_of - 1) // 2
    source_of, receiver = lengths[1:1 + 2 * couples:2], lengths[2:2 + 2 * couples:2]
    room = jnp.minimum(source_of - 1, most - receiver)
    shifted = jax.random.randint(jax.random.fold_in(rng, 1), (couples,), 0, 1 << 20) % (room + 1)
    lengths = lengths.at[1:1 + 2 * couples:2].set(source_of - shifted).at[2:2 + 2 * couples:2].set(receiver + shifted)
    return lengths[jax.random.permutation(jax.random.fold_in(rng, 2), number_of)]


def bell_draw(rng, dims, scale, reach, shards=(), kind=jnp.bfloat16):
    values = scale * jax.random.normal(rng, dims, jnp.float32)
    if shards:
        values = values * block_levels(rng, dims, shards, -0.22, 0.18)
    return jnp.clip(values, -reach, reach).astype(kind)


def setup_inputs(seed: int = 0) -> dict:
    splits = jax.random.split(jax.random.key(seed), 25)
    return {
        "visual_in": bell_draw(splits[0], (NV, D), 1.0, 6.0, ((0, 32),)),
        "question_in": bell_draw(splits[1], (QUERIES, D), 1.0, 6.0, ((0, 4),)),
        "segment_ids": jax.vmap(lambda own: jnp.searchsorted(jnp.cumsum(ragged_sizes(own, QUESTIONS, Q_LEN, Q_LEN // 2, 0)), jnp.arange(Q_LEN), side="right"))(jax.random.split(splits[2], N_PAGE)).reshape((N_PAGE, Q_LEN)).astype(jnp.int32),
        "regions": plant(jax.random.randint(splits[3], (NV,), 0, 4), jax.random.fold_in(splits[3], 1), 0, 3).astype(jnp.int32),
        "rel_index": plant(jax.random.randint(splits[4], (WIN, WIN), 0, RELS), jax.random.fold_in(splits[4], 1), 0, RELS - 1).astype(jnp.int32),
        "rel_table": bell_draw(splits[5], (HEADS, RELS), 0.5, 3.0, (), jnp.float32),
        "window_project": bell_draw(splits[6], (3 * D * D,), D ** -0.5, 0.21875, ((0, 32),)),
        "window_output": bell_draw(splits[7], (D * D,), (D // 16) ** -0.5, 0.875, ((0, 32),)),
        "causal_project": bell_draw(splits[8], (3 * D * D,), D ** -0.5, 0.21875, ((0, 32),)),
        "causal_output": bell_draw(splits[9], (D * D,), (D // 32) ** -0.5, 1.25, ((0, 32),)),
        "reader_query": bell_draw(splits[10], (D * D,), (D // 4) ** -0.5, 0.4375, ((0, 32),)),
        "reader_pair": bell_draw(splits[11], (2 * D * D,), D ** -0.5, 0.21875, ((0, 32),)),
        "reader_output": bell_draw(splits[12], (D * D,), (D // 64) ** -0.5, 1.75, ((0, 32),)),
        "viewer_query": bell_draw(splits[13], (D * D,), (D // 2) ** -0.5, 0.3125, ((0, 32),)),
        "viewer_pair": bell_draw(splits[14], (2 * D * D,), D ** -0.5, 0.21875, ((0, 32),)),
        "viewer_output": bell_draw(splits[15], (D * D,), (D // 64) ** -0.5, 1.75, ((0, 32),)),
        "visual_up": bell_draw(splits[16], (D * FF,), D ** -0.5, 0.21875, ((0, 32),)),
        "visual_down": bell_draw(splits[17], (FF * D,), (FF // 2) ** -0.5, 0.15625, ((0, 32),)),
        "question_up": bell_draw(splits[18], (D * FF,), D ** -0.5, 0.21875, ((0, 32),)),
        "question_down": bell_draw(splits[19], (FF * D,), (FF // 2) ** -0.5, 0.15625, ((0, 32),)),
        "norm_gains": jnp.clip(1.0 + 0.1 * jax.random.normal(splits[20], (6 * D,), jnp.float32), 0.5, 1.5).astype(jnp.bfloat16),
        "norm_shifts": bell_draw(splits[21], (6 * D,), 0.2, 1.0, ((0, 32),)),
        "visual_cot": bell_draw(splits[22], (NV, D), 1.0, 6.0, ((0, 32),)),
        "question_cot": bell_draw(splits[23], (QUERIES, D), 1.0, 6.0, ((0, 4),)),
    }


EPS = 1e-05
NEG = -1000000000.0
HIGH = lax.Precision.HIGHEST

@jax.custom_vjp
def low(v):
    return lax.optimization_barrier(v.astype(jnp.bfloat16)).astype(jnp.float32)

@jax.custom_vjp
def low_back(v):
    return v

def low_keep(v):
    return (low(v), None)

def low_pass(kept, grad):
    return (grad,)

def back_keep(v):
    return (v, None)

def back_low(kept, grad):
    return (low(grad),)
low.defvjp(low_keep, low_pass)
low_back.defvjp(back_keep, back_low)

def matrix_shapes():
    return ((D, 3 * D), (D, D), (D, 3 * D), (D, D), (D, D), (D, 2 * D), (D, D), (D, D), (D, 2 * D), (D, D), (D, FF), (FF, D), (D, FF), (FF, D), (6, D), (6, D))

def matmul(left, right):
    return jnp.dot(left, right, precision=HIGH)

def normalize(rows, gain, shift):
    mean = lax.optimization_barrier(jnp.mean(rows, axis=-1, keepdims=True))
    centred = rows - mean
    spread = lax.optimization_barrier(jnp.mean(centred * centred, axis=-1, keepdims=True))
    return centred * lax.rsqrt(spread + EPS) * gain + shift

def split_heads(rows):
    return rows.reshape(rows.shape[0], HEADS, HEAD_DIM)

def attend(queries, keys, values, extra):
    scores = low_back(jnp.einsum('nhe,mhe->hnm', queries, keys, precision=HIGH) * HEAD_DIM ** (-0.5) + extra)
    shares = low(jax.nn.softmax(scores, axis=-1))
    output = jnp.einsum('hnm,mhe->nhe', shares, values, precision=HIGH)
    return low_back(low(output.reshape(output.shape[0], -1)))

def feed_forward(rows, gain, shift, up_weight, down_weight):
    normed = low(normalize(rows, gain, shift))
    upward = low_back(matmul(normed, up_weight))
    active = low(jax.nn.gelu(upward, approximate=False))
    return rows + low_back(matmul(active, down_weight))

def page_forward(visual, question, segments, labels, weights, table, rel_index):
    window_project, window_output, causal_project, causal_output, reader_query, reader_pair, reader_output, viewer_query, viewer_pair, viewer_output, visual_up, visual_down, question_up, question_down, gains, shifts = weights
    bias = table[:, rel_index]

    def window_block(block):
        rows, marks = block
        normed = low(normalize(rows, gains[0], shifts[0]))
        project = low_back(low(matmul(normed, window_project)))
        count = rows.shape[0] // WIN

        def as_windows(part):
            return part.reshape(count, WIN, HEADS, HEAD_DIM)
        marks = marks.reshape(count, WIN)
        extra = bias[None] + jnp.where(marks[:, :, None] == marks[:, None, :], 0.0, NEG)[:, None]
        output = jax.vmap(attend)(as_windows(project[:, :D]), as_windows(project[:, D:2 * D]), as_windows(project[:, 2 * D:]), extra)
        return rows + low_back(matmul(output.reshape(-1, D), window_output))
    visual_one = lax.map(jax.checkpoint(window_block), (visual.reshape(N_BLK, -1, D), labels.reshape(N_BLK, -1))).reshape(-1, D)
    normed = low(normalize(question, gains[1], shifts[1]))
    project = low_back(low(matmul(normed, causal_project)))
    place = jnp.arange(Q_LEN)
    allowed = (segments[:, None] == segments[None, :]) & (place[None, :] <= place[:, None])
    extra = jnp.where(allowed, 0.0, NEG)[None]
    attended = attend(split_heads(project[:, :D]), split_heads(project[:, D:2 * D]), split_heads(project[:, 2 * D:]), extra)
    question_one = question + low_back(matmul(attended, causal_output))
    cross_question = low(normalize(question_one, gains[2], shifts[2]))
    cross_visual = low(normalize(visual_one, gains[3], shifts[3]))
    reader_rows = low_back(low(matmul(cross_question, reader_query)))
    reader_keys = low_back(low(matmul(cross_visual, reader_pair)))

    def key_block(pair):
        scores = low_back(jnp.einsum('nhe,mhe->nhm', split_heads(reader_rows), split_heads(pair[:, :D]), precision=HIGH) * HEAD_DIM ** (-0.5))
        top = lax.optimization_barrier(jnp.max(scores, axis=-1))
        expo = jnp.exp(scores - top[..., None])
        part = low_back(jnp.einsum('nhm,mhe->nhe', low(expo), split_heads(pair[:, D:]), precision=HIGH))
        return (top, lax.optimization_barrier(jnp.sum(expo, axis=-1)), part)
    tops, totals, parts = lax.map(jax.checkpoint(key_block), reader_keys.reshape(N_BLK, -1, 2 * D))
    highest = lax.optimization_barrier(jnp.max(tops, axis=0))
    factor = jnp.exp(tops - highest)
    denom = lax.optimization_barrier(jnp.sum(factor * totals, axis=0))
    read = lax.optimization_barrier(jnp.sum(factor[..., None] * parts, axis=0)) / denom[..., None]
    read = low_back(low(read.reshape(-1, D)))
    question_two = question_one + low_back(matmul(read, reader_output))
    viewer_rows = low_back(low(matmul(cross_visual, viewer_query)))
    viewer_keys = low_back(low(matmul(cross_question, viewer_pair)))
    keys = split_heads(viewer_keys[:, :D])
    values = split_heads(viewer_keys[:, D:])

    def view_block(rows):
        return attend(split_heads(rows), keys, values, 0.0)
    viewed = lax.map(jax.checkpoint(view_block), viewer_rows.reshape(N_BLK, -1, D)).reshape(-1, D)
    visual_two = visual_one + low_back(matmul(viewed, viewer_output))

    def visual_mlp(rows):
        return feed_forward(rows, gains[4], shifts[4], visual_up, visual_down)
    visual_three = lax.map(jax.checkpoint(visual_mlp), visual_two.reshape(N_BLK, -1, D)).reshape(-1, D)
    question_three = feed_forward(question_two, gains[5], shifts[5], question_up, question_down)
    return (visual_three, question_three)

def reference(visual_in, question_in, segment_ids, regions, rel_index, rel_table, window_project, window_output, causal_project, causal_output, reader_query, reader_pair, reader_output, viewer_query, viewer_pair, viewer_output, visual_up, visual_down, question_up, question_down, norm_gains, norm_shifts, visual_cot, question_cot):
    flats = tuple((item.astype(jnp.float32) for item in (window_project, window_output, causal_project, causal_output, reader_query, reader_pair, reader_output, viewer_query, viewer_pair, viewer_output, visual_up, visual_down, question_up, question_down, norm_gains, norm_shifts)))

    def forward(visual, question, table, pieces):
        weights = tuple((item.reshape(shape) for item, shape in zip(pieces, matrix_shapes())))

        def one_page(page):
            return page_forward(page[0], page[1], page[2], page[3], weights, table, rel_index)
        result = lax.map(jax.checkpoint(one_page), (visual.reshape(N_PAGE, -1, D), question.reshape(N_PAGE, Q_LEN, D), segment_ids, regions.reshape(N_PAGE, -1)))
        return (result[0].reshape(-1, D), result[1].reshape(-1, D))
    outputs, pull = jax.vjp(forward, visual_in.astype(jnp.float32), question_in.astype(jnp.float32), rel_table.astype(jnp.float32), flats)
    back_visual, back_question, back_table, deltas = pull((visual_cot.astype(jnp.float32), question_cot.astype(jnp.float32)))
    question_shift = deltas[15][5 * D:6 * D]
    return (outputs[0].astype(jnp.bfloat16), outputs[1].astype(jnp.bfloat16), back_visual, back_question, back_table, deltas[0], deltas[1], deltas[2], deltas[3], deltas[4], deltas[5], deltas[6], deltas[7], deltas[8], deltas[9], deltas[10], deltas[11], deltas[12], deltas[13], deltas[14], deltas[15], question_shift)
```

```python
import functools

import jax
import jax.numpy as jnp
from jax import lax
from jax.experimental import pallas as pl
from jax.experimental.pallas import tpu as pltpu
from jax.sharding import PartitionSpec as P

D = 768
HEADS = 12
HEAD_DIM = 64
FF = 3072
Q_LEN = 1024
WIN = 144
RELS = 529
LONGEST = Q_LEN // 2
LANES = 128
PAIRS = D // LANES
RELS_PAD = 640

EPS = 1e-05
NEG = -1000000000.0
SCALE = HEAD_DIM ** (-0.5)
MIB = 1 << 20


def product(left, right):
    return jnp.dot(left, right, preferred_element_type=jnp.float32)


def times_transposed(left, right):
    return lax.dot_general(
        left, right, (((1,), (1,)), ((), ())), preferred_element_type=jnp.float32
    )


def transposed_times(left, right):
    return lax.dot_general(
        left, right, (((0,), (0,)), ((), ())), preferred_element_type=jnp.float32
    )


def low(values):
    return values.astype(jnp.bfloat16)


def normalize(rows, gain, shift):
    mean = jnp.mean(rows, axis=-1, keepdims=True)
    centred = rows - mean
    spread = jnp.mean(centred * centred, axis=-1, keepdims=True)
    return centred * lax.rsqrt(spread + EPS) * gain + shift


def smooth(values):
    return jax.nn.gelu(values, approximate=False)


def ring_order(blocks):
    return tuple(range(0, blocks, 2)) + tuple(range(blocks - 1, 0, -2))


def ring_seat(blk, blocks):
    return jnp.where(blk % 2 == 0, blk // 2, blocks - 1 - blk // 2)


def ring_place(seat, blocks):
    seat = lax.rem(seat + 2 * blocks, blocks)
    return jnp.where(seat < blocks // 2, 2 * seat, 2 * (blocks - 1 - seat) + 1)


def forward_hop(blocks):
    order = ring_order(blocks)
    return [(order[i], order[(i + 1) % blocks]) for i in range(blocks)]


def backward_hop(blocks):
    return [(there, here) for here, there in forward_hop(blocks)]


def swap_far(values):
    return lax.ppermute(values, "page", [(i, i ^ 2) for i in range(4)])


def swap_core(values):
    return lax.ppermute(values, "page", [(i, i ^ 1) for i in range(4)])


OFFSETS = (0, -1, 1, -2, 2, -3, 3, 4)


def ring_pieces(own, blocks):
    ahead, behind = forward_hop(blocks), backward_hop(blocks)
    half = own.shape[0] // 2
    pieces = {0: own}
    one, two = own, own
    for step in (1, 2, 3):
        one = lax.ppermute(one, "blk", ahead)
        two = lax.ppermute(two, "blk", behind)
        pieces[-step], pieces[step] = one, two
    pieces["first"] = lax.ppermute(one[:half], "blk", ahead)
    pieces["second"] = lax.ppermute(two[half:], "blk", behind)
    return pieces


def ring_reduce(chunk, blocks):
    ahead, behind = forward_hop(blocks), backward_hop(blocks)
    most = chunk(4)
    half = most.shape[0] // 2
    one = lax.ppermute(low(most[:half]), "blk", ahead).astype(jnp.float32)
    two = lax.ppermute(low(most[half:]), "blk", behind).astype(jnp.float32)
    blank = jnp.zeros(one.shape, jnp.float32)
    one, two = jnp.concatenate([one, blank]), jnp.concatenate([blank, two])
    for step in (3, 2, 1):
        one = lax.ppermute(low(chunk(step) + one), "blk", ahead).astype(jnp.float32)
        two = lax.ppermute(low(chunk(-step) + two), "blk", behind).astype(jnp.float32)
    return chunk(0) + one + two


def whole_block(array):
    blank = (0,) * len(array.shape)
    return pl.BlockSpec(array.shape, lambda i, where: blank)


def assemble_kernel(plan, count, where_ref, *refs):
    pieces, outs = refs[:count], refs[count:]
    for piece, (index, first, core) in zip(pieces, plan):
        start = 0
        for out in outs:
            width = out.shape[-1]
            for number in range(piece.shape[0]):
                target = (first + number, where_ref[core], where_ref[index])
                out[target] = piece[number, :, start : start + width]
            start += width


def assemble(own, other, splits, core, seat, blocks):
    rows = own[0].shape[1]
    places = [ring_place(seat + k, blocks) for k in OFFSETS]
    where = jnp.stack([core, 1 - core] + places).astype(jnp.int32)
    pieces, plan = [], []
    for side, group in ((0, own), (1, other)):
        for number, offset in enumerate(OFFSETS):
            if offset == 4:
                pieces += [group["first"], group["second"]]
                plan += [(2 + number, 0, side), (2 + number, 1, side)]
            else:
                pieces.append(group[offset])
                plan.append((2 + number, 0, side))
    outs = [jax.ShapeDtypeStruct((2, 2, blocks, rows, width), jnp.bfloat16) for width in splits]
    found = pl.pallas_call(
        functools.partial(assemble_kernel, plan, len(pieces)),
        out_shape=outs,
        grid_spec=pltpu.PrefetchScalarGridSpec(
            num_scalar_prefetch=1,
            grid=(1,),
            in_specs=[whole_block(item) for item in pieces],
            out_specs=[whole_block(item) for item in outs],
        ),
        compiler_params=pltpu.CompilerParams(vmem_limit_bytes=32 * MIB),
        cost_estimate=pl.CostEstimate(
            flops=0, bytes_accessed=16 * blocks * rows * sum(splits), transcendentals=0
        ),
    )(where, *pieces)
    return [item.reshape(4 * blocks * rows, -1) for item in found]


def place_kernel(plan, where_ref, *refs):
    pieces, out = refs[:-1], refs[-1]
    for piece, (index, first, last) in zip(pieces, plan):
        out[where_ref[index], first:last] = piece[...].astype(out.dtype)


def gather_seats(own, seat, blocks, dtype):
    rows = own.shape[0]
    if blocks != 8:
        stacked = lax.all_gather(own, "blk", axis=0)
        ordered = jnp.stack([stacked[i] for i in ring_order(blocks)])
        return ordered.reshape(blocks * rows, -1).astype(dtype)
    found = ring_pieces(own, blocks)
    where = jnp.stack([lax.rem(seat + k + blocks, blocks) for k in OFFSETS]).astype(jnp.int32)
    pieces, plan = [], []
    for number, offset in enumerate(OFFSETS):
        if offset == 4:
            pieces += [found["first"], found["second"]]
            plan += [(number, 0, rows // 2), (number, rows // 2, rows)]
        else:
            pieces.append(found[offset])
            plan.append((number, 0, rows))
    out = jax.ShapeDtypeStruct((blocks,) + own.shape, dtype)
    placed = pl.pallas_call(
        functools.partial(place_kernel, plan),
        out_shape=out,
        grid_spec=pltpu.PrefetchScalarGridSpec(
            num_scalar_prefetch=1,
            grid=(1,),
            in_specs=[whole_block(item) for item in pieces],
            out_specs=whole_block(out),
        ),
        compiler_params=pltpu.CompilerParams(vmem_limit_bytes=24 * MIB),
        cost_estimate=pl.CostEstimate(
            flops=0, bytes_accessed=4 * blocks * own.size, transcendentals=0
        ),
    )(where, *pieces)
    return placed.reshape(blocks * rows, -1)


def bias_kernel(table_ref, index_ref, out_ref):
    def one(i, carry):
        row = index_ref[pl.ds(i, 1), :]
        marks = lax.broadcasted_iota(jnp.int32, (RELS_PAD, WIN), 0) == row
        hot = low(jnp.where(marks, 1.0, 0.0))
        both = jnp.dot(table_ref[...], hot, preferred_element_type=jnp.float32)
        out_ref[i] = both[:16] + both[16:]
        return carry

    lax.fori_loop(0, WIN, one, 0, unroll=4)


def window_bias(rel_table, rel_index):
    table = jnp.pad(rel_table, ((0, 16 - HEADS), (0, RELS_PAD - RELS)))
    coarse = lax.reduce_precision(table, 8, 7)
    both = low(jnp.concatenate([coarse, table - coarse]))
    found = pl.pallas_call(
        bias_kernel,
        out_shape=jax.ShapeDtypeStruct((WIN, 16, WIN), jnp.float32),
        cost_estimate=pl.CostEstimate(
            flops=64 * RELS_PAD * WIN * WIN, bytes_accessed=4 * 17 * WIN * WIN, transcendentals=0
        ),
    )(both, rel_index)
    return found[:, :HEADS].transpose(1, 0, 2)


def table_kernel(scores_ref, index_ref, out_ref):
    def one(i, total):
        row = index_ref[pl.ds(i, 1), :]
        marks = lax.broadcasted_iota(jnp.int32, (RELS_PAD, WIN), 0) == row
        hot = low(jnp.where(marks, 1.0, 0.0))
        return total + times_transposed(scores_ref[i], hot)

    out_ref[...] = lax.fori_loop(
        0, WIN, one, jnp.zeros((2 * HEADS, RELS_PAD), jnp.float32), unroll=4
    )


def table_sums(back_scores, rel_index):
    rows = back_scores.reshape(2 * HEADS, WIN, WIN).transpose(1, 0, 2)
    found = pl.pallas_call(
        table_kernel,
        out_shape=jax.ShapeDtypeStruct((2 * HEADS, RELS_PAD), jnp.float32),
        cost_estimate=pl.CostEstimate(
            flops=48 * RELS_PAD * WIN * WIN, bytes_accessed=52 * WIN * WIN, transcendentals=0
        ),
    )(rows, rel_index)
    return jnp.sum(found.reshape(HEADS, 2, RELS_PAD), axis=1)[:, :RELS]


def head_lanes(side):
    lane = lax.broadcasted_iota(jnp.int32, (1, LANES), 1)
    return (lane < HEAD_DIM) if side == 0 else (lane >= HEAD_DIM)


def attend_pair(query, keys, values, extras):
    result, logs = None, None
    for side in (0, 1):
        mine = head_lanes(side)
        one = jnp.where(mine, query * SCALE, 0).astype(jnp.bfloat16)
        scores = times_transposed(one, keys) + extras[side]
        top = jnp.max(scores, axis=-1, keepdims=True)
        expo = jnp.exp(scores - top)
        total = jnp.sum(expo, axis=-1, keepdims=True)
        found = product(low(expo), values) / total
        log_total = jnp.broadcast_to(top + jnp.log(total), found.shape)
        result = found if side == 0 else jnp.where(mine, found, result)
        logs = log_total if side == 0 else jnp.where(mine, log_total, logs)
    return low(result), logs


def pair_backward(query, keys, values, extras, logs, back_out):
    back_query, back_keys, back_values, kept = None, None, None, []
    for side in (0, 1):
        mine = head_lanes(side)
        one = jnp.where(mine, query * SCALE, 0).astype(jnp.bfloat16)
        back_one = jnp.where(mine, back_out, 0).astype(jnp.bfloat16)
        scores = times_transposed(one, keys) + extras[side]
        first = side * HEAD_DIM
        shares = jnp.exp(scores - logs[:, first : first + 1])
        back_shares = times_transposed(back_one, values)
        inner = jnp.sum(shares * back_shares, axis=-1, keepdims=True)
        back_scores = low(shares * (back_shares - inner))
        found = product(back_scores, keys) * SCALE
        found_keys = transposed_times(back_scores, one)
        found_values = transposed_times(low(shares), back_one)
        kept.append(back_scores)
        if side == 0:
            back_query, back_keys, back_values = found, found_keys, found_values
        else:
            back_query = jnp.where(mine, found, back_query)
            back_keys, back_values = back_keys + found_keys, back_values + found_values
    return low(back_query), low(back_keys), low(back_values), kept


def question_extra(role_ref, qid, kid):
    shape = (qid.shape[0], kid.shape[1])
    row = lax.broadcasted_iota(jnp.int32, shape, 0) + role_ref[1]
    column = lax.broadcasted_iota(jnp.int32, shape, 1)
    return jnp.where((qid == kid) & (column <= row), 0.0, NEG)


def window_extras(bias_ref, qid, kid):
    same = jnp.where(qid == kid, 0.0, NEG)
    return [bias_ref[0] + same, bias_ref[1] + same]


def self_forward_kernel(
    role_ref, q_ref, k_ref, v_ref, bias_ref, qid_ref, kid_ref, o_ref, log_ref
):
    rows = q_ref.shape[1]

    @pl.when(role_ref[0] == 0)
    def question():
        for s in (0, 1):
            extra = question_extra(role_ref, qid_ref[s], kid_ref[s])
            o_ref[s], log_ref[s] = attend_pair(q_ref[s], k_ref[s], v_ref[s], [extra, extra])

    @pl.when(role_ref[0] != 0)
    def visual():
        for s in (0, 1):
            extras = window_extras(bias_ref, qid_ref[s], kid_ref[s, :, :rows])
            o_ref[s], log_ref[s] = attend_pair(
                q_ref[s], k_ref[s, :rows], v_ref[s, :rows], extras
            )


def self_backward_kernel(
    role_ref,
    q_ref,
    k_ref,
    v_ref,
    bias_ref,
    qid_ref,
    kid_ref,
    log_ref,
    back_ref,
    dq_ref,
    dk_ref,
    dv_ref,
    ds_ref,
):
    rows = q_ref.shape[1]

    @pl.when(role_ref[0] == 0)
    def question():
        ds_ref[...] = jnp.zeros_like(ds_ref)
        for s in (0, 1):
            extra = question_extra(role_ref, qid_ref[s], kid_ref[s])
            dq_ref[s], dk_ref[s], dv_ref[s], unused = pair_backward(
                q_ref[s], k_ref[s], v_ref[s], [extra, extra], log_ref[s], back_ref[s]
            )

    @pl.when(role_ref[0] != 0)
    def visual():
        dk_ref[...] = jnp.zeros_like(dk_ref)
        dv_ref[...] = jnp.zeros_like(dv_ref)
        for s in (0, 1):
            extras = window_extras(bias_ref, qid_ref[s], kid_ref[s, :, :rows])
            dq_ref[s], found_keys, found_values, kept = pair_backward(
                q_ref[s], k_ref[s, :rows], v_ref[s, :rows], extras, log_ref[s], back_ref[s]
            )
            dk_ref[s, :rows] = found_keys
            dv_ref[s, :rows] = found_values
            ds_ref[0, s] = kept[0]
            ds_ref[1, s] = kept[1]


def self_specs(rows, span):
    query = pl.BlockSpec((2, rows, LANES), lambda h, role: (0, 0, h))
    keys = pl.BlockSpec((2, span, LANES), lambda h, role: (0, 0, h))
    values = pl.BlockSpec((2, span, LANES), lambda h, role: (0, 0, h + PAIRS))
    bias = pl.BlockSpec((2, rows, rows), lambda h, role: (h, 0, 0))
    qid = pl.BlockSpec((2, rows, 1), lambda h, role: (0, 0, 0))
    kid = pl.BlockSpec((2, 1, span), lambda h, role: (0, 0, 0))
    return query, keys, values, bias, qid, kid


def self_forward(role, query, pair, bias, qid, kid):
    rows, span = query.shape[1], pair.shape[1]
    specs = self_specs(rows, span)
    return pl.pallas_call(
        self_forward_kernel,
        out_shape=[
            jax.ShapeDtypeStruct((2, rows, D), jnp.bfloat16),
            jax.ShapeDtypeStruct((2, rows, D), jnp.float32),
        ],
        grid_spec=pltpu.PrefetchScalarGridSpec(
            num_scalar_prefetch=1, grid=(PAIRS,), in_specs=list(specs), out_specs=[specs[0]] * 2
        ),
        compiler_params=pltpu.CompilerParams(vmem_limit_bytes=24 * MIB),
        cost_estimate=pl.CostEstimate(
            flops=16 * rows * span * D, bytes_accessed=12 * span * D, transcendentals=0
        ),
    )(role, query, pair, pair, bias, qid, kid)


def self_backward(role, query, pair, bias, qid, kid, logs, back_out):
    rows, span = query.shape[1], pair.shape[1]
    specs = self_specs(rows, span)
    return pl.pallas_call(
        self_backward_kernel,
        out_shape=[
            jax.ShapeDtypeStruct((2, rows, D), jnp.bfloat16),
            jax.ShapeDtypeStruct((2, span, D), jnp.bfloat16),
            jax.ShapeDtypeStruct((2, span, D), jnp.bfloat16),
            jax.ShapeDtypeStruct((HEADS, 2, rows, rows), jnp.bfloat16),
        ],
        grid_spec=pltpu.PrefetchScalarGridSpec(
            num_scalar_prefetch=1,
            grid=(PAIRS,),
            in_specs=list(specs) + [specs[0]] * 2,
            out_specs=[
                specs[0],
                specs[1],
                specs[1],
                pl.BlockSpec((2, 2, rows, rows), lambda h, role: (h, 0, 0, 0)),
            ],
        ),
        compiler_params=pltpu.CompilerParams(vmem_limit_bytes=24 * MIB),
        cost_estimate=pl.CostEstimate(
            flops=40 * rows * span * D, bytes_accessed=16 * span * D, transcendentals=0
        ),
    )(role, query, pair, pair, bias, qid, kid, logs, back_out)


def cross_forward_kernel(q_ref, k_ref, v_ref, extra_ref, o_ref, log_ref):
    extra = extra_ref[...]
    o_ref[...], log_ref[...] = attend_pair(
        q_ref[...], k_ref[...], v_ref[...], [extra, extra]
    )


def cross_backward_kernel(
    q_ref, k_ref, v_ref, extra_ref, log_ref, back_ref, dq_ref, dk_ref, dv_ref
):
    extra = extra_ref[...]
    dq_ref[...], dk_ref[...], dv_ref[...], unused = pair_backward(
        q_ref[...], k_ref[...], v_ref[...], [extra, extra], log_ref[...], back_ref[...]
    )


def cross_specs(rows, span):
    query = pl.BlockSpec((rows, LANES), lambda h: (0, h))
    keys = pl.BlockSpec((span, LANES), lambda h: (0, h))
    values = pl.BlockSpec((span, LANES), lambda h: (0, h + PAIRS))
    extra = pl.BlockSpec((1, span), lambda h: (0, 0))
    return query, keys, values, extra


def cross_limit(span):
    return (24 if span <= 2048 else 60) * MIB


def cross_forward(query, pair, extra):
    rows, span = query.shape[0], pair.shape[0]
    specs = cross_specs(rows, span)
    return pl.pallas_call(
        cross_forward_kernel,
        out_shape=[
            jax.ShapeDtypeStruct((rows, D), jnp.bfloat16),
            jax.ShapeDtypeStruct((rows, D), jnp.float32),
        ],
        grid=(PAIRS,),
        in_specs=list(specs),
        out_specs=[specs[0]] * 2,
        compiler_params=pltpu.CompilerParams(vmem_limit_bytes=cross_limit(span)),
        cost_estimate=pl.CostEstimate(
            flops=16 * rows * span * D, bytes_accessed=4 * span * D, transcendentals=0
        ),
    )(query, pair, pair, extra)


def cross_backward(query, pair, extra, logs, back_out):
    rows, span = query.shape[0], pair.shape[0]
    specs = cross_specs(rows, span)
    return pl.pallas_call(
        cross_backward_kernel,
        out_shape=[
            jax.ShapeDtypeStruct((rows, D), jnp.bfloat16),
            jax.ShapeDtypeStruct((span, D), jnp.bfloat16),
            jax.ShapeDtypeStruct((span, D), jnp.bfloat16),
        ],
        grid=(PAIRS,),
        in_specs=list(specs) + [specs[0]] * 2,
        out_specs=[specs[0], specs[1], specs[1]],
        compiler_params=pltpu.CompilerParams(vmem_limit_bytes=cross_limit(span)),
        cost_estimate=pl.CostEstimate(
            flops=40 * rows * span * D, bytes_accessed=8 * span * D, transcendentals=0
        ),
    )(query, pair, pair, extra, logs, back_out)


def body(
    visual_in,
    question_in,
    segment_ids,
    regions,
    rel_index,
    rel_table,
    window_project,
    window_output,
    causal_project,
    causal_output,
    reader_query,
    reader_pair,
    reader_output,
    viewer_query,
    viewer_pair,
    viewer_output,
    visual_up,
    visual_down,
    question_up,
    question_down,
    norm_gains,
    norm_shifts,
    visual_cot,
    question_cot,
):
    blocks = lax.axis_size("blk")
    share = Q_LEN // blocks
    rows = visual_in.shape[0]
    page, blk = lax.axis_index("page"), lax.axis_index("blk")
    asks, core = page < 2, page % 2
    seat = ring_seat(blk, blocks)
    early = -(-(LONGEST - 1) // share)
    reach = min(Q_LEN, share * (early + 1))
    span = reach + rows - share
    first = jnp.clip((seat - early) * share, 0, Q_LEN - reach)
    inset = jnp.where(asks, seat * share - first, 0)
    cut = D // (4 * blocks)

    def own_of(question_side, visual_side):
        return jnp.where(asks, question_side, visual_side)

    def trade(question_side, visual_side):
        got = swap_far(own_of(visual_side, question_side))
        kept = own_of(question_side, visual_side)
        return jnp.stack([own_of(kept, got), own_of(got, kept)])

    def gather_weight(question_side, visual_side, splits):
        both = trade(question_side, visual_side)
        if blocks == 8:
            pieces = ring_pieces(both, blocks)
            other = {key: swap_core(item) for key, item in pieces.items()}
            return assemble(pieces, other, splits, core, seat, blocks)
        here = lax.all_gather(both, "blk", axis=0)
        there = swap_core(here)
        pair = jnp.where(core == 0, jnp.stack([here, there]), jnp.stack([there, here]))
        whole = pair.transpose(2, 0, 1, 3, 4).reshape(4 * blocks * both.shape[1], -1)
        places = [sum(splits[:i]) for i in range(len(splits))]
        return [whole[:, at : at + width] for at, width in zip(places, splits)]

    def pad_rows(values, total):
        return jnp.pad(values, ((0, total - values.shape[0]),) + ((0, 0),) * (values.ndim - 1))

    def block_of(flat, columns):
        return flat.reshape(-1, columns)

    norms = jnp.pad(jnp.concatenate([norm_gains, norm_shifts]), (0, cut * LANES - 2 * norm_gains.size))
    norms = norms.reshape(cut, LANES)
    self_query_weight, self_pair_weight, self_exit, norm_rows = gather_weight(
        jnp.concatenate([block_of(causal_project, 3 * D), block_of(causal_output, D), norms], 1),
        jnp.concatenate([block_of(window_project, 3 * D), block_of(window_output, D), norms], 1),
        (D, 2 * D, D, LANES),
    )
    slots = trade(
        pad_rows(lax.dynamic_slice_in_dim(question_in, first, reach, 0), span),
        pad_rows(visual_in, span),
    )
    marks = trade(segment_ids[0], jnp.pad(regions, (0, Q_LEN - rows)))
    cross_query_weight, cross_pair_weight, cross_exit = gather_weight(
        jnp.concatenate(
            [block_of(reader_query, D), block_of(reader_pair, 2 * D), block_of(reader_output, D)], 1
        ),
        jnp.concatenate(
            [block_of(viewer_query, D), block_of(viewer_pair, 2 * D), block_of(viewer_output, D)], 1
        ),
        (D, 2 * D, D),
    )
    (raise_weight,) = gather_weight(block_of(question_up, FF), block_of(visual_up, FF), (FF,))
    (lower_weight,) = gather_weight(block_of(question_down, D), block_of(visual_down, D), (D,))
    cot = trade(
        pad_rows(lax.dynamic_slice_in_dim(question_cot, seat * share, share, 0), rows), visual_cot
    ).astype(jnp.float32)
    norm_flat = norm_rows.reshape(4 * blocks, -1)[:, : 2 * norm_gains.size].astype(jnp.float32)
    gains = norm_flat[:, : norm_gains.size].reshape(6, D)
    shifts = norm_flat[:, norm_gains.size :].reshape(6, D)
    bias = window_bias(rel_table, rel_index)

    role = jnp.stack([jnp.where(asks, 0, 1), inset]).astype(jnp.int32)
    key_marks = own_of(
        jnp.pad(
            lax.dynamic_slice_in_dim(marks, first, reach, 1),
            ((0, 0), (0, span - reach)),
            constant_values=-2,
        ),
        marks[:, :span],
    )[:, None, :]
    row_marks = own_of(
        jnp.pad(
            lax.dynamic_slice_in_dim(marks, seat * share, share, 1),
            ((0, 0), (0, rows - share)),
            constant_values=-1,
        ),
        marks[:, :rows],
    )[:, :, None]
    own = lax.dynamic_slice_in_dim(slots, inset, rows, 1).astype(jnp.float32)
    self_gain, self_shift = own_of(gains[1], gains[0]), own_of(shifts[1], shifts[0])
    self_norm, self_pull = jax.vjp(normalize, own, self_gain, self_shift)
    self_low = low(self_norm).reshape(2 * rows, D)
    every_low = low(normalize(slots.astype(jnp.float32), self_gain, self_shift))
    every_low = every_low.reshape(2 * span, D)
    self_query = low(product(self_low, self_query_weight)).reshape(2, rows, D)
    self_pair = low(product(every_low, self_pair_weight)).reshape(2, span, 2 * D)
    self_attn, self_logs = self_forward(role, self_query, self_pair, bias, row_marks, key_marks)
    self_attn = self_attn.reshape(2 * rows, D)
    rows_one = own + product(self_attn, self_exit).reshape(2, rows, D)

    cross_gain, cross_shift = own_of(gains[2], gains[3]), own_of(shifts[2], shifts[3])
    cross_norm, cross_pull = jax.vjp(normalize, rows_one, cross_gain, cross_shift)
    cross_low = low(cross_norm)
    sent = swap_far(cross_low)

    def all_blocks(piece):
        if blocks != 8:
            return lax.all_gather(piece, "blk", axis=0, tiled=True)
        found = ring_pieces(piece, blocks)
        ordered = [found[k] for k in OFFSETS[:-1]] + [found["first"], found["second"]]
        return jnp.concatenate(ordered)

    def sum_blocks(partial):
        if blocks != 8:
            return lax.psum_scatter(partial, "blk", scatter_dimension=0, tiled=True)

        def chunk(k):
            at = OFFSETS.index(k) * rows
            return partial[at : at + rows]

        return ring_reduce(chunk, blocks)

    sources = [all_blocks(sent[s]) for s in (0, 1)]
    cross_query = low(product(cross_low.reshape(2 * rows, D), cross_query_weight))
    cross_query = cross_query.reshape(2, rows, D)
    column = jnp.arange(blocks * rows) % rows
    cross_extra = own_of(0.0, jnp.where(column < share, 0.0, NEG))[None]
    cross_pairs = [low(product(source, cross_pair_weight)) for source in sources]
    cross_found = [cross_forward(cross_query[s], cross_pairs[s], cross_extra) for s in (0, 1)]
    cross_attn = jnp.concatenate([found[0] for found in cross_found])
    rows_two = rows_one + product(cross_attn, cross_exit).reshape(2, rows, D)

    mlp_gain, mlp_shift = own_of(gains[5], gains[4]), own_of(shifts[5], shifts[4])
    mlp_norm, mlp_pull = jax.vjp(normalize, rows_two, mlp_gain, mlp_shift)
    mlp_low = low(mlp_norm).reshape(2 * rows, D)
    active, smooth_pull = jax.vjp(smooth, product(mlp_low, raise_weight))
    active_low = low(active)
    rows_three = rows_two + product(active_low, lower_weight).reshape(2, rows, D)
    mlp_branch = low(cot).reshape(2 * rows, D)
    (back_raise,) = smooth_pull(times_transposed(mlp_branch, lower_weight))
    back_raise = low(back_raise)
    delta_lower = low(transposed_times(active_low, mlp_branch))
    delta_raise = low(transposed_times(mlp_low, back_raise))
    back_mlp = times_transposed(back_raise, raise_weight).reshape(2, rows, D)
    back_mlp_in, gain_mlp, shift_mlp = mlp_pull(back_mlp)
    back_two = cot + back_mlp_in

    def sum_weight(parts):
        height = parts[0].shape[0] // (4 * blocks)
        views = [part.reshape(2, 2, blocks, height, -1) for part in parts]

        def pick(side):
            return [
                lax.dynamic_index_in_dim(view, side, 1, keepdims=False) for view in views
            ]

        got = [swap_core(item) for item in pick(1 - core)]

        if blocks == 8:

            def chunk(k):
                place = ring_place(seat + k, blocks)
                both = []
                for view, item in zip(views, got):
                    mine = lax.dynamic_slice(
                        view, (0, core, place, 0, 0), (2, 1, 1) + view.shape[3:]
                    ).reshape(2, height, -1)
                    theirs = lax.dynamic_index_in_dim(item, place, 1, keepdims=False)
                    both.append(mine.astype(jnp.float32) + theirs.astype(jnp.float32))
                return jnp.concatenate(both, -1)

            total = ring_reduce(chunk, blocks)
        else:
            kept = jnp.concatenate(
                [a.astype(jnp.float32) + b.astype(jnp.float32) for a, b in zip(pick(core), got)], -1
            )
            total = lax.psum_scatter(kept, "blk", scatter_dimension=1, tiled=True)
            total = total.reshape(2, height, -1)
        mine, away = own_of(total[0], total[1]), own_of(total[1], total[0])
        came = swap_far(low(away)).astype(jnp.float32)
        return own_of(mine, came), own_of(came, mine)

    lower_sums = sum_weight([delta_lower])
    raise_sums = sum_weight([delta_raise])

    cross_branch = low(back_two).reshape(2 * rows, D)
    delta_cross_exit = low(transposed_times(cross_attn, cross_branch))
    back_attn = low(times_transposed(cross_branch, cross_exit)).reshape(2, rows, D)
    cross_back = [
        cross_backward(
            cross_query[s], cross_pairs[s], cross_extra, cross_found[s][1], back_attn[s]
        )
        for s in (0, 1)
    ]
    key_half, value_half = cross_pair_weight[:, :D], cross_pair_weight[:, D:]
    back_sent = []
    for unused, found_keys, found_values in cross_back:
        partial = times_transposed(found_keys, key_half) + times_transposed(found_values, value_half)
        back_sent.append(sum_blocks(partial))
    back_query = jnp.concatenate([found[0] for found in cross_back])
    back_cross = times_transposed(back_query, cross_query_weight).reshape(2, rows, D)
    back_cross = back_cross + swap_far(low(jnp.stack(back_sent))).astype(jnp.float32)
    back_cross_in, gain_cross, shift_cross = cross_pull(back_cross)
    back_one = back_two + back_cross_in
    all_sources = jnp.concatenate(sources)
    delta_cross_keys = low(
        transposed_times(all_sources, jnp.concatenate([found[1] for found in cross_back]))
    )
    delta_cross_values = low(
        transposed_times(all_sources, jnp.concatenate([found[2] for found in cross_back]))
    )
    delta_cross_query = low(transposed_times(cross_low.reshape(2 * rows, D), back_query))
    cross_sums = sum_weight(
        [delta_cross_query, delta_cross_keys, delta_cross_values, delta_cross_exit]
    )

    self_branch = low(back_one).reshape(2 * rows, D)
    delta_self_exit = low(transposed_times(self_attn, self_branch))
    back_attn = low(times_transposed(self_branch, self_exit)).reshape(2, rows, D)
    back_query, back_keys, back_values, back_scores = self_backward(
        role, self_query, self_pair, bias, row_marks, key_marks, self_logs, back_attn
    )
    back_query = back_query.reshape(2 * rows, D)
    back_keys, back_values = back_keys.reshape(2 * span, D), back_values.reshape(2 * span, D)
    delta_self_query = low(transposed_times(self_low, back_query))
    delta_self_keys = low(transposed_times(every_low, back_keys))
    delta_self_values = low(transposed_times(every_low, back_values))
    self_sums = sum_weight(
        [delta_self_query, delta_self_keys, delta_self_values, delta_self_exit]
    )
    back_every = times_transposed(back_keys, self_pair_weight[:, :D])
    back_every = back_every + times_transposed(back_values, self_pair_weight[:, D:])
    back_every = back_every.reshape(2, span, D)

    def for_earlier(j):
        at = jnp.maximum(inset - j * share, 0)
        found = lax.dynamic_slice_in_dim(back_every, at, share, 1)
        return jnp.where(asks & (seat >= j), found, 0.0)

    order = ring_order(blocks)
    earlier_hop = [(order[i], order[i - 1]) for i in range(1, blocks)]
    running = for_earlier(early)
    for j in range(early - 1, -1, -1):
        running = lax.ppermute(low(running), "blk", earlier_hop).astype(jnp.float32) + for_earlier(j)
    back_self = times_transposed(back_query, self_query_weight).reshape(2, rows, D) + own_of(
        jnp.pad(running, ((0, 0), (0, rows - share), (0, 0))), back_every[:, :rows]
    )
    back_self_in, gain_self, shift_self = self_pull(back_self)
    back_in = back_one + back_self_in

    blank = jnp.zeros((D,), jnp.float32)
    gain_delta = [
        own_of(blank, gain_self),
        own_of(gain_self, blank),
        own_of(gain_cross, blank),
        own_of(blank, gain_cross),
        own_of(blank, gain_mlp),
        own_of(gain_mlp, blank),
    ]
    shift_delta = [
        own_of(blank, shift_self),
        own_of(shift_self, blank),
        own_of(shift_cross, blank),
        own_of(blank, shift_cross),
        own_of(blank, shift_mlp),
        own_of(shift_mlp, blank),
    ]
    table_part = table_sums(back_scores, rel_index)
    small = jnp.concatenate(gain_delta + shift_delta + [table_part.reshape(-1)])
    size = small.size
    small = jnp.pad(small, (0, LANES * LANES - size)).reshape(LANES, LANES)
    small = small + swap_core(small)
    small = small + swap_far(small)
    bit = 1
    while bit < blocks:
        small = small + lax.ppermute(small, "blk", [(i, i ^ bit) for i in range(blocks)])
        bit *= 2
    small = small.reshape(-1)
    at = (page * blocks + blk) * norm_gains.size
    delta_gains = lax.dynamic_slice_in_dim(small, at, norm_gains.size, 0)
    delta_shifts = lax.dynamic_slice_in_dim(small, 6 * D + at, norm_gains.size, 0)
    table_delta = small[12 * D : size].reshape(HEADS, RELS)
    question_shift = small[11 * D : 12 * D]

    def home(values):
        got = swap_far(own_of(values[1], values[0]))
        kept = own_of(values[0], values[1])
        return own_of(kept, got)[:share], own_of(got, kept)

    question_rows, visual_out = home(low(rows_three))
    question_out = gather_seats(question_rows, seat, blocks, jnp.bfloat16)
    question_back, visual_back = home(low(back_in))
    question_delta = gather_seats(question_back, seat, blocks, jnp.float32)

    def cuts(sums, widths):
        places = [sum(widths[:i]) for i in range(len(widths))]
        return [
            [side[:, at : at + width].reshape(-1) for at, width in zip(places, widths)]
            for side in sums
        ]

    causal, window = cuts(self_sums, (3 * D, D))
    reader, viewer = cuts(cross_sums, (D, 2 * D, D))
    return (
        visual_out,
        question_out,
        visual_back.astype(jnp.float32),
        question_delta,
        table_delta,
        window[0],
        window[1],
        causal[0],
        causal[1],
        reader[0],
        reader[1],
        reader[2],
        viewer[0],
        viewer[1],
        viewer[2],
        raise_sums[1].reshape(-1),
        lower_sums[1].reshape(-1),
        raise_sums[0].reshape(-1),
        lower_sums[0].reshape(-1),
        delta_gains,
        delta_shifts,
        question_shift,
    )


def solution(mesh):
    split, by_page, flat, whole = P(("page", "blk"), None), P("page", None), P(("page", "blk")), P()
    in_specs = (split, by_page, by_page, flat, whole, whole) + (flat,) * 16 + (split, by_page)
    out_specs = (split, by_page, split, by_page, whole) + (flat,) * 16 + (whole,)
    return jax.shard_map(body, mesh=mesh, in_specs=in_specs, out_specs=out_specs, check_vma=False)
```

```python
import functools

import jax
import jax.numpy as jnp
from jax import lax
from jax.experimental import pallas as pl
from jax.experimental.pallas import tpu as pltpu
from jax.sharding import PartitionSpec as P

D = 768
HEADS = 12
HEAD_DIM = 64
FF = 3072
Q_LEN = 1024
WIN = 144
RELS = 529
LONGEST = Q_LEN // 2
LANES = 128
PAIRS = D // LANES
RELS_PAD = 640

EPS = 1e-05
NEG = -1000000000.0
SCALE = HEAD_DIM ** (-0.5)
MIB = 1 << 20


def product(left, right):
    return jnp.dot(left, right, preferred_element_type=jnp.float32)


def times_transposed(left, right):
    return lax.dot_general(
        left, right, (((1,), (1,)), ((), ())), preferred_element_type=jnp.float32
    )


def transposed_times(left, right):
    return lax.dot_general(
        left, right, (((0,), (0,)), ((), ())), preferred_element_type=jnp.float32
    )


def low(values):
    return values.astype(jnp.bfloat16)


def normalize(rows, gain, shift):
    mean = jnp.mean(rows, axis=-1, keepdims=True)
    centred = rows - mean
    spread = jnp.mean(centred * centred, axis=-1, keepdims=True)
    return centred * lax.rsqrt(spread + EPS) * gain + shift


def smooth(values):
    return jax.nn.gelu(values, approximate=False)


def ring_order(blocks):
    return tuple(range(0, blocks, 2)) + tuple(range(blocks - 1, 0, -2))


def ring_seat(blk, blocks):
    return jnp.where(blk % 2 == 0, blk // 2, blocks - 1 - blk // 2)


def ring_place(seat, blocks):
    seat = lax.rem(seat + 2 * blocks, blocks)
    return jnp.where(seat < blocks // 2, 2 * seat, 2 * (blocks - 1 - seat) + 1)


def forward_hop(blocks):
    order = ring_order(blocks)
    return [(order[i], order[(i + 1) % blocks]) for i in range(blocks)]


def backward_hop(blocks):
    return [(there, here) for here, there in forward_hop(blocks)]


def swap_far(values):
    return lax.ppermute(values, "far", [(0, 1), (1, 0)])


def swap_core(values):
    return lax.ppermute(values, "core", [(0, 1), (1, 0)])


OFFSETS = (0, -1, 1, -2, 2, -3, 3, 4)


class Gather:
    def __init__(self, own, blocks):
        self.hops = forward_hop(blocks), backward_hop(blocks)
        self.half = own.shape[0] // 2
        self.pieces, self.step, self.state = {0: own}, 0, (own, own)

    def send(self):
        one, two = self.state
        if self.step == 3:
            one, two = one[: self.half], two[self.half :]
        return lax.ppermute(one, "blk", self.hops[0]), lax.ppermute(two, "blk", self.hops[1])

    def receive(self, found):
        self.step, self.state = self.step + 1, found
        if self.step == 4:
            self.pieces["first"], self.pieces["second"] = found
        else:
            self.pieces[-self.step], self.pieces[self.step] = found


class Circle:
    def __init__(self, own, blocks):
        self.hops, self.left = forward_hop(blocks), blocks - 1
        self.pieces = [own]

    def send(self):
        return lax.ppermute(self.pieces[-1], "blk", self.hops)

    def receive(self, found):
        self.pieces.append(found)
        self.left -= 1


class Sum:
    def __init__(self, chunk, blocks):
        self.hops = forward_hop(blocks), backward_hop(blocks)
        self.chunk, self.step = chunk, 0
        most = chunk(4)
        half = most.shape[0] // 2
        self.state = lax.optimization_barrier((low(most[:half]), low(most[half:])))

    def send(self):
        one, two = self.state
        return lax.ppermute(one, "blk", self.hops[0]), lax.ppermute(two, "blk", self.hops[1])

    def receive(self, found):
        one, two = [item.astype(jnp.float32) for item in found]
        if self.step == 0:
            blank = jnp.zeros(one.shape, jnp.float32)
            one, two = jnp.concatenate([one, blank]), jnp.concatenate([blank, two])
        self.step += 1
        left = 4 - self.step
        if left == 0:
            self.total = self.chunk(0) + one + two
        else:
            self.state = low(self.chunk(left) + one), low(self.chunk(-left) + two)
            self.state = lax.optimization_barrier(self.state)


class Once:
    def __init__(self, send):
        self.send = send

    def receive(self, found):
        self.found = found


def phase(transfers, work=()):
    found = [item.send() for item in transfers]
    found, work = lax.optimization_barrier((found, work))
    for item, one in zip(transfers, found):
        item.receive(one)
    return work


def whole_block(array):
    blank = (0,) * len(array.shape)
    return pl.BlockSpec(array.shape, lambda i, where: blank)


def assemble_kernel(plan, count, where_ref, *refs):
    pieces, outs = refs[:count], refs[count:]
    for piece, (index, first, core) in zip(pieces, plan):
        start = 0
        for out in outs:
            width = out.shape[-1]
            for number in range(piece.shape[0]):
                target = (first + number, where_ref[core], where_ref[index])
                out[target] = piece[number, :, start : start + width]
            start += width


def assemble(own, other, splits, core, seat, blocks):
    rows = own[0].shape[1]
    places = [ring_place(seat + k, blocks) for k in OFFSETS]
    where = jnp.stack([core, 1 - core] + places).astype(jnp.int32)
    pieces, plan = [], []
    for side, group in ((0, own), (1, other)):
        for number, offset in enumerate(OFFSETS):
            if offset == 4:
                pieces += [group["first"], group["second"]]
                plan += [(2 + number, 0, side), (2 + number, 1, side)]
            else:
                pieces.append(group[offset])
                plan.append((2 + number, 0, side))
    outs = [jax.ShapeDtypeStruct((2, 2, blocks, rows, width), jnp.bfloat16) for width in splits]
    found = pl.pallas_call(
        functools.partial(assemble_kernel, plan, len(pieces)),
        out_shape=outs,
        grid_spec=pltpu.PrefetchScalarGridSpec(
            num_scalar_prefetch=1,
            grid=(1,),
            in_specs=[whole_block(item) for item in pieces],
            out_specs=[whole_block(item) for item in outs],
        ),
        compiler_params=pltpu.CompilerParams(vmem_limit_bytes=32 * MIB),
        cost_estimate=pl.CostEstimate(
            flops=0, bytes_accessed=16 * blocks * rows * sum(splits), transcendentals=0
        ),
    )(where, *pieces)
    return [item.reshape(4 * blocks * rows, -1) for item in found]


def place_kernel(plan, where_ref, *refs):
    pieces, out = refs[:-1], refs[-1]
    for piece, (index, first, last) in zip(pieces, plan):
        out[where_ref[index], first:last] = piece[...].astype(out.dtype)


def seats_in_order(found, seat, blocks, dtype):
    columns = found[0][2].shape[1]
    rows = max(piece.shape[0] for unused, also, piece in found)
    where = [lax.rem(seat + offset + blocks, blocks) for offset, unused, also in found]
    where = jnp.stack(where).astype(jnp.int32)
    pieces = [piece for unused, also, piece in found]
    plan = [(i, at, at + item[2].shape[0]) for i, item in enumerate(found) for at in [item[1]]]
    out = jax.ShapeDtypeStruct((blocks, rows, columns), dtype)
    placed = pl.pallas_call(
        functools.partial(place_kernel, plan),
        out_shape=out,
        grid_spec=pltpu.PrefetchScalarGridSpec(
            num_scalar_prefetch=1,
            grid=(1,),
            in_specs=[whole_block(item) for item in pieces],
            out_specs=whole_block(out),
        ),
        compiler_params=pltpu.CompilerParams(vmem_limit_bytes=24 * MIB),
        cost_estimate=pl.CostEstimate(
            flops=0, bytes_accessed=6 * blocks * rows * columns, transcendentals=0
        ),
    )(where, *pieces)
    return placed.reshape(blocks * rows, columns)


def bias_kernel(role_ref, table_ref, index_ref, out_ref):
    def one(i, carry):
        row = index_ref[pl.ds(i, 1), :]
        marks = lax.broadcasted_iota(jnp.int32, (RELS_PAD, WIN), 0) == row
        hot = low(jnp.where(marks, 1.0, 0.0))
        both = jnp.dot(table_ref[...], hot, preferred_element_type=jnp.float32)
        out_ref[i] = both[:16] + both[16:]
        return carry

    @pl.when(role_ref[0] != 0)
    def visual():
        lax.fori_loop(0, WIN, one, 0, unroll=4)

    @pl.when(role_ref[0] == 0)
    def question():
        out_ref[...] = jnp.zeros_like(out_ref)


def window_bias(role, rel_table, rel_index):
    table = jnp.pad(rel_table, ((0, 16 - HEADS), (0, RELS_PAD - RELS)))
    coarse = lax.reduce_precision(table, 8, 7)
    both = low(jnp.concatenate([coarse, table - coarse]))
    found = pl.pallas_call(
        bias_kernel,
        out_shape=jax.ShapeDtypeStruct((WIN, 16, WIN), jnp.float32),
        in_specs=[pl.BlockSpec(memory_space=pltpu.SMEM)] + [pl.BlockSpec()] * 2,
        cost_estimate=pl.CostEstimate(
            flops=64 * RELS_PAD * WIN * WIN, bytes_accessed=4 * 17 * WIN * WIN, transcendentals=0
        ),
    )(role, both, rel_index)
    return found[:, :HEADS].transpose(1, 0, 2)


def table_kernel(role_ref, scores_ref, index_ref, out_ref):
    def one(i, total):
        row = index_ref[pl.ds(i, 1), :]
        marks = lax.broadcasted_iota(jnp.int32, (RELS_PAD, WIN), 0) == row
        hot = low(jnp.where(marks, 1.0, 0.0))
        return total + times_transposed(scores_ref[i], hot)

    blank = jnp.zeros((2 * HEADS, RELS_PAD), jnp.float32)

    @pl.when(role_ref[0] != 0)
    def visual():
        out_ref[...] = lax.fori_loop(0, WIN, one, blank, unroll=4)

    @pl.when(role_ref[0] == 0)
    def question():
        out_ref[...] = blank


def table_sums(role, back_scores, rel_index):
    rows = back_scores.reshape(2 * HEADS, WIN, WIN).transpose(1, 0, 2)
    found = pl.pallas_call(
        table_kernel,
        out_shape=jax.ShapeDtypeStruct((2 * HEADS, RELS_PAD), jnp.float32),
        in_specs=[pl.BlockSpec(memory_space=pltpu.SMEM)] + [pl.BlockSpec()] * 2,
        cost_estimate=pl.CostEstimate(
            flops=48 * RELS_PAD * WIN * WIN, bytes_accessed=52 * WIN * WIN, transcendentals=0
        ),
    )(role, rows, rel_index)
    return jnp.sum(found.reshape(HEADS, 2, RELS_PAD), axis=1)[:, :RELS]


def head_lanes(side):
    lane = lax.broadcasted_iota(jnp.int32, (1, LANES), 1)
    return (lane < HEAD_DIM) if side == 0 else (lane >= HEAD_DIM)


def attend_pair(query, keys, values, extras):
    result, logs = None, None
    for side in (0, 1):
        mine = head_lanes(side)
        one = jnp.where(mine, query * SCALE, 0).astype(jnp.bfloat16)
        scores = times_transposed(one, keys) + extras[side]
        top = jnp.max(scores, axis=-1, keepdims=True)
        expo = jnp.exp(scores - top)
        total = jnp.sum(expo, axis=-1, keepdims=True)
        found = product(low(expo), values) / total
        log_total = jnp.broadcast_to(top + jnp.log(total), found.shape)
        result = found if side == 0 else jnp.where(mine, found, result)
        logs = log_total if side == 0 else jnp.where(mine, log_total, logs)
    return low(result), logs


def pair_backward(query, keys, values, extras, logs, back_out):
    back_query, back_keys, back_values, kept = None, None, None, []
    for side in (0, 1):
        mine = head_lanes(side)
        one = jnp.where(mine, query * SCALE, 0).astype(jnp.bfloat16)
        back_one = jnp.where(mine, back_out, 0).astype(jnp.bfloat16)
        scores = times_transposed(one, keys) + extras[side]
        first = side * HEAD_DIM
        shares = jnp.exp(scores - logs[:, first : first + 1])
        back_shares = times_transposed(back_one, values)
        inner = jnp.sum(shares * back_shares, axis=-1, keepdims=True)
        back_scores = low(shares * (back_shares - inner))
        found = product(back_scores, keys) * SCALE
        found_keys = transposed_times(back_scores, one)
        found_values = transposed_times(low(shares), back_one)
        kept.append(back_scores)
        if side == 0:
            back_query, back_keys, back_values = found, found_keys, found_values
        else:
            back_query = jnp.where(mine, found, back_query)
            back_keys, back_values = back_keys + found_keys, back_values + found_values
    return low(back_query), low(back_keys), low(back_values), kept


def question_extra(role_ref, qid, kid):
    shape = (qid.shape[0], kid.shape[1])
    row = lax.broadcasted_iota(jnp.int32, shape, 0) + role_ref[1]
    column = lax.broadcasted_iota(jnp.int32, shape, 1)
    return jnp.where((qid == kid) & (column <= row), 0.0, NEG)


def window_extras(bias_ref, qid, kid):
    same = jnp.where(qid == kid, 0.0, NEG)
    return [bias_ref[0] + same, bias_ref[1] + same]


def self_forward_kernel(
    role_ref, q_ref, k_ref, v_ref, bias_ref, qid_ref, kid_ref, o_ref, log_ref
):
    rows = q_ref.shape[1]

    @pl.when(role_ref[0] == 0)
    def question():
        for s in (0, 1):
            extra = question_extra(role_ref, qid_ref[s], kid_ref[s])
            o_ref[s], log_ref[s] = attend_pair(q_ref[s], k_ref[s], v_ref[s], [extra, extra])

    @pl.when(role_ref[0] != 0)
    def visual():
        for s in (0, 1):
            extras = window_extras(bias_ref, qid_ref[s], kid_ref[s, :, :rows])
            o_ref[s], log_ref[s] = attend_pair(
                q_ref[s], k_ref[s, :rows], v_ref[s, :rows], extras
            )


def self_backward_kernel(
    role_ref,
    q_ref,
    k_ref,
    v_ref,
    bias_ref,
    qid_ref,
    kid_ref,
    log_ref,
    back_ref,
    dq_ref,
    dk_ref,
    dv_ref,
    ds_ref,
):
    rows = q_ref.shape[1]

    @pl.when(role_ref[0] == 0)
    def question():
        ds_ref[...] = jnp.zeros_like(ds_ref)
        for s in (0, 1):
            extra = question_extra(role_ref, qid_ref[s], kid_ref[s])
            dq_ref[s], dk_ref[s], dv_ref[s], unused = pair_backward(
                q_ref[s], k_ref[s], v_ref[s], [extra, extra], log_ref[s], back_ref[s]
            )

    @pl.when(role_ref[0] != 0)
    def visual():
        dk_ref[...] = jnp.zeros_like(dk_ref)
        dv_ref[...] = jnp.zeros_like(dv_ref)
        for s in (0, 1):
            extras = window_extras(bias_ref, qid_ref[s], kid_ref[s, :, :rows])
            dq_ref[s], found_keys, found_values, kept = pair_backward(
                q_ref[s], k_ref[s, :rows], v_ref[s, :rows], extras, log_ref[s], back_ref[s]
            )
            dk_ref[s, :rows] = found_keys
            dv_ref[s, :rows] = found_values
            ds_ref[0, s] = kept[0]
            ds_ref[1, s] = kept[1]


def self_specs(rows, span):
    query = pl.BlockSpec((2, rows, LANES), lambda h, role: (0, 0, h))
    keys = pl.BlockSpec((2, span, LANES), lambda h, role: (0, 0, h))
    bias = pl.BlockSpec((2, rows, rows), lambda h, role: (h, 0, 0))
    qid = pl.BlockSpec((2, rows, 1), lambda h, role: (0, 0, 0))
    kid = pl.BlockSpec((2, 1, span), lambda h, role: (0, 0, 0))
    return query, keys, keys, bias, qid, kid


def self_forward(role, query, keys, values, bias, qid, kid):
    rows, span = query.shape[1], keys.shape[1]
    specs = self_specs(rows, span)
    return pl.pallas_call(
        self_forward_kernel,
        out_shape=[
            jax.ShapeDtypeStruct((2, rows, D), jnp.bfloat16),
            jax.ShapeDtypeStruct((2, rows, D), jnp.float32),
        ],
        grid_spec=pltpu.PrefetchScalarGridSpec(
            num_scalar_prefetch=1, grid=(PAIRS,), in_specs=list(specs), out_specs=[specs[0]] * 2
        ),
        compiler_params=pltpu.CompilerParams(vmem_limit_bytes=24 * MIB),
        cost_estimate=pl.CostEstimate(
            flops=16 * rows * span * D, bytes_accessed=12 * span * D, transcendentals=0
        ),
    )(role, query, keys, values, bias, qid, kid)


def self_backward(role, query, keys, values, bias, qid, kid, logs, back_out):
    rows, span = query.shape[1], keys.shape[1]
    specs = self_specs(rows, span)
    return pl.pallas_call(
        self_backward_kernel,
        out_shape=[
            jax.ShapeDtypeStruct((2, rows, D), jnp.bfloat16),
            jax.ShapeDtypeStruct((2, span, D), jnp.bfloat16),
            jax.ShapeDtypeStruct((2, span, D), jnp.bfloat16),
            jax.ShapeDtypeStruct((HEADS, 2, rows, rows), jnp.bfloat16),
        ],
        grid_spec=pltpu.PrefetchScalarGridSpec(
            num_scalar_prefetch=1,
            grid=(PAIRS,),
            in_specs=list(specs) + [specs[0]] * 2,
            out_specs=[
                specs[0],
                specs[1],
                specs[1],
                pl.BlockSpec((2, 2, rows, rows), lambda h, role: (h, 0, 0, 0)),
            ],
        ),
        compiler_params=pltpu.CompilerParams(vmem_limit_bytes=24 * MIB),
        cost_estimate=pl.CostEstimate(
            flops=40 * rows * span * D, bytes_accessed=16 * span * D, transcendentals=0
        ),
    )(role, query, keys, values, bias, qid, kid, logs, back_out)


def cross_forward_kernel(q_ref, k_ref, v_ref, extra_ref, o_ref, log_ref):
    extra = extra_ref[...]
    o_ref[0], log_ref[0] = attend_pair(q_ref[0], k_ref[0], v_ref[0], [extra, extra])


def cross_backward_kernel(
    q_ref, k_ref, v_ref, extra_ref, log_ref, back_ref, dq_ref, dk_ref, dv_ref
):
    extra = extra_ref[...]
    dq_ref[0], dk_ref[0], dv_ref[0], unused = pair_backward(
        q_ref[0], k_ref[0], v_ref[0], [extra, extra], log_ref[0], back_ref[0]
    )


def cross_specs(rows, span):
    query = pl.BlockSpec((1, rows, LANES), lambda s, h: (s, 0, h))
    keys = pl.BlockSpec((1, span, LANES), lambda s, h: (s, 0, h))
    extra = pl.BlockSpec((1, span), lambda s, h: (0, 0))
    return query, keys, keys, extra


def cross_limit(span):
    return (24 if span <= 2048 else 60) * MIB


def cross_forward(query, keys, values, extra):
    rows, span = query.shape[1], keys.shape[1]
    specs = cross_specs(rows, span)
    return pl.pallas_call(
        cross_forward_kernel,
        out_shape=[
            jax.ShapeDtypeStruct((2, rows, D), jnp.bfloat16),
            jax.ShapeDtypeStruct((2, rows, D), jnp.float32),
        ],
        grid=(2, PAIRS),
        in_specs=list(specs),
        out_specs=[specs[0]] * 2,
        compiler_params=pltpu.CompilerParams(vmem_limit_bytes=cross_limit(span)),
        cost_estimate=pl.CostEstimate(
            flops=32 * rows * span * D, bytes_accessed=8 * span * D, transcendentals=0
        ),
    )(query, keys, values, extra)


def cross_backward(query, keys, values, extra, logs, back_out):
    rows, span = query.shape[1], keys.shape[1]
    specs = cross_specs(rows, span)
    return pl.pallas_call(
        cross_backward_kernel,
        out_shape=[
            jax.ShapeDtypeStruct((2, rows, D), jnp.bfloat16),
            jax.ShapeDtypeStruct((2, span, D), jnp.bfloat16),
            jax.ShapeDtypeStruct((2, span, D), jnp.bfloat16),
        ],
        grid=(2, PAIRS),
        in_specs=list(specs) + [specs[0]] * 2,
        out_specs=[specs[0], specs[1], specs[1]],
        compiler_params=pltpu.CompilerParams(vmem_limit_bytes=cross_limit(span)),
        cost_estimate=pl.CostEstimate(
            flops=80 * rows * span * D, bytes_accessed=16 * span * D, transcendentals=0
        ),
    )(query, keys, values, extra, logs, back_out)


TILES = FF // D
HALF_ROOT = 0.5**0.5
BELL = (0.5 / 3.141592653589793) ** 0.5


def mlp_kernel(places, h_ref, g_ref, up_ref, down_ref, out_ref, back_ref, delta_ref, tile_ref):
    step = pl.program_id(0)
    far, core = step // 2, step % 2
    cut = delta_ref.shape[3]

    for place in range(places):
        for part in range(TILES):
            row = (place * TILES + part) * cut
            tile_ref[row : row + cut] = down_ref[part, place * cut : (place + 1) * cut]
    rows, branch, up, down = h_ref[...], g_ref[...], up_ref[0], tile_ref[...]
    upward = product(rows, up)
    lift = times_transposed(branch, down)
    chance = 0.5 * (1.0 + lax.erf(upward * HALF_ROOT))
    active = low(upward * chance)
    slope = chance + upward * jnp.exp(-0.5 * upward * upward) * BELL
    back_up = low(slope * lift)
    out, back = product(active, down), times_transposed(back_up, up)

    @pl.when(step == 0)
    def start():
        out_ref[...] = out
        back_ref[...] = back

    @pl.when(step > 0)
    def add():
        out_ref[...] += out
        back_ref[...] += back

    delta_up = low(transposed_times(rows, back_up))
    for side in range(2):
        for place in range(2 * places):
            row = (side * 2 * places + place) * cut
            delta_ref[place, step, side] = delta_up[row : row + cut]
    delta_down = low(transposed_times(active, branch))
    for place in range(places):
        for part in range(TILES):
            row = (place * TILES + part) * cut
            delta_ref[core * places + place, TILES + part, far] = delta_down[row : row + cut]


def mlp(rows, branch, weights, blocks):
    count = rows.shape[0]
    cut = D // (4 * blocks)
    resident = pl.BlockSpec((count, D), lambda i: (0, 0))
    shape = (2 * blocks, 2 * TILES, 2, cut, D)
    return pl.pallas_call(
        functools.partial(mlp_kernel, blocks),
        out_shape=[
            jax.ShapeDtypeStruct((count, D), jnp.float32),
            jax.ShapeDtypeStruct((count, D), jnp.float32),
            jax.ShapeDtypeStruct(shape, jnp.bfloat16),
        ],
        grid=(TILES,),
        in_specs=[
            resident,
            resident,
            pl.BlockSpec((1, D, D), lambda i: (4 + i, 0, 0)),
            pl.BlockSpec((TILES, D // TILES, D), lambda i: (2, i, 0)),
        ],
        out_specs=[resident, resident, pl.BlockSpec(shape, lambda i: (0, 0, 0, 0, 0))],
        scratch_shapes=[pltpu.VMEM((D, D), jnp.bfloat16)],
        compiler_params=pltpu.CompilerParams(vmem_limit_bytes=48 * MIB),
        cost_estimate=pl.CostEstimate(
            flops=12 * count * D * FF, bytes_accessed=8 * D * FF, transcendentals=0
        ),
    )(rows, branch, weights, weights)


def body(
    visual_in,
    question_in,
    segment_ids,
    regions,
    rel_index,
    rel_table,
    window_project,
    window_output,
    causal_project,
    causal_output,
    reader_query,
    reader_pair,
    reader_output,
    viewer_query,
    viewer_pair,
    viewer_output,
    visual_up,
    visual_down,
    question_up,
    question_down,
    norm_gains,
    norm_shifts,
    visual_cot,
    question_cot,
):
    blocks = lax.axis_size("blk")
    ringed = blocks == 8
    share = Q_LEN // blocks
    rows = visual_in.shape[0]
    far, core, blk = lax.axis_index("far"), lax.axis_index("core"), lax.axis_index("blk")
    asks = far == 0
    seat = ring_seat(blk, blocks)
    early = -(-(LONGEST - 1) // share)
    reach = min(Q_LEN, share * (early + 1))
    span = reach + rows - share
    first = jnp.clip((seat - early) * share, 0, Q_LEN - reach)
    inset = jnp.where(asks, seat * share - first, 0)
    role = jnp.stack([far, inset]).astype(jnp.int32)
    cut = D // (4 * blocks)

    def own_of(question_side, visual_side):
        return jnp.where(asks, question_side, visual_side)

    class Trade(Once):
        def __init__(self, question_side, visual_side):
            self.kept = own_of(question_side, visual_side)
            self.away = own_of(visual_side, question_side)

        def send(self):
            return swap_far(self.away)

        def receive(self, got):
            self.found = jnp.stack([own_of(self.kept, got), own_of(got, self.kept)])

    def pad_rows(values, total):
        return jnp.pad(values, ((0, total - values.shape[0]),) + ((0, 0),) * (values.ndim - 1))

    def block_of(flat, columns):
        return flat.reshape(-1, columns)

    def cross_squares(query, pair, out):
        pair = pair.reshape(cut, 2, D).transpose(1, 0, 2)
        return jnp.concatenate([query.reshape(1, cut, D), pair, out.reshape(1, cut, D)])

    def mlp_squares(up, down):
        up = up.reshape(cut, TILES, D).transpose(1, 0, 2)
        return jnp.concatenate([up, down.reshape(TILES, cut, D)])

    def matrices(ring, splits):
        if ringed:
            other = {key: swap_core(item) for key, item in ring.pieces.items()}
            return assemble(ring.pieces, other, splits, core, seat, blocks)
        here = lax.all_gather(ring, "blk", axis=0)
        there = swap_core(here)
        pair = jnp.where(core == 0, jnp.stack([here, there]), jnp.stack([there, here]))
        whole = pair.transpose(2, 0, 1, 3, 4).reshape(4 * blocks * ring.shape[1], -1)
        places = [sum(splits[:i]) for i in range(len(splits))]
        return [whole[:, at : at + width] for at, width in zip(places, splits)]

    def ring_of(own):
        return Gather(own, blocks) if ringed else own

    def step(rings, transfers=(), work=()):
        return phase((list(rings) if ringed else []) + list(transfers), work)

    norms = jnp.pad(jnp.concatenate([norm_gains, norm_shifts]), (0, cut * LANES - 2 * norm_gains.size))
    norms = norms.reshape(cut, LANES)
    self_shards = Trade(
        jnp.concatenate([block_of(causal_project, 3 * D), block_of(causal_output, D), norms], 1),
        jnp.concatenate([block_of(window_project, 3 * D), block_of(window_output, D), norms], 1),
    )
    phase([self_shards])
    self_ring = ring_of(self_shards.found)
    later_shards = Trade(
        jnp.concatenate(
            [
                cross_squares(reader_query, reader_pair, reader_output),
                mlp_squares(question_up, question_down),
            ]
        ),
        jnp.concatenate(
            [
                cross_squares(viewer_query, viewer_pair, viewer_output),
                mlp_squares(visual_up, visual_down),
            ]
        ),
    )
    step([self_ring], [later_shards])
    row_shards = Trade(
        pad_rows(lax.dynamic_slice_in_dim(question_in, first, reach, 0), span),
        pad_rows(visual_in, span),
    )
    marks = Trade(segment_ids[0], jnp.pad(regions, (0, Q_LEN - rows)))
    cot = Trade(
        pad_rows(lax.dynamic_slice_in_dim(question_cot, seat * share, share, 0), rows), visual_cot
    )
    later = step([self_ring], [], later_shards.found)
    later = later.transpose(1, 0, 2, 3).reshape(-1, cut, D)
    later = lax.all_gather(later, ("core", "blk"), axis=1, tiled=True).reshape(-1, D, D)
    bias = window_bias(role, rel_table, rel_index)
    bias = step([self_ring], [], bias)
    step([self_ring], [row_shards, marks])
    slots, marks = row_shards.found, marks.found
    key_marks = own_of(
        jnp.pad(
            lax.dynamic_slice_in_dim(marks, first, reach, 1),
            ((0, 0), (0, span - reach)),
            constant_values=-2,
        ),
        marks[:, :span],
    )[:, None, :]
    row_marks = own_of(
        jnp.pad(
            lax.dynamic_slice_in_dim(marks, seat * share, share, 1),
            ((0, 0), (0, rows - share)),
            constant_values=-1,
        ),
        marks[:, :rows],
    )[:, :, None]
    self_weights = matrices(self_ring, (D, D, D, D, LANES))
    self_query_weight, self_key_weight, self_value_weight, self_exit, norm_rows = self_weights
    norm_flat = norm_rows.reshape(4 * blocks, -1)[:, : 2 * norm_gains.size].astype(jnp.float32)
    gains = norm_flat[:, : norm_gains.size].reshape(6, D)
    shifts = norm_flat[:, norm_gains.size :].reshape(6, D)

    own = lax.dynamic_slice_in_dim(slots, inset, rows, 1).astype(jnp.float32)
    self_gain, self_shift = own_of(gains[1], gains[0]), own_of(shifts[1], shifts[0])
    self_norm, self_pull = jax.vjp(normalize, own, self_gain, self_shift)
    self_low = low(self_norm).reshape(2 * rows, D)
    every_low = low(normalize(slots.astype(jnp.float32), self_gain, self_shift))
    every_low = every_low.reshape(2 * span, D)
    self_query = low(product(self_low, self_query_weight)).reshape(2, rows, D)
    self_keys = low(product(every_low, self_key_weight)).reshape(2, span, D)
    self_values = low(product(every_low, self_value_weight)).reshape(2, span, D)
    self_attn, self_logs = self_forward(
        role, self_query, self_keys, self_values, bias, row_marks, key_marks
    )
    self_attn = self_attn.reshape(2 * rows, D)
    rows_one = own + product(self_attn, self_exit).reshape(2, rows, D)

    cross_gain, cross_shift = own_of(gains[2], gains[3]), own_of(shifts[2], shifts[3])
    cross_norm, cross_pull = jax.vjp(normalize, rows_one, cross_gain, cross_shift)
    cross_low = low(cross_norm)
    sent = Once(lambda: swap_far(cross_low))
    phase([sent])
    cross_weights = lax.optimization_barrier([later[i] for i in range(4)])
    cross_query_weight, cross_key_weight, cross_value_weight, cross_exit = cross_weights
    cross_query = low(product(cross_low.reshape(2 * rows, D), cross_query_weight))
    cross_query = cross_query.reshape(2, rows, D)
    source_ring = ring_of(sent.found)
    if ringed:
        for number in range(4):
            phase([source_ring] + ([cot] if number == 0 else []))
        pieces = [source_ring.pieces[k] for k in OFFSETS[:-1]]
        pieces.append(jnp.concatenate([source_ring.pieces["first"], source_ring.pieces["second"]]))
        sources = jnp.concatenate(pieces, axis=1)
    else:
        phase([cot])
        sources = lax.all_gather(sent.found, "blk", axis=1, tiled=True)
    sources = sources.reshape(-1, D)
    cot = cot.found
    column = jnp.arange(blocks * rows) % rows
    cross_extra = own_of(0.0, jnp.where(column < share, 0.0, NEG))[None]
    cross_keys = low(product(sources, cross_key_weight)).reshape(2, -1, D)
    cross_values = low(product(sources, cross_value_weight)).reshape(2, -1, D)
    cross_attn, cross_logs = cross_forward(cross_query, cross_keys, cross_values, cross_extra)
    cross_attn = cross_attn.reshape(2 * rows, D)
    rows_two = rows_one + product(cross_attn, cross_exit).reshape(2, rows, D)

    mlp_gain, mlp_shift = own_of(gains[5], gains[4]), own_of(shifts[5], shifts[4])
    mlp_norm, mlp_pull = jax.vjp(normalize, rows_two, mlp_gain, mlp_shift)
    mlp_low = low(mlp_norm).reshape(2 * rows, D)
    mlp_out, back_mlp, mlp_delta = mlp(mlp_low, cot.reshape(2 * rows, D), later, blocks)
    rows_three = rows_two + mlp_out.reshape(2, rows, D)
    back_mlp_in, gain_mlp, shift_mlp = mlp_pull(back_mlp.reshape(2, rows, D))
    back_two = cot.astype(jnp.float32) + back_mlp_in
    mlp_delta = mlp_delta.reshape(2 * blocks, -1, D)
    mlp_delta = lax.psum_scatter(mlp_delta, ("core", "blk"), scatter_dimension=0, tiled=True)

    class Owners(Once):
        def __init__(self, total):
            self.total = total

        def send(self):
            return swap_far(low(own_of(self.total[1], self.total[0])))

        def receive(self, came):
            mine = own_of(self.total[0], self.total[1]).astype(jnp.float32)
            came = came.astype(jnp.float32)
            self.found = own_of(mine, came), own_of(came, mine)

    class Home(Once):
        def __init__(self, values):
            self.values = values

        def send(self):
            return swap_far(own_of(self.values[1], self.values[0]))

        def receive(self, got):
            kept = own_of(self.values[0], self.values[1])
            self.found = own_of(kept, got)[:share], own_of(got, kept)

    home_out = Home(low(rows_three))

    def by_owner(parts):
        whole = jnp.stack([part.reshape(2, -1, D) for part in parts], 1)
        return whole.reshape(2, 4, -1, D).transpose(2, 1, 0, 3).reshape(2 * blocks * cut, 8, D)

    cross_branch = low(back_two).reshape(2 * rows, D)
    back_attn = low(times_transposed(cross_branch, cross_exit)).reshape(2, rows, D)
    back_query, back_keys, back_values = cross_backward(
        cross_query, cross_keys, cross_values, cross_extra, cross_logs, back_attn
    )
    back_query = back_query.reshape(2 * rows, D)
    back_keys, back_values = back_keys.reshape(-1, D), back_values.reshape(-1, D)
    back_sources = times_transposed(back_keys, cross_key_weight)
    back_sources = back_sources + times_transposed(back_values, cross_value_weight)
    back_sources = back_sources.reshape(2, -1, D)
    if ringed:

        def source_chunk(k):
            at = OFFSETS.index(k) * rows
            return back_sources[:, at : at + rows]

        back_sent = Sum(source_chunk, blocks)
        delta_cross_exit = low(transposed_times(cross_attn, cross_branch))
        delta_cross_query = low(transposed_times(cross_low.reshape(2 * rows, D), back_query))
        back_cross = times_transposed(back_query, cross_query_weight).reshape(2, rows, D)
        works = [
            (delta_cross_exit, delta_cross_query, back_cross),
            low(transposed_times(sources, back_keys)),
            low(transposed_times(sources, back_values)),
            (),
        ]
        extra = [[home_out], [], [], []]
        works = [phase([back_sent] + more, work) for work, more in zip(works, extra)]
        delta_cross_exit, delta_cross_query, back_cross = works[0]
        delta_cross_keys, delta_cross_values = works[1:3]
        back_sent = back_sent.total
    else:
        back_sent = lax.psum_scatter(back_sources, "blk", scatter_dimension=1, tiled=True)
        phase([home_out])
        delta_cross_exit = low(transposed_times(cross_attn, cross_branch))
        delta_cross_query = low(transposed_times(cross_low.reshape(2 * rows, D), back_query))
        back_cross = times_transposed(back_query, cross_query_weight).reshape(2, rows, D)
        delta_cross_keys = low(transposed_times(sources, back_keys))
        delta_cross_values = low(transposed_times(sources, back_values))
    returned = Once(lambda: swap_far(low(back_sent)))
    cross_delta = by_owner(
        [delta_cross_query, delta_cross_keys, delta_cross_values, delta_cross_exit]
    )
    cross_delta, mlp_delta = phase([returned], (cross_delta, mlp_delta))
    cross_delta = lax.psum_scatter(cross_delta, ("core", "blk"), scatter_dimension=0, tiled=True)
    back_cross = back_cross + returned.found.astype(jnp.float32)
    back_cross_in, gain_cross, shift_cross = cross_pull(back_cross)
    back_one = back_two + back_cross_in

    self_branch = low(back_one).reshape(2 * rows, D)
    back_attn = low(times_transposed(self_branch, self_exit)).reshape(2, rows, D)
    back_query, back_keys, back_values, back_scores = self_backward(
        role, self_query, self_keys, self_values, bias, row_marks, key_marks, self_logs, back_attn
    )
    back_query = back_query.reshape(2 * rows, D)
    back_keys, back_values = back_keys.reshape(2 * span, D), back_values.reshape(2 * span, D)
    back_every = times_transposed(back_keys, self_key_weight)
    back_every = back_every + times_transposed(back_values, self_value_weight)
    back_every = back_every.reshape(2, span, D)
    back_self = times_transposed(back_query, self_query_weight).reshape(2, rows, D)

    def for_earlier(j):
        at = jnp.maximum(inset - j * share, 0)
        found = lax.dynamic_slice_in_dim(back_every, at, share, 1)
        return jnp.where(asks & (seat >= j), found, 0.0)

    order = ring_order(blocks)
    earlier_hop = [(order[i], order[i - 1]) for i in range(1, blocks)]

    class Chain:
        def __init__(self):
            self.left, self.state = early, low(for_earlier(early))

        def send(self):
            return lax.ppermute(self.state, "blk", earlier_hop)

        def receive(self, found):
            self.left -= 1
            self.total = found.astype(jnp.float32) + for_earlier(self.left)
            self.state = low(self.total)

    chain = Chain()
    chain.state, back_query, back_keys, back_values = lax.optimization_barrier(
        (chain.state, back_query, back_keys, back_values)
    )
    self_parts = [
        low(transposed_times(self_low, back_query)),
        low(transposed_times(every_low, back_keys)),
        low(transposed_times(every_low, back_values)),
        low(transposed_times(self_attn, self_branch)),
    ]
    question_rows, visual_out = home_out.found
    out_ring = Circle(question_rows, blocks)
    outs = [out_ring] if ringed else []
    self_delta = jnp.stack(self_parts).reshape(4, 2, 2, blocks, cut, D)
    self_delta = phase([chain] + outs, self_delta)
    self_other = Once(
        lambda: swap_core(lax.dynamic_index_in_dim(self_delta, 1 - core, 2, keepdims=False))
    )
    table_part = table_sums(role, back_scores, rel_index)
    table_part = phase([chain, self_other] + outs, table_part)
    self_other = self_other.found
    if ringed:

        def self_chunk(k):
            place = ring_place(seat + k, blocks)
            mine = lax.dynamic_slice(
                self_delta, (0, 0, core, place, 0, 0), (4, 2, 1, 1, cut, D)
            ).reshape(4, 2, cut, D)
            theirs = lax.dynamic_index_in_dim(self_other, place, 2, keepdims=False)
            return mine.astype(jnp.float32) + theirs.astype(jnp.float32)

        self_sum = Sum(self_chunk, blocks)
        sums = [self_sum]
    else:
        kept = lax.dynamic_index_in_dim(self_delta, core, 2, keepdims=False)
        kept = kept.astype(jnp.float32) + self_other.astype(jnp.float32)
        self_total = lax.psum_scatter(kept, "blk", scatter_dimension=2, tiled=True)[:, :, 0]
        sums = []
    mlp_sums = Owners(mlp_delta.reshape(2 * TILES, 2, cut, D).transpose(1, 0, 2, 3))
    for number in range(early - 2):
        phase([chain] + outs + (sums if number < 2 else []))
    back_self = back_self + own_of(
        jnp.pad(chain.total, ((0, 0), (0, rows - share), (0, 0))), back_every[:, :rows]
    )
    back_self_in, gain_self, shift_self = self_pull(back_self)
    back_in = back_one + back_self_in

    blank = jnp.zeros((D,), jnp.float32)
    gain_delta = [
        own_of(blank, gain_self),
        own_of(gain_self, blank),
        own_of(gain_cross, blank),
        own_of(blank, gain_cross),
        own_of(blank, gain_mlp),
        own_of(gain_mlp, blank),
    ]
    shift_delta = [
        own_of(blank, shift_self),
        own_of(shift_self, blank),
        own_of(shift_cross, blank),
        own_of(blank, shift_cross),
        own_of(blank, shift_mlp),
        own_of(shift_mlp, blank),
    ]
    small = jnp.concatenate(gain_delta + shift_delta + [table_part.reshape(-1)])
    size = small.size
    small = jnp.pad(small, (0, LANES * LANES - size)).reshape(LANES, LANES)

    class Everywhere:
        def __init__(self, total):
            self.total, self.bit = total, 0
            self.bits = [("core", 1, 2), ("far", 1, 2)]
            self.bits += [("blk", 1 << i, blocks) for i in range(blocks.bit_length() - 1)]

        def send(self):
            axis, bit, count = self.bits[self.bit]
            return lax.ppermute(self.total, axis, [(i, i ^ bit) for i in range(count)])

        def receive(self, found):
            self.total, self.bit = self.total + found, self.bit + 1

    small = Everywhere(small)
    home_back = Home(low(back_in))
    cross_delta = phase([home_back, mlp_sums] + outs + sums, cross_delta)
    cross_sums = Owners(cross_delta.reshape(cut, 4, 2, D).transpose(2, 1, 0, 3))
    question_back, visual_back = home_back.found
    if ringed:
        back_ring = Gather(question_back, blocks)
        phase([back_ring, small] + outs + sums)
        self_total = self_sum.total
    self_sums = Owners(self_total.transpose(1, 0, 2, 3))
    if ringed:
        for number in range(3):
            more = (outs if out_ring.left else []) + [[], [cross_sums], [self_sums]][number]
            phase([back_ring, small] + more)
        found = [(k, 0, back_ring.pieces[k]) for k in OFFSETS[:-1]]
        found += [(4, 0, back_ring.pieces["first"]), (4, share // 2, back_ring.pieces["second"])]
        question_delta = seats_in_order(found, seat, blocks, jnp.float32)
        found = [(-k, 0, piece) for k, piece in enumerate(out_ring.pieces)]
        question_out = seats_in_order(found, seat, blocks, jnp.bfloat16)
    else:
        both = jnp.stack([question_rows, question_back])
        both = lax.all_gather(both, "blk", axis=0)
        both = jnp.concatenate([both[i] for i in ring_order(blocks)], 1)
        question_out, question_delta = both[0], both[1].astype(jnp.float32)
        phase([cross_sums, self_sums])
    while small.bit < len(small.bits):
        phase([small])
    small = small.total.reshape(-1)
    at = ((2 * far + core) * blocks + blk) * norm_gains.size
    delta_gains = lax.dynamic_slice_in_dim(small, at, norm_gains.size, 0)
    delta_shifts = lax.dynamic_slice_in_dim(small, 6 * D + at, norm_gains.size, 0)
    table_delta = small[12 * D : size].reshape(HEADS, RELS)
    question_shift = small[11 * D : 12 * D]

    def joined(side, start, stop):
        return side[start:stop].transpose(1, 0, 2).reshape(-1)

    causal, window = [[joined(side, 0, 3), joined(side, 3, 4)] for side in self_sums.found]
    reader, viewer = [
        [joined(side, 0, 1), joined(side, 1, 3), joined(side, 3, 4)] for side in cross_sums.found
    ]
    question_mlp, visual_mlp = [
        [joined(side, 0, TILES), side[TILES:].reshape(-1)] for side in mlp_sums.found
    ]
    return (
        visual_out,
        question_out,
        visual_back.astype(jnp.float32),
        question_delta,
        table_delta,
        window[0],
        window[1],
        causal[0],
        causal[1],
        reader[0],
        reader[1],
        reader[2],
        viewer[0],
        viewer[1],
        viewer[2],
        visual_mlp[0],
        visual_mlp[1],
        question_mlp[0],
        question_mlp[1],
        delta_gains,
        delta_shifts,
        question_shift,
    )


def solution(mesh):
    pages, blocks = mesh.devices.shape
    cut = jax.sharding.Mesh(
        mesh.devices.reshape(2, pages // 2, blocks), ("far", "core", "blk")
    )
    flat, whole, by_page = P(("far", "core", "blk")), P(), P(("far", "core"), None)
    split = P(("far", "core", "blk"), None)
    in_specs = (split, by_page, by_page, flat, whole, whole) + (flat,) * 16 + (split, by_page)
    out_specs = (split, by_page, split, by_page, whole) + (flat,) * 16 + (whole,)
    return jax.shard_map(body, mesh=cut, in_specs=in_specs, out_specs=out_specs, check_vma=False)
```

```python
import functools

import jax
import jax.numpy as jnp
from jax import lax
from jax.experimental import pallas as pl
from jax.experimental.pallas import tpu as pltpu
from jax.sharding import PartitionSpec as P

D = 768
HEADS = 12
HEAD_DIM = 64
FF = 3072
Q_LEN = 1024
WIN = 144
RELS = 529
LONGEST = Q_LEN // 2
LANES = 128
PAIRS = D // LANES
RELS_PAD = 544

EPS = 1e-05
NEG = -1000000000.0
SCALE = HEAD_DIM ** (-0.5)
MIB = 1 << 20


def product(left, right):
    return jnp.dot(left, right, preferred_element_type=jnp.float32)


def times_transposed(left, right):
    return lax.dot_general(
        left, right, (((1,), (1,)), ((), ())), preferred_element_type=jnp.float32
    )


def transposed_times(left, right):
    return lax.dot_general(
        left, right, (((0,), (0,)), ((), ())), preferred_element_type=jnp.float32
    )


def low(values):
    return values.astype(jnp.bfloat16)


def normalize(rows, gain, shift):
    mean = jnp.mean(rows, axis=-1, keepdims=True)
    centred = rows - mean
    spread = jnp.mean(centred * centred, axis=-1, keepdims=True)
    return centred * lax.rsqrt(spread + EPS) * gain + shift


def smooth(values):
    return jax.nn.gelu(values, approximate=False)


def ring_order(blocks):
    return tuple(range(0, blocks, 2)) + tuple(range(blocks - 1, 0, -2))


def ring_seat(blk, blocks):
    return jnp.where(blk % 2 == 0, blk // 2, blocks - 1 - blk // 2)


def ring_place(seat, blocks):
    seat = lax.rem(seat + 2 * blocks, blocks)
    return jnp.where(seat < blocks // 2, 2 * seat, 2 * (blocks - 1 - seat) + 1)


def forward_hop(blocks):
    order = ring_order(blocks)
    return [(order[i], order[(i + 1) % blocks]) for i in range(blocks)]


def backward_hop(blocks):
    return [(there, here) for here, there in forward_hop(blocks)]


def swap_far(values):
    return lax.ppermute(values, "far", [(0, 1), (1, 0)])


def swap_core(values):
    return lax.ppermute(values, "core", [(0, 1), (1, 0)])


OFFSETS = (0, -1, 1, -2, 2, -3, 3, 4)


class Ring:
    state = None
    within = None


class Gather(Ring):
    def __init__(self, own):
        self.half = own.shape[0] // 2
        self.pieces, self.step, self.state = {0: own}, 0, (own, own)
        self.places = {0: (own, 0)}

    def receive(self, found):
        self.step += 1
        if self.step == 4:
            self.pieces["first"], self.pieces["second"] = found
            self.places["first"], self.places["second"] = self.within
        else:
            self.pieces[-self.step], self.pieces[self.step] = found
            self.places[-self.step], self.places[self.step] = self.within
            one, two = found
            self.state = (one[: self.half], two[self.half :]) if self.step == 3 else found


class Sum(Ring):
    def __init__(self, chunk):
        self.chunk, self.step = chunk, 0
        most = chunk(4)
        half = most.shape[0] // 2
        self.state = low(most[:half]), low(most[half:])

    def receive(self, found):
        one, two = [item.astype(jnp.float32) for item in found]
        if self.step == 0:
            blank = jnp.zeros(one.shape, jnp.float32)
            one, two = jnp.concatenate([one, blank]), jnp.concatenate([blank, two])
        self.step += 1
        left = 4 - self.step
        if left == 0:
            self.total = self.chunk(0) + one + two
        else:
            self.state = low(self.chunk(left) + one), low(self.chunk(-left) + two)


class Once:
    def __init__(self, send):
        self.send = send

    def receive(self, found):
        self.found = found


def phase(transfers, work=()):
    rings = [item for item in transfers if isinstance(item, Ring)]
    others = [item for item in transfers if not isinstance(item, Ring)]
    states = lax.optimization_barrier([item.state for item in rings])
    both = []
    if rings:
        blocks = lax.axis_size("blk")
        for side, hop in ((0, forward_hop(blocks)), (1, backward_hop(blocks))):
            parts = [state[side] for state in states]
            both.append(
                lax.ppermute(parts[0] if len(parts) == 1 else jnp.concatenate(parts), "blk", hop)
            )
    found = [item.send() for item in others]
    both, found, work = lax.optimization_barrier((both, found, work))
    for item, one in zip(others, found):
        item.receive(one)
    starts = [0, 0]
    for item, state in zip(rings, states):
        pieces = []
        item.within = [(both[side], starts[side]) for side in (0, 1)]
        for side in (0, 1):
            size = state[side].shape[0]
            pieces.append(both[side][starts[side] : starts[side] + size])
            starts[side] += size
        item.receive(tuple(pieces) if len(rings) > 1 else tuple(both))
    return work


def whole_block(array):
    blank = (0,) * len(array.shape)
    return pl.BlockSpec(array.shape, lambda i, where: blank)


def assemble_kernel(plan, count, where_ref, *refs):
    pieces, outs = refs[:count], refs[count:]
    for piece, (index, first, core) in zip(pieces, plan):
        start = 0
        for out in outs:
            width = out.shape[-1]
            for number in range(piece.shape[0]):
                target = (first + number, where_ref[core], where_ref[index])
                out[target] = piece[number, :, start : start + width]
            start += width


def assemble(own, other, splits, core, seat, blocks):
    rows = own[0].shape[1]
    places = [ring_place(seat + k, blocks) for k in OFFSETS]
    where = jnp.stack([core, 1 - core] + places).astype(jnp.int32)
    pieces, plan = [], []
    for side, group in ((0, own), (1, other)):
        for number, offset in enumerate(OFFSETS):
            if offset == 4:
                pieces += [group["first"], group["second"]]
                plan += [(2 + number, 0, side), (2 + number, 1, side)]
            else:
                pieces.append(group[offset])
                plan.append((2 + number, 0, side))
    outs = [jax.ShapeDtypeStruct((2, 2, blocks, rows, width), jnp.bfloat16) for width in splits]
    found = pl.pallas_call(
        functools.partial(assemble_kernel, plan, len(pieces)),
        out_shape=outs,
        grid_spec=pltpu.PrefetchScalarGridSpec(
            num_scalar_prefetch=1,
            grid=(1,),
            in_specs=[whole_block(item) for item in pieces],
            out_specs=[whole_block(item) for item in outs],
        ),
        compiler_params=pltpu.CompilerParams(vmem_limit_bytes=32 * MIB),
        cost_estimate=pl.CostEstimate(
            flops=0, bytes_accessed=16 * blocks * rows * sum(splits), transcendentals=0
        ),
    )(where, *pieces)
    return [item.reshape(4 * blocks * rows, -1) for item in found]


def place_kernel(plan, where_ref, *refs):
    pieces, out = refs[:-1], refs[-1]
    for piece, (index, start, first, last) in zip(pieces, plan):
        found = piece[start : start + last - first]
        out[where_ref[index], first:last] = found.astype(out.dtype)


def seats_in_order(ring, far, seat, blocks, dtype):
    rows, columns = ring.pieces[0].shape
    found = [(k, ring.places[k], 0, rows) for k in OFFSETS[:-1]]
    found += [(4, ring.places["first"], 0, rows // 2), (4, ring.places["second"], rows // 2, rows)]
    where = [lax.rem(seat + item[0] + blocks, blocks) for item in found]
    where = [jnp.where(far == 0, item, blocks - 1 - item) for item in where]
    where = jnp.stack(where).astype(jnp.int32)
    pieces = [item[1][0] for item in found]
    plan = [(i, item[1][1], item[2], item[3]) for i, item in enumerate(found)]
    out = jax.ShapeDtypeStruct((blocks, rows, columns), dtype)
    placed = pl.pallas_call(
        functools.partial(place_kernel, plan),
        out_shape=out,
        grid_spec=pltpu.PrefetchScalarGridSpec(
            num_scalar_prefetch=1,
            grid=(1,),
            in_specs=[whole_block(item) for item in pieces],
            out_specs=whole_block(out),
        ),
        compiler_params=pltpu.CompilerParams(vmem_limit_bytes=24 * MIB),
        cost_estimate=pl.CostEstimate(
            flops=0, bytes_accessed=6 * blocks * rows * columns, transcendentals=0
        ),
    )(where, *pieces)
    return placed.reshape(blocks * rows, columns)


def bias_kernel(part, role_ref, table_ref, index_ref, out_ref):
    count = out_ref.shape[0]

    def one(i, carry):
        row = index_ref[pl.ds(part * count + i, 1), :]
        marks = lax.broadcasted_iota(jnp.int32, (RELS_PAD, WIN), 0) == row
        hot = low(jnp.where(marks, 1.0, 0.0))
        both = jnp.dot(table_ref[...], hot, preferred_element_type=jnp.float32)
        out_ref[i] = both[:16] + both[16:]
        return carry

    @pl.when(role_ref[0] != 0)
    def visual():
        lax.fori_loop(0, count, one, 0, unroll=4)


def window_bias(role, rel_table, rel_index, part, parts):
    table = jnp.pad(rel_table, ((0, 16 - HEADS), (0, RELS_PAD - RELS)))
    coarse = lax.reduce_precision(table, 8, 7)
    both = low(jnp.concatenate([coarse, table - coarse]))
    return pl.pallas_call(
        functools.partial(bias_kernel, part),
        out_shape=jax.ShapeDtypeStruct((WIN // parts, 16, WIN), jnp.float32),
        in_specs=[pl.BlockSpec(memory_space=pltpu.SMEM)] + [pl.BlockSpec()] * 2,
        cost_estimate=pl.CostEstimate(
            flops=64 * RELS_PAD * WIN * WIN // parts,
            bytes_accessed=4 * 17 * WIN * WIN // parts,
            transcendentals=0,
        ),
    )(role, both, rel_index)


def table_kernel(part, role_ref, scores_ref, index_ref, out_ref):
    count = scores_ref.shape[0]

    def one(i, total):
        row = index_ref[pl.ds(part * count + i, 1), :]
        marks = lax.broadcasted_iota(jnp.int32, (RELS_PAD, WIN), 0) == row
        hot = low(jnp.where(marks, 1.0, 0.0))
        return total + times_transposed(scores_ref[i], hot)

    blank = jnp.zeros((2 * HEADS, RELS_PAD), jnp.float32)

    @pl.when(role_ref[0] != 0)
    def visual():
        out_ref[...] = lax.fori_loop(0, count, one, blank, unroll=4)

    @pl.when(role_ref[0] == 0)
    def question():
        out_ref[...] = blank


def table_sums(role, rows, rel_index, part, parts):
    count = WIN // parts
    return pl.pallas_call(
        functools.partial(table_kernel, part),
        out_shape=jax.ShapeDtypeStruct((2 * HEADS, RELS_PAD), jnp.float32),
        grid=(1,),
        in_specs=[
            pl.BlockSpec(memory_space=pltpu.SMEM),
            pl.BlockSpec((count, 2 * HEADS, WIN), lambda i: (part, 0, 0)),
            pl.BlockSpec((WIN, WIN), lambda i: (0, 0)),
        ],
        out_specs=pl.BlockSpec((2 * HEADS, RELS_PAD), lambda i: (0, 0)),
        cost_estimate=pl.CostEstimate(
            flops=48 * RELS_PAD * WIN * count, bytes_accessed=52 * WIN * count, transcendentals=0
        ),
    )(role, rows, rel_index)


def head_lanes(side):
    lane = lax.broadcasted_iota(jnp.int32, (1, LANES), 1)
    return (lane < HEAD_DIM) if side == 0 else (lane >= HEAD_DIM)


def attend_pair(query, keys, values, extras):
    result, logs = None, None
    for side in (0, 1):
        mine = head_lanes(side)
        one = jnp.where(mine, query * SCALE, 0).astype(jnp.bfloat16)
        scores = times_transposed(one, keys) + extras[side]
        top = jnp.max(scores, axis=-1, keepdims=True)
        expo = jnp.exp(scores - top)
        total = jnp.sum(expo, axis=-1, keepdims=True)
        found = product(low(expo), values) / total
        log_total = jnp.broadcast_to(top + jnp.log(total), found.shape)
        result = found if side == 0 else jnp.where(mine, found, result)
        logs = log_total if side == 0 else jnp.where(mine, log_total, logs)
    return low(result), logs


def pair_backward(query, keys, values, extras, logs, back_out):
    back_query, back_keys, back_values, kept = None, None, None, []
    for side in (0, 1):
        mine = head_lanes(side)
        one = jnp.where(mine, query * SCALE, 0).astype(jnp.bfloat16)
        back_one = jnp.where(mine, back_out, 0).astype(jnp.bfloat16)
        scores = times_transposed(one, keys) + extras[side]
        first = side * HEAD_DIM
        shares = jnp.exp(scores - logs[:, first : first + 1])
        back_shares = times_transposed(back_one, values)
        inner = jnp.sum(shares * back_shares, axis=-1, keepdims=True)
        back_scores = low(shares * (back_shares - inner))
        found = product(back_scores, keys) * SCALE
        found_keys = transposed_times(back_scores, one)
        found_values = transposed_times(low(shares), back_one)
        kept.append(back_scores)
        if side == 0:
            back_query, back_keys, back_values = found, found_keys, found_values
        else:
            back_query = jnp.where(mine, found, back_query)
            back_keys, back_values = back_keys + found_keys, back_values + found_values
    return low(back_query), low(back_keys), low(back_values), kept


def question_extra(slot, role_ref, qid, kid):
    shape = (qid.shape[0], kid.shape[1])
    row = lax.broadcasted_iota(jnp.int32, shape, 0) + role_ref[1 + slot]
    column = lax.broadcasted_iota(jnp.int32, shape, 1)
    return jnp.where((qid == kid) & (column <= row), 0.0, NEG)


def window_extras(bias_ref, qid, kid):
    same = jnp.where(qid == kid, 0.0, NEG)
    return [bias_ref[0] + same, bias_ref[1] + same]


def self_forward_kernel(
    role_ref, q_ref, k_ref, v_ref, bias_ref, qid_ref, kid_ref, o_ref, log_ref
):
    rows = q_ref.shape[1]

    @pl.when(role_ref[0] == 0)
    def question():
        for s in (0, 1):
            extra = question_extra(s, role_ref, qid_ref[s], kid_ref[s])
            o_ref[s], log_ref[s] = attend_pair(q_ref[s], k_ref[s], v_ref[s], [extra, extra])

    @pl.when(role_ref[0] != 0)
    def visual():
        for s in (0, 1):
            extras = window_extras(bias_ref, qid_ref[s], kid_ref[s, :, :rows])
            o_ref[s], log_ref[s] = attend_pair(
                q_ref[s], k_ref[s, :rows], v_ref[s, :rows], extras
            )


def self_backward_kernel(
    role_ref,
    q_ref,
    k_ref,
    v_ref,
    bias_ref,
    qid_ref,
    kid_ref,
    log_ref,
    back_ref,
    dq_ref,
    dk_ref,
    dv_ref,
    ds_ref,
):
    rows = q_ref.shape[1]

    @pl.when(role_ref[0] == 0)
    def question():
        ds_ref[...] = jnp.zeros_like(ds_ref)
        for s in (0, 1):
            extra = question_extra(s, role_ref, qid_ref[s], kid_ref[s])
            dq_ref[s], dk_ref[s], dv_ref[s], unused = pair_backward(
                q_ref[s], k_ref[s], v_ref[s], [extra, extra], log_ref[s], back_ref[s]
            )

    @pl.when(role_ref[0] != 0)
    def visual():
        dk_ref[...] = jnp.zeros_like(dk_ref)
        dv_ref[...] = jnp.zeros_like(dv_ref)
        for s in (0, 1):
            extras = window_extras(bias_ref, qid_ref[s], kid_ref[s, :, :rows])
            dq_ref[s], found_keys, found_values, kept = pair_backward(
                q_ref[s], k_ref[s, :rows], v_ref[s, :rows], extras, log_ref[s], back_ref[s]
            )
            dk_ref[s, :rows] = found_keys
            dv_ref[s, :rows] = found_values
            ds_ref[0, s] = kept[0]
            ds_ref[1, s] = kept[1]


def self_specs(rows, span):
    query = pl.BlockSpec((2, rows, LANES), lambda h, role: (0, 0, h))
    keys = pl.BlockSpec((2, span, LANES), lambda h, role: (0, 0, h))
    bias = pl.BlockSpec((2, rows, rows), lambda h, role: (h, 0, 0))
    qid = pl.BlockSpec((2, rows, 1), lambda h, role: (0, 0, 0))
    kid = pl.BlockSpec((2, 1, span), lambda h, role: (0, 0, 0))
    return query, keys, keys, bias, qid, kid


def self_forward(role, query, keys, values, bias, qid, kid):
    rows, span = query.shape[1], keys.shape[1]
    specs = self_specs(rows, span)
    return pl.pallas_call(
        self_forward_kernel,
        out_shape=[
            jax.ShapeDtypeStruct((2, rows, D), jnp.bfloat16),
            jax.ShapeDtypeStruct((2, rows, D), jnp.float32),
        ],
        grid_spec=pltpu.PrefetchScalarGridSpec(
            num_scalar_prefetch=1, grid=(PAIRS,), in_specs=list(specs), out_specs=[specs[0]] * 2
        ),
        compiler_params=pltpu.CompilerParams(vmem_limit_bytes=24 * MIB),
        cost_estimate=pl.CostEstimate(
            flops=16 * rows * span * D, bytes_accessed=12 * span * D, transcendentals=0
        ),
    )(role, query, keys, values, bias, qid, kid)


def self_backward(role, query, keys, values, bias, qid, kid, logs, back_out):
    rows, span = query.shape[1], keys.shape[1]
    specs = self_specs(rows, span)
    return pl.pallas_call(
        self_backward_kernel,
        out_shape=[
            jax.ShapeDtypeStruct((2, rows, D), jnp.bfloat16),
            jax.ShapeDtypeStruct((2, span, D), jnp.bfloat16),
            jax.ShapeDtypeStruct((2, span, D), jnp.bfloat16),
            jax.ShapeDtypeStruct((HEADS, 2, rows, rows), jnp.bfloat16),
        ],
        grid_spec=pltpu.PrefetchScalarGridSpec(
            num_scalar_prefetch=1,
            grid=(PAIRS,),
            in_specs=list(specs) + [specs[0]] * 2,
            out_specs=[
                specs[0],
                specs[1],
                specs[1],
                pl.BlockSpec((2, 2, rows, rows), lambda h, role: (h, 0, 0, 0)),
            ],
        ),
        compiler_params=pltpu.CompilerParams(vmem_limit_bytes=24 * MIB),
        cost_estimate=pl.CostEstimate(
            flops=40 * rows * span * D, bytes_accessed=16 * span * D, transcendentals=0
        ),
    )(role, query, keys, values, bias, qid, kid, logs, back_out)


def cross_forward_kernel(q_ref, k_ref, v_ref, extra_ref, o_ref, log_ref):
    extra = extra_ref[...]
    o_ref[0], log_ref[0] = attend_pair(q_ref[0], k_ref[0], v_ref[0], [extra, extra])


def cross_backward_kernel(
    q_ref, k_ref, v_ref, extra_ref, log_ref, back_ref, dq_ref, dk_ref, dv_ref
):
    extra = extra_ref[...]
    dq_ref[0], dk_ref[0], dv_ref[0], unused = pair_backward(
        q_ref[0], k_ref[0], v_ref[0], [extra, extra], log_ref[0], back_ref[0]
    )


def cross_specs(rows, span):
    query = pl.BlockSpec((1, rows, LANES), lambda s, h: (s, 0, h))
    keys = pl.BlockSpec((1, span, LANES), lambda s, h: (s, 0, h))
    extra = pl.BlockSpec((1, span), lambda s, h: (0, 0))
    return query, keys, keys, extra


def cross_limit(span):
    return (24 if span <= 2048 else 60) * MIB


def cross_forward(query, keys, values, extra):
    rows, span = query.shape[1], keys.shape[1]
    specs = cross_specs(rows, span)
    return pl.pallas_call(
        cross_forward_kernel,
        out_shape=[
            jax.ShapeDtypeStruct((2, rows, D), jnp.bfloat16),
            jax.ShapeDtypeStruct((2, rows, D), jnp.float32),
        ],
        grid=(2, PAIRS),
        in_specs=list(specs),
        out_specs=[specs[0]] * 2,
        compiler_params=pltpu.CompilerParams(vmem_limit_bytes=cross_limit(span)),
        cost_estimate=pl.CostEstimate(
            flops=32 * rows * span * D, bytes_accessed=8 * span * D, transcendentals=0
        ),
    )(query, keys, values, extra)


def cross_backward(query, keys, values, extra, logs, back_out):
    rows, span = query.shape[1], keys.shape[1]
    specs = cross_specs(rows, span)
    return pl.pallas_call(
        cross_backward_kernel,
        out_shape=[
            jax.ShapeDtypeStruct((2, rows, D), jnp.bfloat16),
            jax.ShapeDtypeStruct((2, span, D), jnp.bfloat16),
            jax.ShapeDtypeStruct((2, span, D), jnp.bfloat16),
        ],
        grid=(2, PAIRS),
        in_specs=list(specs) + [specs[0]] * 2,
        out_specs=[specs[0], specs[1], specs[1]],
        compiler_params=pltpu.CompilerParams(vmem_limit_bytes=cross_limit(span)),
        cost_estimate=pl.CostEstimate(
            flops=80 * rows * span * D, bytes_accessed=16 * span * D, transcendentals=0
        ),
    )(query, keys, values, extra, logs, back_out)


TILES = FF // D
HALF_ROOT = 0.5**0.5
BELL = (0.5 / 3.141592653589793) ** 0.5


def mlp_kernel(places, h_ref, g_ref, up_ref, down_ref, out_ref, back_ref, delta_ref, tile_ref):
    step = pl.program_id(0)
    far, core = step // 2, step % 2
    cut = delta_ref.shape[3]

    for place in range(places):
        for part in range(TILES):
            row = (place * TILES + part) * cut
            tile_ref[row : row + cut] = down_ref[part, place * cut : (place + 1) * cut]
    rows, branch, up, down = h_ref[...], g_ref[...], up_ref[0], tile_ref[...]
    upward = product(rows, up)
    lift = times_transposed(branch, down)
    chance = 0.5 * (1.0 + lax.erf(upward * HALF_ROOT))
    active = low(upward * chance)
    slope = chance + upward * jnp.exp(-0.5 * upward * upward) * BELL
    back_up = low(slope * lift)
    out, back = product(active, down), times_transposed(back_up, up)

    @pl.when(step == 0)
    def start():
        out_ref[...] = out
        back_ref[...] = back

    @pl.when(step > 0)
    def add():
        out_ref[...] += out
        back_ref[...] += back

    delta_up = low(transposed_times(rows, back_up))
    for side in range(2):
        for place in range(2 * places):
            row = (side * 2 * places + place) * cut
            delta_ref[place, step, side] = delta_up[row : row + cut]
    delta_down = low(transposed_times(active, branch))
    for place in range(places):
        for part in range(TILES):
            row = (place * TILES + part) * cut
            delta_ref[core * places + place, TILES + part, far] = delta_down[row : row + cut]


def mlp(rows, branch, weights, blocks):
    count = rows.shape[0]
    cut = D // (4 * blocks)
    resident = pl.BlockSpec((count, D), lambda i: (0, 0))
    shape = (2 * blocks, 2 * TILES, 2, cut, D)
    return pl.pallas_call(
        functools.partial(mlp_kernel, blocks),
        out_shape=[
            jax.ShapeDtypeStruct((count, D), jnp.float32),
            jax.ShapeDtypeStruct((count, D), jnp.float32),
            jax.ShapeDtypeStruct(shape, jnp.bfloat16),
        ],
        grid=(TILES,),
        in_specs=[
            resident,
            resident,
            pl.BlockSpec((1, D, D), lambda i: (4 + i, 0, 0)),
            pl.BlockSpec((TILES, D // TILES, D), lambda i: (2, i, 0)),
        ],
        out_specs=[resident, resident, pl.BlockSpec(shape, lambda i: (0, 0, 0, 0, 0))],
        scratch_shapes=[pltpu.VMEM((D, D), jnp.bfloat16)],
        compiler_params=pltpu.CompilerParams(vmem_limit_bytes=48 * MIB),
        cost_estimate=pl.CostEstimate(
            flops=12 * count * D * FF, bytes_accessed=8 * D * FF, transcendentals=0
        ),
    )(rows, branch, weights, weights)


def weight_kernel(places, *refs):
    delta_ref = refs[-1]
    cut = delta_ref.shape[3]
    for number in range(len(refs) // 2):
        delta = low(transposed_times(refs[2 * number][...], refs[2 * number + 1][...]))
        for place in range(places):
            delta_ref[place, number, 0] = delta[place * cut : (place + 1) * cut]


def weight_gradients(pairs, blocks):
    cut = D // (4 * blocks)
    total = sum(rows.shape[0] for rows, unused in pairs)
    if total > 8 * D:
        parts = [low(transposed_times(rows, back)) for rows, back in pairs]
        parts = jnp.stack([part.reshape(2, 2 * blocks, cut, D) for part in parts])
        return parts.transpose(2, 0, 1, 3, 4)
    specs, arrays = [], []
    for rows, back in pairs:
        specs.append(pl.BlockSpec((rows.shape[0], D // 2), lambda i: (0, i)))
        specs.append(pl.BlockSpec(back.shape, lambda i: (0, 0)))
        arrays += [rows, back]
    return pl.pallas_call(
        functools.partial(weight_kernel, 2 * blocks),
        out_shape=jax.ShapeDtypeStruct((2 * blocks, len(pairs), 2, cut, D), jnp.bfloat16),
        grid=(2,),
        in_specs=specs,
        out_specs=pl.BlockSpec(
            (2 * blocks, len(pairs), 1, cut, D), lambda i: (0, 0, i, 0, 0)
        ),
        compiler_params=pltpu.CompilerParams(vmem_limit_bytes=32 * MIB),
        cost_estimate=pl.CostEstimate(
            flops=2 * total * D * D, bytes_accessed=4 * total * D, transcendentals=0
        ),
    )(*arrays)


def body(
    visual_in,
    question_in,
    segment_ids,
    regions,
    rel_index,
    rel_table,
    window_project,
    window_output,
    causal_project,
    causal_output,
    reader_query,
    reader_pair,
    reader_output,
    viewer_query,
    viewer_pair,
    viewer_output,
    visual_up,
    visual_down,
    question_up,
    question_down,
    norm_gains,
    norm_shifts,
    visual_cot,
    question_cot,
):
    blocks = lax.axis_size("blk")
    ringed = blocks == 8
    share = Q_LEN // blocks
    rows = visual_in.shape[0]
    far, core, blk = lax.axis_index("far"), lax.axis_index("core"), lax.axis_index("blk")
    asks = far == 0
    seat = ring_seat(blk, blocks)
    early = -(-(LONGEST - 1) // share)
    reach = min(Q_LEN, share * (early + 1))
    span = reach + rows - share
    turns = (seat, blocks - 1 - seat)
    firsts = [jnp.clip((turn - early) * share, 0, Q_LEN - reach) for turn in turns]
    insets = [jnp.where(far == 0, turn * share - at, 0) for turn, at in zip(turns, firsts)]
    turn = jnp.where(far == 0, turns[0], turns[1])
    first = jnp.where(far == 0, firsts[0], firsts[1])
    role = jnp.stack([far] + insets).astype(jnp.int32)
    cut = D // (4 * blocks)

    def own_of(question_side, visual_side):
        return jnp.where(asks, question_side, visual_side)

    class Trade(Once):
        def __init__(self, question_side, visual_side):
            self.kept = own_of(question_side, visual_side)
            self.away = own_of(visual_side, question_side)

        def begin(self):
            self.coming = swap_far(self.away)

        def send(self):
            return self.coming if hasattr(self, "coming") else swap_far(self.away)

        def receive(self, got):
            self.found = jnp.stack([own_of(self.kept, got), own_of(got, self.kept)])

    def pad_rows(values, total):
        return jnp.pad(values, ((0, total - values.shape[0]),) + ((0, 0),) * (values.ndim - 1))

    def block_of(flat, columns):
        return flat.reshape(-1, columns)

    def cross_squares(query, pair, out):
        pair = pair.reshape(cut, 2, D).transpose(1, 0, 2)
        return jnp.concatenate([query.reshape(1, cut, D), pair, out.reshape(1, cut, D)])

    def mlp_squares(up, down):
        up = up.reshape(cut, TILES, D).transpose(1, 0, 2)
        return jnp.concatenate([up, down.reshape(TILES, cut, D)])

    def matrices(ring, splits):
        if ringed:
            other = {key: swap_core(item) for key, item in ring.pieces.items()}
            return assemble(ring.pieces, other, splits, core, seat, blocks)
        here = lax.all_gather(ring, "blk", axis=0)
        there = swap_core(here)
        pair = jnp.where(core == 0, jnp.stack([here, there]), jnp.stack([there, here]))
        whole = pair.transpose(2, 0, 1, 3, 4).reshape(4 * blocks * ring.shape[1], -1)
        places = [sum(splits[:i]) for i in range(len(splits))]
        return [whole[:, at : at + width] for at, width in zip(places, splits)]

    def ring_of(own):
        return Gather(own) if ringed else own

    def step(rings, transfers=(), work=()):
        return phase((list(rings) if ringed else []) + list(transfers), work)

    norms = jnp.pad(jnp.concatenate([norm_gains, norm_shifts]), (0, cut * LANES - 2 * norm_gains.size))
    norms = norms.reshape(cut, LANES)
    self_shards = Trade(
        jnp.concatenate([block_of(causal_project, 3 * D), block_of(causal_output, D), norms], 1),
        jnp.concatenate([block_of(window_project, 3 * D), block_of(window_output, D), norms], 1),
    )
    cross_shards = Trade(
        cross_squares(reader_query, reader_pair, reader_output),
        cross_squares(viewer_query, viewer_pair, viewer_output),
    )
    cross_shards.kept, cross_shards.away = phase([self_shards], (cross_shards.kept, cross_shards.away))
    self_ring = ring_of(self_shards.found)
    mlp_shards = Trade(mlp_squares(question_up, question_down), mlp_squares(visual_up, visual_down))
    mlp_shards.kept, mlp_shards.away = step(
        [self_ring], [cross_shards], (mlp_shards.kept, mlp_shards.away)
    )
    row_shards = Trade(
        pad_rows(lax.dynamic_slice_in_dim(question_in, first, reach, 0), span),
        pad_rows(visual_in, span),
    )
    marks = Trade(segment_ids[0], jnp.pad(regions, (0, Q_LEN - rows)))
    cot = Trade(
        pad_rows(lax.dynamic_slice_in_dim(question_cot, turn * share, share, 0), rows), visual_cot
    )
    row_shards.away, later = step([self_ring], [mlp_shards], (row_shards.away, cross_shards.found))
    row_shards.begin()
    later = jnp.concatenate([later, mlp_shards.found], 1)
    later = later.transpose(1, 0, 2, 3).reshape(-1, cut, D)
    later = lax.all_gather(later, ("core", "blk"), axis=1, tiled=True).reshape(-1, D, D)
    bias = window_bias(role, rel_table, rel_index, 0, 2)
    bias, rel_table = step([self_ring], [marks], (bias, rel_table))
    bias_rest = window_bias(role, rel_table, rel_index, 1, 2)
    bias_rest = step([self_ring], [row_shards], bias_rest)
    bias = jnp.concatenate([bias, bias_rest])[:, :HEADS].transpose(1, 0, 2)
    slots, marks = row_shards.found, marks.found

    def of_slots(values, starts, size):
        return jnp.stack(
            [lax.dynamic_slice_in_dim(values[i], start, size, 0) for i, start in enumerate(starts)]
        )

    key_marks = own_of(
        jnp.pad(
            of_slots(marks, firsts, reach), ((0, 0), (0, span - reach)), constant_values=-2
        ),
        marks[:, :span],
    )[:, None, :]
    row_marks = own_of(
        jnp.pad(
            of_slots(marks, [turn * share for turn in turns], share),
            ((0, 0), (0, rows - share)),
            constant_values=-1,
        ),
        marks[:, :rows],
    )[:, :, None]
    self_weights = matrices(self_ring, (D, D, D, D, LANES))
    self_query_weight, self_key_weight, self_value_weight, self_exit, norm_rows = self_weights
    norm_flat = norm_rows.reshape(4 * blocks, -1)[:, : 2 * norm_gains.size].astype(jnp.float32)
    gains = norm_flat[:, : norm_gains.size].reshape(6, D)
    shifts = norm_flat[:, norm_gains.size :].reshape(6, D)

    own = of_slots(slots, insets, rows).astype(jnp.float32)
    self_gain, self_shift = own_of(gains[1], gains[0]), own_of(shifts[1], shifts[0])
    self_norm, self_pull = jax.vjp(normalize, own, self_gain, self_shift)
    self_low = low(self_norm).reshape(2 * rows, D)
    every_low = low(normalize(slots.astype(jnp.float32), self_gain, self_shift))
    every_low = every_low.reshape(2 * span, D)
    self_query = low(product(self_low, self_query_weight)).reshape(2, rows, D)
    self_keys = low(product(every_low, self_key_weight)).reshape(2, span, D)
    self_values = low(product(every_low, self_value_weight)).reshape(2, span, D)
    self_attn, self_logs = self_forward(
        role, self_query, self_keys, self_values, bias, row_marks, key_marks
    )
    self_attn = self_attn.reshape(2 * rows, D)
    rows_one = own + product(self_attn, self_exit).reshape(2, rows, D)

    cross_gain, cross_shift = own_of(gains[2], gains[3]), own_of(shifts[2], shifts[3])
    cross_norm, cross_pull = jax.vjp(normalize, rows_one, cross_gain, cross_shift)
    cross_low = low(cross_norm)
    sent = Once(lambda: swap_far(cross_low))
    phase([sent])
    cross_weights = lax.optimization_barrier([later[i] for i in range(4)])
    cross_query_weight, cross_key_weight, cross_value_weight, cross_exit = cross_weights
    cross_query = low(product(cross_low.reshape(2 * rows, D), cross_query_weight))
    cross_query = cross_query.reshape(2, rows, D)
    source_ring = ring_of(sent.found)
    if ringed:
        for number in range(4):
            phase([source_ring] + ([cot] if number == 0 else []))
        pieces = [source_ring.pieces[k] for k in OFFSETS[:-1]]
        pieces.append(jnp.concatenate([source_ring.pieces["first"], source_ring.pieces["second"]]))
        sources = jnp.concatenate(pieces, axis=1)
    else:
        phase([cot])
        sources = lax.all_gather(sent.found, "blk", axis=1, tiled=True)
    sources = sources.reshape(-1, D)
    cot = cot.found
    column = jnp.arange(blocks * rows) % rows
    cross_extra = own_of(0.0, jnp.where(column < share, 0.0, NEG))[None]
    cross_keys = low(product(sources, cross_key_weight)).reshape(2, -1, D)
    cross_values = low(product(sources, cross_value_weight)).reshape(2, -1, D)
    cross_attn, cross_logs = cross_forward(cross_query, cross_keys, cross_values, cross_extra)
    cross_attn = cross_attn.reshape(2 * rows, D)
    rows_two = rows_one + product(cross_attn, cross_exit).reshape(2, rows, D)

    mlp_gain, mlp_shift = own_of(gains[5], gains[4]), own_of(shifts[5], shifts[4])
    mlp_norm, mlp_pull = jax.vjp(normalize, rows_two, mlp_gain, mlp_shift)
    mlp_low = low(mlp_norm).reshape(2 * rows, D)
    mlp_out, back_mlp, mlp_delta = mlp(mlp_low, cot.reshape(2 * rows, D), later, blocks)
    rows_three = rows_two + mlp_out.reshape(2, rows, D)
    back_mlp_in, gain_mlp, shift_mlp = mlp_pull(back_mlp.reshape(2, rows, D))
    back_two = cot.astype(jnp.float32) + back_mlp_in
    mlp_delta = mlp_delta.reshape(2, blocks, -1, D)

    class Shares:
        def __init__(self, delta):
            self.delta = delta
            self.swap = Once(
                lambda: swap_core(lax.dynamic_index_in_dim(delta, 1 - core, 0, keepdims=False))
            )

        def start(self):
            if ringed:
                self.ring = Sum(self.chunk)
            else:
                kept = lax.dynamic_index_in_dim(self.delta, core, 0, keepdims=False)
                kept = kept.astype(jnp.float32) + self.swap.found.astype(jnp.float32)
                self.sum = lax.psum_scatter(kept, "blk", scatter_dimension=0, tiled=True)[0]

        def chunk(self, k):
            place = ring_place(seat + k, blocks)
            mine = lax.dynamic_slice(self.delta, (core, place, 0, 0), (1, 1) + self.delta.shape[2:])
            theirs = lax.dynamic_index_in_dim(self.swap.found, place, 0, keepdims=False)
            mine = mine.reshape(theirs.shape)
            return mine.astype(jnp.float32) + theirs.astype(jnp.float32)

        def rings(self):
            return [self.ring] if ringed else []

        def total(self):
            found = self.ring.total if ringed else self.sum
            return found.reshape(-1, 2, cut, D).transpose(1, 0, 2, 3)

    mlp_shares = Shares(mlp_delta)
    class Owners(Once):
        def __init__(self, total):
            self.total = total

        def send(self):
            return swap_far(low(own_of(self.total[1], self.total[0])))

        def receive(self, came):
            mine = own_of(self.total[0], self.total[1]).astype(jnp.float32)
            came = came.astype(jnp.float32)
            self.found = own_of(mine, came), own_of(came, mine)

    class Home(Once):
        def __init__(self, values):
            self.values = values

        def send(self):
            return swap_far(own_of(self.values[1], self.values[0]))

        def receive(self, got):
            kept = own_of(self.values[0], self.values[1])
            self.found = own_of(kept, got)[:share], own_of(got, kept)

    home_out = Home(low(rows_three))

    cross_branch = low(back_two).reshape(2 * rows, D)
    back_attn = low(times_transposed(cross_branch, cross_exit)).reshape(2, rows, D)
    back_attn = phase([mlp_shares.swap], back_attn)
    mlp_shares.start()
    back_query, back_keys, back_values = phase(
        mlp_shares.rings(),
        cross_backward(cross_query, cross_keys, cross_values, cross_extra, cross_logs, back_attn),
    )
    back_query = back_query.reshape(2 * rows, D)
    back_keys, back_values = back_keys.reshape(-1, D), back_values.reshape(-1, D)
    back_sources = times_transposed(back_keys, cross_key_weight)
    back_sources = back_sources + times_transposed(back_values, cross_value_weight)
    back_sources = phase(mlp_shares.rings(), back_sources.reshape(2, -1, D))

    def owned(delta):
        delta = delta.reshape(2 * blocks, -1, D)
        return lax.psum_scatter(delta, ("core", "blk"), scatter_dimension=0, tiled=True)

    cross_pairs = [
        (cross_low.reshape(2 * rows, D), back_query),
        (sources, back_keys),
        (sources, back_values),
        (cross_attn, cross_branch),
    ]
    if ringed:

        def source_chunk(k):
            at = OFFSETS.index(k) * rows
            return back_sources[:, at : at + rows].reshape(2 * rows, D)

        back_sent = Sum(source_chunk)
        cross_delta = weight_gradients(cross_pairs, blocks)
        back_cross = times_transposed(back_query, cross_query_weight).reshape(2, rows, D)
        works = [back_cross, cross_delta, (), ()]
        extra = [[home_out], [], [], []]
        works = [phase([back_sent] + more, work) for work, more in zip(works, extra)]
        back_cross, cross_delta = works[:2]
        cross_delta = owned(cross_delta)
        back_sent = back_sent.total.reshape(2, rows, D)
    else:
        back_sent = lax.psum_scatter(back_sources, "blk", scatter_dimension=1, tiled=True)
        phase([home_out])
        cross_delta = owned(weight_gradients(cross_pairs, blocks))
        back_cross = times_transposed(back_query, cross_query_weight).reshape(2, rows, D)
    returned = Once(lambda: swap_far(low(back_sent)))
    phase([returned] + mlp_shares.rings())
    back_cross = back_cross + returned.found.astype(jnp.float32)
    back_cross_in, gain_cross, shift_cross = cross_pull(back_cross)
    back_one = back_two + back_cross_in

    self_branch = low(back_one).reshape(2 * rows, D)
    back_attn = low(times_transposed(self_branch, self_exit)).reshape(2, rows, D)
    back_query, back_keys, back_values, back_scores = phase(
        mlp_shares.rings(),
        self_backward(
            role,
            self_query,
            self_keys,
            self_values,
            bias,
            row_marks,
            key_marks,
            self_logs,
            back_attn,
        ),
    )
    back_query = back_query.reshape(2 * rows, D)
    back_keys, back_values = back_keys.reshape(2 * span, D), back_values.reshape(2 * span, D)
    back_every = times_transposed(back_keys, self_key_weight)
    back_every = back_every + times_transposed(back_values, self_value_weight)
    back_every = back_every.reshape(2, span, D)
    back_self = times_transposed(back_query, self_query_weight).reshape(2, rows, D)

    def for_earlier(j):
        parts = []
        for slot in (0, 1):
            at = jnp.maximum(insets[slot] - j * share, 0)
            found = lax.dynamic_slice_in_dim(back_every[slot], at, share, 0)
            parts.append(jnp.where(asks & (turns[slot] >= j), found, 0.0))
        return parts

    class Chain(Ring):
        def __init__(self):
            self.left = early
            self.set(for_earlier(early))

        def set(self, total):
            self.total = total
            self.state = low(total[1]), low(total[0])

        def receive(self, found):
            self.left -= 1
            own = for_earlier(self.left)
            self.set([found[1].astype(jnp.float32) + own[0], found[0].astype(jnp.float32) + own[1]])

    chain = Chain()
    chain.state, back_query, back_keys, back_values = lax.optimization_barrier(
        (chain.state, back_query, back_keys, back_values)
    )
    self_pairs = [
        (self_low, back_query),
        (every_low, back_keys),
        (every_low, back_values),
        (self_attn, self_branch),
    ]
    self_delta = weight_gradients(self_pairs, blocks).reshape(2, blocks, 8 * cut, D)
    question_rows, visual_out = home_out.found
    outs = [Gather(question_rows)] if ringed else []
    score_rows = back_scores.reshape(2 * HEADS, WIN, WIN).transpose(1, 0, 2)
    table_parts = [table_sums(role, score_rows, rel_index, part, 4) for part in range(4)]
    self_delta, table_parts[0] = phase([chain] + outs, (self_delta, table_parts[0]))
    self_shares = Shares(self_delta)
    table_parts[1], cross_delta = phase(
        [chain, self_shares.swap] + outs, (table_parts[1], cross_delta)
    )
    self_shares.start()
    sums = self_shares.rings()
    for number in range(early - 2):
        work = table_parts[2 + number] if number < 2 else ()
        work = phase([chain] + (outs + sums if number < 2 else []), work)
        if number < 2:
            table_parts[2 + number] = work
    table_part = sum(table_parts).reshape(HEADS, 2, RELS_PAD)
    table_part = jnp.sum(table_part, axis=1)[:, :RELS]
    back_self = back_self + own_of(
        jnp.pad(jnp.stack(chain.total), ((0, 0), (0, rows - share), (0, 0))), back_every[:, :rows]
    )
    back_self_in, gain_self, shift_self = self_pull(back_self)
    back_in = back_one + back_self_in

    blank = jnp.zeros((D,), jnp.float32)
    gain_delta = [
        own_of(blank, gain_self),
        own_of(gain_self, blank),
        own_of(gain_cross, blank),
        own_of(blank, gain_cross),
        own_of(blank, gain_mlp),
        own_of(gain_mlp, blank),
    ]
    shift_delta = [
        own_of(blank, shift_self),
        own_of(shift_self, blank),
        own_of(shift_cross, blank),
        own_of(blank, shift_cross),
        own_of(blank, shift_mlp),
        own_of(shift_mlp, blank),
    ]
    small = jnp.concatenate(gain_delta + shift_delta + [table_part.reshape(-1)])
    size = small.size
    small = jnp.pad(small, (0, LANES * LANES - size)).reshape(LANES, LANES)

    class Everywhere:
        def __init__(self, total):
            self.total, self.bit = total, 0
            self.bits = [("far", 1, 2)]
            self.bits += [("blk", 1 << i, blocks) for i in range(blocks.bit_length() - 1)]
            self.bits += [("core", 1, 2)]

        def send(self):
            axis, bit, count = self.bits[self.bit]
            return lax.ppermute(self.total, axis, [(i, i ^ bit) for i in range(count)])

        def receive(self, found):
            self.total, self.bit = self.total + found, self.bit + 1

    small = Everywhere(small)
    home_back = Home(low(back_in))
    mlp_sums = Owners(mlp_shares.total())
    phase([home_back, mlp_sums, small] + sums)
    cross_sums = Owners(cross_delta.reshape(4, 2, cut, D).transpose(1, 0, 2, 3))
    question_back, visual_back = home_back.found
    if ringed:
        back_ring = Gather(question_back)
        phase([back_ring, small] + sums)
    self_sums = Owners(self_shares.total())
    if ringed:
        for number in range(3):
            phase([back_ring, small] + [[], [cross_sums], [self_sums]][number])
        question_delta = seats_in_order(back_ring, far, seat, blocks, jnp.float32)
        question_out = seats_in_order(outs[0], far, seat, blocks, jnp.bfloat16)
    else:
        both = jnp.stack([question_rows, question_back])
        both = lax.all_gather(both, "blk", axis=0)
        order = ring_order(blocks)
        both = own_of(
            jnp.concatenate([both[i] for i in order], 1),
            jnp.concatenate([both[i] for i in order[::-1]], 1),
        )
        question_out, question_delta = both[0], both[1].astype(jnp.float32)
        phase([cross_sums, self_sums])
    while small.bit < len(small.bits):
        phase([small])
    small = small.total.reshape(-1)
    at = ((2 * far + core) * blocks + blk) * norm_gains.size
    delta_gains = lax.dynamic_slice_in_dim(small, at, norm_gains.size, 0)
    delta_shifts = lax.dynamic_slice_in_dim(small, 6 * D + at, norm_gains.size, 0)
    table_delta = small[12 * D : size].reshape(HEADS, RELS)
    question_shift = small[11 * D : 12 * D]

    def joined(side, start, stop):
        return side[start:stop].transpose(1, 0, 2).reshape(-1)

    causal, window = [[joined(side, 0, 3), joined(side, 3, 4)] for side in self_sums.found]
    reader, viewer = [
        [joined(side, 0, 1), joined(side, 1, 3), joined(side, 3, 4)] for side in cross_sums.found
    ]
    question_mlp, visual_mlp = [
        [joined(side, 0, TILES), side[TILES:].reshape(-1)] for side in mlp_sums.found
    ]
    return (
        visual_out,
        question_out,
        visual_back.astype(jnp.float32),
        question_delta,
        table_delta,
        window[0],
        window[1],
        causal[0],
        causal[1],
        reader[0],
        reader[1],
        reader[2],
        viewer[0],
        viewer[1],
        viewer[2],
        visual_mlp[0],
        visual_mlp[1],
        question_mlp[0],
        question_mlp[1],
        delta_gains,
        delta_shifts,
        question_shift,
    )


def solution(mesh):
    pages, blocks = mesh.devices.shape
    cut = jax.sharding.Mesh(
        mesh.devices.reshape(2, pages // 2, blocks), ("far", "core", "blk")
    )
    flat, whole, by_page = P(("far", "core", "blk")), P(), P(("far", "core"), None)
    split = P(("far", "core", "blk"), None)
    in_specs = (split, by_page, by_page, flat, whole, whole) + (flat,) * 16 + (split, by_page)
    out_specs = (split, by_page, split, by_page, whole) + (flat,) * 16 + (whole,)
    return jax.shard_map(body, mesh=cut, in_specs=in_specs, out_specs=out_specs, check_vma=False)
```

```python
import functools

import jax
import jax.numpy as jnp
from jax import lax
from jax.experimental import pallas as pl
from jax.experimental.pallas import tpu as pltpu
from jax.sharding import PartitionSpec as P

D = 768
HEADS = 12
HEAD_DIM = 64
FF = 3072
Q_LEN = 1024
WIN = 144
RELS = 529
LONGEST = Q_LEN // 2
LANES = 128
PAIRS = D // LANES
RELS_PAD = 544

EPS = 1e-05
NEG = -1000000000.0
SCALE = HEAD_DIM ** (-0.5)
MIB = 1 << 20


def product(left, right):
    return jnp.dot(left, right, preferred_element_type=jnp.float32)


def times_transposed(left, right):
    return lax.dot_general(
        left, right, (((1,), (1,)), ((), ())), preferred_element_type=jnp.float32
    )


def transposed_times(left, right):
    return lax.dot_general(
        left, right, (((0,), (0,)), ((), ())), preferred_element_type=jnp.float32
    )


def low(values):
    return values.astype(jnp.bfloat16)


def normalize(rows, gain, shift):
    mean = jnp.mean(rows, axis=-1, keepdims=True)
    centred = rows - mean
    spread = jnp.mean(centred * centred, axis=-1, keepdims=True)
    return centred * lax.rsqrt(spread + EPS) * gain + shift


def smooth(values):
    return jax.nn.gelu(values, approximate=False)


def ring_order(blocks):
    return tuple(range(0, blocks, 2)) + tuple(range(blocks - 1, 0, -2))


def ring_seat(blk, blocks):
    return jnp.where(blk % 2 == 0, blk // 2, blocks - 1 - blk // 2)


def ring_place(seat, blocks):
    seat = lax.rem(seat + 2 * blocks, blocks)
    return jnp.where(seat < blocks // 2, 2 * seat, 2 * (blocks - 1 - seat) + 1)


def forward_hop(blocks):
    order = ring_order(blocks)
    return [(order[i], order[(i + 1) % blocks]) for i in range(blocks)]


def backward_hop(blocks):
    return [(there, here) for here, there in forward_hop(blocks)]


def swap_far(values):
    return lax.ppermute(values, "far", [(0, 1), (1, 0)])


def swap_core(values):
    return lax.ppermute(values, "core", [(0, 1), (1, 0)])


OFFSETS = (0, -1, 1, -2, 2, -3, 3, 4)


class Ring:
    state = None
    within = None


class Gather(Ring):
    def __init__(self, own):
        self.half = own.shape[0] // 2
        self.pieces, self.step, self.state = {0: own}, 0, (own, own)
        self.places = {0: (own, 0)}

    def receive(self, found):
        self.step += 1
        if self.step == 4:
            self.pieces["first"], self.pieces["second"] = found
            self.places["first"], self.places["second"] = self.within
        else:
            self.pieces[-self.step], self.pieces[self.step] = found
            self.places[-self.step], self.places[self.step] = self.within
            one, two = found
            self.state = (one[: self.half], two[self.half :]) if self.step == 3 else found


class Sum(Ring):
    def __init__(self, chunk):
        self.chunk, self.step = chunk, 0
        most = chunk(4)
        half = most.shape[0] // 2
        self.state = low(most[:half]), low(most[half:])

    def receive(self, found):
        one, two = [item.astype(jnp.float32) for item in found]
        if self.step == 0:
            blank = jnp.zeros(one.shape, jnp.float32)
            one, two = jnp.concatenate([one, blank]), jnp.concatenate([blank, two])
        self.step += 1
        left = 4 - self.step
        if left == 0:
            self.total = self.chunk(0) + one + two
        else:
            self.state = low(self.chunk(left) + one), low(self.chunk(-left) + two)


class Once:
    def __init__(self, send):
        self.send = send

    def receive(self, found):
        self.found = found


def phase(transfers, work=()):
    rings = [item for item in transfers if isinstance(item, Ring)]
    others = [item for item in transfers if not isinstance(item, Ring)]
    states = lax.optimization_barrier([item.state for item in rings])
    both = []
    if rings:
        blocks = lax.axis_size("blk")
        for side, hop in ((0, forward_hop(blocks)), (1, backward_hop(blocks))):
            parts = [state[side] for state in states]
            both.append(
                lax.ppermute(parts[0] if len(parts) == 1 else jnp.concatenate(parts), "blk", hop)
            )
    found = [item.send() for item in others]
    both, found, work = lax.optimization_barrier((both, found, work))
    for item, one in zip(others, found):
        item.receive(one)
    starts = [0, 0]
    for item, state in zip(rings, states):
        pieces = []
        item.within = [(both[side], starts[side]) for side in (0, 1)]
        for side in (0, 1):
            size = state[side].shape[0]
            pieces.append(both[side][starts[side] : starts[side] + size])
            starts[side] += size
        item.receive(tuple(pieces) if len(rings) > 1 else tuple(both))
    return work


def whole_block(array):
    blank = (0,) * len(array.shape)
    return pl.BlockSpec(array.shape, lambda i, where: blank)


def assemble_kernel(plan, count, where_ref, *refs):
    pieces, outs = refs[:count], refs[count:]
    for piece, (index, first, core) in zip(pieces, plan):
        start = 0
        for out in outs:
            width = out.shape[-1]
            for number in range(piece.shape[0]):
                target = (first + number, where_ref[core], where_ref[index])
                out[target] = piece[number, :, start : start + width]
            start += width


def assemble(own, other, splits, core, seat, blocks):
    rows = own[0].shape[1]
    places = [ring_place(seat + k, blocks) for k in OFFSETS]
    where = jnp.stack([core, 1 - core] + places).astype(jnp.int32)
    pieces, plan = [], []
    for side, group in ((0, own), (1, other)):
        for number, offset in enumerate(OFFSETS):
            if offset == 4:
                pieces += [group["first"], group["second"]]
                plan += [(2 + number, 0, side), (2 + number, 1, side)]
            else:
                pieces.append(group[offset])
                plan.append((2 + number, 0, side))
    outs = [jax.ShapeDtypeStruct((2, 2, blocks, rows, width), jnp.bfloat16) for width in splits]
    found = pl.pallas_call(
        functools.partial(assemble_kernel, plan, len(pieces)),
        out_shape=outs,
        grid_spec=pltpu.PrefetchScalarGridSpec(
            num_scalar_prefetch=1,
            grid=(1,),
            in_specs=[whole_block(item) for item in pieces],
            out_specs=[whole_block(item) for item in outs],
        ),
        compiler_params=pltpu.CompilerParams(vmem_limit_bytes=32 * MIB),
        cost_estimate=pl.CostEstimate(
            flops=0, bytes_accessed=16 * blocks * rows * sum(splits), transcendentals=0
        ),
    )(where, *pieces)
    return [item.reshape(4 * blocks * rows, -1) for item in found]


def place_kernel(plan, where_ref, *refs):
    pieces, out = refs[:-1], refs[-1]
    for piece, (index, start, first, last) in zip(pieces, plan):
        found = piece[start : start + last - first]
        out[where_ref[index], first:last] = found.astype(out.dtype)


def seats_in_order(ring, far, seat, blocks, dtype):
    rows, columns = ring.pieces[0].shape
    found = [(k, ring.places[k], 0, rows) for k in OFFSETS[:-1]]
    found += [(4, ring.places["first"], 0, rows // 2), (4, ring.places["second"], rows // 2, rows)]
    where = [lax.rem(seat + item[0] + blocks, blocks) for item in found]
    where = [jnp.where(far == 0, item, blocks - 1 - item) for item in where]
    where = jnp.stack(where).astype(jnp.int32)
    pieces = [item[1][0] for item in found]
    plan = [(i, item[1][1], item[2], item[3]) for i, item in enumerate(found)]
    out = jax.ShapeDtypeStruct((blocks, rows, columns), dtype)
    placed = pl.pallas_call(
        functools.partial(place_kernel, plan),
        out_shape=out,
        grid_spec=pltpu.PrefetchScalarGridSpec(
            num_scalar_prefetch=1,
            grid=(1,),
            in_specs=[whole_block(item) for item in pieces],
            out_specs=whole_block(out),
        ),
        compiler_params=pltpu.CompilerParams(vmem_limit_bytes=24 * MIB),
        cost_estimate=pl.CostEstimate(
            flops=0, bytes_accessed=6 * blocks * rows * columns, transcendentals=0
        ),
    )(where, *pieces)
    return placed.reshape(blocks * rows, columns)


def bias_kernel(part, role_ref, table_ref, index_ref, out_ref):
    count = out_ref.shape[0]

    def one(i, carry):
        row = index_ref[pl.ds(part * count + i, 1), :]
        marks = lax.broadcasted_iota(jnp.int32, (RELS_PAD, WIN), 0) == row
        hot = low(jnp.where(marks, 1.0, 0.0))
        both = jnp.dot(table_ref[...], hot, preferred_element_type=jnp.float32)
        out_ref[i] = both[:16] + both[16:]
        return carry

    @pl.when(role_ref[0] != 0)
    def visual():
        lax.fori_loop(0, count, one, 0, unroll=4)


def window_bias(role, rel_table, rel_index, part, parts):
    table = jnp.pad(rel_table, ((0, 16 - HEADS), (0, RELS_PAD - RELS)))
    coarse = lax.reduce_precision(table, 8, 7)
    both = low(jnp.concatenate([coarse, table - coarse]))
    return pl.pallas_call(
        functools.partial(bias_kernel, part),
        out_shape=jax.ShapeDtypeStruct((WIN // parts, 16, WIN), jnp.float32),
        in_specs=[pl.BlockSpec(memory_space=pltpu.SMEM)] + [pl.BlockSpec()] * 2,
        cost_estimate=pl.CostEstimate(
            flops=64 * RELS_PAD * WIN * WIN // parts,
            bytes_accessed=4 * 17 * WIN * WIN // parts,
            transcendentals=0,
        ),
    )(role, both, rel_index)


def table_kernel(part, role_ref, scores_ref, index_ref, out_ref):
    count = scores_ref.shape[0]

    def one(i, total):
        row = index_ref[pl.ds(part * count + i, 1), :]
        marks = lax.broadcasted_iota(jnp.int32, (RELS_PAD, WIN), 0) == row
        hot = low(jnp.where(marks, 1.0, 0.0))
        return total + times_transposed(scores_ref[i], hot)

    blank = jnp.zeros((2 * HEADS, RELS_PAD), jnp.float32)

    @pl.when(role_ref[0] != 0)
    def visual():
        out_ref[...] = lax.fori_loop(0, count, one, blank, unroll=4)

    @pl.when(role_ref[0] == 0)
    def question():
        out_ref[...] = blank


def table_sums(role, rows, rel_index, part, parts):
    count = WIN // parts
    return pl.pallas_call(
        functools.partial(table_kernel, part),
        out_shape=jax.ShapeDtypeStruct((2 * HEADS, RELS_PAD), jnp.float32),
        grid=(1,),
        in_specs=[
            pl.BlockSpec(memory_space=pltpu.SMEM),
            pl.BlockSpec((count, 2 * HEADS, WIN), lambda i: (part, 0, 0)),
            pl.BlockSpec((WIN, WIN), lambda i: (0, 0)),
        ],
        out_specs=pl.BlockSpec((2 * HEADS, RELS_PAD), lambda i: (0, 0)),
        cost_estimate=pl.CostEstimate(
            flops=48 * RELS_PAD * WIN * count, bytes_accessed=52 * WIN * count, transcendentals=0
        ),
    )(role, rows, rel_index)


def both_heads(rows):
    first = lax.broadcasted_iota(jnp.int32, (1, LANES), 1) < HEAD_DIM
    blank = jnp.zeros_like(rows)
    return jnp.concatenate([jnp.where(first, rows, blank), jnp.where(first, blank, rows)])


def own_lanes(stacked):
    rows = stacked.shape[0] // 2
    first = lax.broadcasted_iota(jnp.int32, (1, LANES), 1) < HEAD_DIM
    return jnp.where(first, stacked[:rows], stacked[rows:])


def attend_pair(query, keys, values, extra):
    scores = times_transposed(both_heads(query * SCALE), keys) + extra
    top = jnp.max(scores, axis=-1, keepdims=True)
    expo = jnp.exp(scores - top)
    total = jnp.sum(expo, axis=-1, keepdims=True)
    found = product(low(expo), values) / total
    return low(own_lanes(found)), own_lanes(jnp.broadcast_to(top + jnp.log(total), found.shape))


def pair_backward(query, keys, values, extra, logs, back_out):
    query, back_out = both_heads(query * SCALE), both_heads(back_out)
    logs = jnp.concatenate([logs[:, :1], logs[:, HEAD_DIM : HEAD_DIM + 1]])
    shares = jnp.exp(times_transposed(query, keys) + extra - logs)
    back_shares = times_transposed(back_out, values)
    inner = jnp.sum(shares * back_shares, axis=-1, keepdims=True)
    back_scores = low(shares * (back_shares - inner))
    back_query = own_lanes(product(back_scores, keys) * SCALE)
    back_keys = transposed_times(back_scores, query)
    back_values = transposed_times(low(shares), back_out)
    return low(back_query), low(back_keys), low(back_values), back_scores


def question_extra(slot, role_ref, qid, kid):
    shape = (qid.shape[0], kid.shape[1])
    row = lax.broadcasted_iota(jnp.int32, shape, 0) + role_ref[1 + slot]
    column = lax.broadcasted_iota(jnp.int32, shape, 1)
    extra = jnp.where((qid == kid) & (column <= row), 0.0, NEG)
    return jnp.concatenate([extra, extra])


def window_extra(bias_ref, qid, kid):
    same = jnp.where(qid == kid, 0.0, NEG)
    return jnp.concatenate([bias_ref[0] + same, bias_ref[1] + same])


def self_forward_kernel(
    role_ref, q_ref, k_ref, v_ref, bias_ref, qid_ref, kid_ref, o_ref, log_ref
):
    rows = q_ref.shape[1]

    @pl.when(role_ref[0] == 0)
    def question():
        for s in (0, 1):
            extra = question_extra(s, role_ref, qid_ref[s], kid_ref[s])
            o_ref[s], log_ref[s] = attend_pair(q_ref[s], k_ref[s], v_ref[s], extra)

    @pl.when(role_ref[0] != 0)
    def visual():
        for s in (0, 1):
            extra = window_extra(bias_ref, qid_ref[s], kid_ref[s, :, :rows])
            o_ref[s], log_ref[s] = attend_pair(
                q_ref[s], k_ref[s, :rows], v_ref[s, :rows], extra
            )


def self_backward_kernel(
    role_ref,
    q_ref,
    k_ref,
    v_ref,
    bias_ref,
    qid_ref,
    kid_ref,
    log_ref,
    back_ref,
    dq_ref,
    dk_ref,
    dv_ref,
    ds_ref,
):
    rows = q_ref.shape[1]

    @pl.when(role_ref[0] == 0)
    def question():
        ds_ref[...] = jnp.zeros_like(ds_ref)
        for s in (0, 1):
            extra = question_extra(s, role_ref, qid_ref[s], kid_ref[s])
            dq_ref[s], dk_ref[s], dv_ref[s], unused = pair_backward(
                q_ref[s], k_ref[s], v_ref[s], extra, log_ref[s], back_ref[s]
            )

    @pl.when(role_ref[0] != 0)
    def visual():
        dk_ref[...] = jnp.zeros_like(dk_ref)
        dv_ref[...] = jnp.zeros_like(dv_ref)
        for s in (0, 1):
            extra = window_extra(bias_ref, qid_ref[s], kid_ref[s, :, :rows])
            dq_ref[s], found_keys, found_values, kept = pair_backward(
                q_ref[s], k_ref[s, :rows], v_ref[s, :rows], extra, log_ref[s], back_ref[s]
            )
            dk_ref[s, :rows] = found_keys
            dv_ref[s, :rows] = found_values
            ds_ref[0, s] = kept[:rows]
            ds_ref[1, s] = kept[rows:]


def self_specs(rows, span):
    query = pl.BlockSpec((2, rows, LANES), lambda h, role: (0, 0, h))
    keys = pl.BlockSpec((2, span, LANES), lambda h, role: (0, 0, h))
    bias = pl.BlockSpec((2, rows, rows), lambda h, role: (h, 0, 0))
    qid = pl.BlockSpec((2, rows, 1), lambda h, role: (0, 0, 0))
    kid = pl.BlockSpec((2, 1, span), lambda h, role: (0, 0, 0))
    return query, keys, keys, bias, qid, kid


def self_forward(role, query, keys, values, bias, qid, kid):
    rows, span = query.shape[1], keys.shape[1]
    specs = self_specs(rows, span)
    return pl.pallas_call(
        self_forward_kernel,
        out_shape=[
            jax.ShapeDtypeStruct((2, rows, D), jnp.bfloat16),
            jax.ShapeDtypeStruct((2, rows, D), jnp.float32),
        ],
        grid_spec=pltpu.PrefetchScalarGridSpec(
            num_scalar_prefetch=1, grid=(PAIRS,), in_specs=list(specs), out_specs=[specs[0]] * 2
        ),
        compiler_params=pltpu.CompilerParams(vmem_limit_bytes=24 * MIB),
        cost_estimate=pl.CostEstimate(
            flops=16 * rows * span * D, bytes_accessed=12 * span * D, transcendentals=0
        ),
    )(role, query, keys, values, bias, qid, kid)


def self_backward(role, query, keys, values, bias, qid, kid, logs, back_out):
    rows, span = query.shape[1], keys.shape[1]
    specs = self_specs(rows, span)
    return pl.pallas_call(
        self_backward_kernel,
        out_shape=[
            jax.ShapeDtypeStruct((2, rows, D), jnp.bfloat16),
            jax.ShapeDtypeStruct((2, span, D), jnp.bfloat16),
            jax.ShapeDtypeStruct((2, span, D), jnp.bfloat16),
            jax.ShapeDtypeStruct((HEADS, 2, rows, rows), jnp.bfloat16),
        ],
        grid_spec=pltpu.PrefetchScalarGridSpec(
            num_scalar_prefetch=1,
            grid=(PAIRS,),
            in_specs=list(specs) + [specs[0]] * 2,
            out_specs=[
                specs[0],
                specs[1],
                specs[1],
                pl.BlockSpec((2, 2, rows, rows), lambda h, role: (h, 0, 0, 0)),
            ],
        ),
        compiler_params=pltpu.CompilerParams(vmem_limit_bytes=24 * MIB),
        cost_estimate=pl.CostEstimate(
            flops=40 * rows * span * D, bytes_accessed=16 * span * D, transcendentals=0
        ),
    )(role, query, keys, values, bias, qid, kid, logs, back_out)


def cross_forward_kernel(q_ref, k_ref, v_ref, extra_ref, o_ref, log_ref):
    extra = extra_ref[...]
    o_ref[0], log_ref[0] = attend_pair(q_ref[0], k_ref[0], v_ref[0], extra)


def cross_backward_kernel(
    q_ref, k_ref, v_ref, extra_ref, log_ref, back_ref, dq_ref, dk_ref, dv_ref
):
    extra = extra_ref[...]
    dq_ref[0], dk_ref[0], dv_ref[0], unused = pair_backward(
        q_ref[0], k_ref[0], v_ref[0], extra, log_ref[0], back_ref[0]
    )


def cross_specs(rows, span):
    query = pl.BlockSpec((1, rows, LANES), lambda s, h: (s, 0, h))
    keys = pl.BlockSpec((1, span, LANES), lambda s, h: (s, 0, h))
    extra = pl.BlockSpec((1, span), lambda s, h: (0, 0))
    return query, keys, keys, extra


def cross_limit(span):
    return (24 if span <= 2048 else 60) * MIB


def cross_forward(query, keys, values, extra):
    rows, span = query.shape[1], keys.shape[1]
    specs = cross_specs(rows, span)
    return pl.pallas_call(
        cross_forward_kernel,
        out_shape=[
            jax.ShapeDtypeStruct((2, rows, D), jnp.bfloat16),
            jax.ShapeDtypeStruct((2, rows, D), jnp.float32),
        ],
        grid=(2, PAIRS),
        in_specs=list(specs),
        out_specs=[specs[0]] * 2,
        compiler_params=pltpu.CompilerParams(vmem_limit_bytes=cross_limit(span)),
        cost_estimate=pl.CostEstimate(
            flops=32 * rows * span * D, bytes_accessed=8 * span * D, transcendentals=0
        ),
    )(query, keys, values, extra)


def cross_backward(query, keys, values, extra, logs, back_out):
    rows, span = query.shape[1], keys.shape[1]
    specs = cross_specs(rows, span)
    return pl.pallas_call(
        cross_backward_kernel,
        out_shape=[
            jax.ShapeDtypeStruct((2, rows, D), jnp.bfloat16),
            jax.ShapeDtypeStruct((2, span, D), jnp.bfloat16),
            jax.ShapeDtypeStruct((2, span, D), jnp.bfloat16),
        ],
        grid=(2, PAIRS),
        in_specs=list(specs) + [specs[0]] * 2,
        out_specs=[specs[0], specs[1], specs[1]],
        compiler_params=pltpu.CompilerParams(vmem_limit_bytes=cross_limit(span)),
        cost_estimate=pl.CostEstimate(
            flops=80 * rows * span * D, bytes_accessed=16 * span * D, transcendentals=0
        ),
    )(query, keys, values, extra, logs, back_out)


TILES = FF // D
HALF_ROOT = 0.5**0.5
BELL = (0.5 / 3.141592653589793) ** 0.5


def mlp_kernel(places, h_ref, g_ref, up_ref, down_ref, out_ref, back_ref, delta_ref, tile_ref):
    step = pl.program_id(0)
    far, core = step // 2, step % 2
    cut = delta_ref.shape[3]

    for place in range(places):
        for part in range(TILES):
            row = (place * TILES + part) * cut
            tile_ref[row : row + cut] = down_ref[part, place * cut : (place + 1) * cut]
    rows, branch, up, down = h_ref[...], g_ref[...], up_ref[0], tile_ref[...]
    upward = product(rows, up)
    lift = times_transposed(branch, down)
    chance = 0.5 * (1.0 + lax.erf(upward * HALF_ROOT))
    active = low(upward * chance)
    slope = chance + upward * jnp.exp(-0.5 * upward * upward) * BELL
    back_up = low(slope * lift)
    out, back = product(active, down), times_transposed(back_up, up)

    @pl.when(step == 0)
    def start():
        out_ref[...] = out
        back_ref[...] = back

    @pl.when(step > 0)
    def add():
        out_ref[...] += out
        back_ref[...] += back

    delta_up = low(transposed_times(rows, back_up))
    for side in range(2):
        for place in range(2 * places):
            row = (side * 2 * places + place) * cut
            delta_ref[place, step, side] = delta_up[row : row + cut]
    delta_down = low(transposed_times(active, branch))
    for place in range(places):
        for part in range(TILES):
            row = (place * TILES + part) * cut
            delta_ref[core * places + place, TILES + part, far] = delta_down[row : row + cut]


def mlp(rows, branch, weights, blocks):
    count = rows.shape[0]
    cut = D // (4 * blocks)
    resident = pl.BlockSpec((count, D), lambda i: (0, 0))
    shape = (2 * blocks, 2 * TILES, 2, cut, D)
    return pl.pallas_call(
        functools.partial(mlp_kernel, blocks),
        out_shape=[
            jax.ShapeDtypeStruct((count, D), jnp.float32),
            jax.ShapeDtypeStruct((count, D), jnp.float32),
            jax.ShapeDtypeStruct(shape, jnp.bfloat16),
        ],
        grid=(TILES,),
        in_specs=[
            resident,
            resident,
            pl.BlockSpec((1, D, D), lambda i: (4 + i, 0, 0)),
            pl.BlockSpec((TILES, D // TILES, D), lambda i: (2, i, 0)),
        ],
        out_specs=[resident, resident, pl.BlockSpec(shape, lambda i: (0, 0, 0, 0, 0))],
        scratch_shapes=[pltpu.VMEM((D, D), jnp.bfloat16)],
        compiler_params=pltpu.CompilerParams(vmem_limit_bytes=48 * MIB),
        cost_estimate=pl.CostEstimate(
            flops=12 * count * D * FF, bytes_accessed=8 * D * FF, transcendentals=0
        ),
    )(rows, branch, weights, weights)


def weight_kernel(places, *refs):
    delta_ref = refs[-1]
    cut = delta_ref.shape[3]
    for number in range(len(refs) // 2):
        delta = low(transposed_times(refs[2 * number][...], refs[2 * number + 1][...]))
        for place in range(places):
            delta_ref[place, number, 0] = delta[place * cut : (place + 1) * cut]


def weight_gradients(pairs, blocks):
    cut = D // (4 * blocks)
    total = sum(rows.shape[0] for rows, unused in pairs)
    if total > 8 * D:
        parts = [low(transposed_times(rows, back)) for rows, back in pairs]
        parts = jnp.stack([part.reshape(2, 2 * blocks, cut, D) for part in parts])
        return parts.transpose(2, 0, 1, 3, 4)
    specs, arrays = [], []
    for rows, back in pairs:
        specs.append(pl.BlockSpec((rows.shape[0], D // 2), lambda i: (0, i)))
        specs.append(pl.BlockSpec(back.shape, lambda i: (0, 0)))
        arrays += [rows, back]
    return pl.pallas_call(
        functools.partial(weight_kernel, 2 * blocks),
        out_shape=jax.ShapeDtypeStruct((2 * blocks, len(pairs), 2, cut, D), jnp.bfloat16),
        grid=(2,),
        in_specs=specs,
        out_specs=pl.BlockSpec(
            (2 * blocks, len(pairs), 1, cut, D), lambda i: (0, 0, i, 0, 0)
        ),
        compiler_params=pltpu.CompilerParams(vmem_limit_bytes=32 * MIB),
        cost_estimate=pl.CostEstimate(
            flops=2 * total * D * D, bytes_accessed=4 * total * D, transcendentals=0
        ),
    )(*arrays)


def body(
    visual_in,
    question_in,
    segment_ids,
    regions,
    rel_index,
    rel_table,
    window_project,
    window_output,
    causal_project,
    causal_output,
    reader_query,
    reader_pair,
    reader_output,
    viewer_query,
    viewer_pair,
    viewer_output,
    visual_up,
    visual_down,
    question_up,
    question_down,
    norm_gains,
    norm_shifts,
    visual_cot,
    question_cot,
):
    blocks = lax.axis_size("blk")
    ringed = blocks == 8
    share = Q_LEN // blocks
    rows = visual_in.shape[0]
    far, core, blk = lax.axis_index("far"), lax.axis_index("core"), lax.axis_index("blk")
    asks = far == 0
    seat = ring_seat(blk, blocks)
    early = -(-(LONGEST - 1) // share)
    reach = min(Q_LEN, share * (early + 1))
    span = reach + rows - share
    turns = (seat, blocks - 1 - seat)
    firsts = [jnp.clip((turn - early) * share, 0, Q_LEN - reach) for turn in turns]
    insets = [jnp.where(far == 0, turn * share - at, 0) for turn, at in zip(turns, firsts)]
    turn = jnp.where(far == 0, turns[0], turns[1])
    first = jnp.where(far == 0, firsts[0], firsts[1])
    role = jnp.stack([far] + insets).astype(jnp.int32)
    cut = D // (4 * blocks)

    def own_of(question_side, visual_side):
        return jnp.where(asks, question_side, visual_side)

    class Trade(Once):
        def __init__(self, question_side, visual_side):
            self.kept = own_of(question_side, visual_side)
            self.away = own_of(visual_side, question_side)

        def begin(self):
            self.coming = swap_far(self.away)

        def send(self):
            return self.coming if hasattr(self, "coming") else swap_far(self.away)

        def receive(self, got):
            self.found = jnp.stack([own_of(self.kept, got), own_of(got, self.kept)])

    def pad_rows(values, total):
        return jnp.pad(values, ((0, total - values.shape[0]),) + ((0, 0),) * (values.ndim - 1))

    def block_of(flat, columns):
        return flat.reshape(-1, columns)

    def cross_squares(query, pair, out):
        pair = pair.reshape(cut, 2, D).transpose(1, 0, 2)
        return jnp.concatenate([query.reshape(1, cut, D), pair, out.reshape(1, cut, D)])

    def mlp_squares(up, down):
        up = up.reshape(cut, TILES, D).transpose(1, 0, 2)
        return jnp.concatenate([up, down.reshape(TILES, cut, D)])

    def matrices(ring, splits):
        if ringed:
            other = {key: swap_core(item) for key, item in ring.pieces.items()}
            return assemble(ring.pieces, other, splits, core, seat, blocks)
        here = lax.all_gather(ring, "blk", axis=0)
        there = swap_core(here)
        pair = jnp.where(core == 0, jnp.stack([here, there]), jnp.stack([there, here]))
        whole = pair.transpose(2, 0, 1, 3, 4).reshape(4 * blocks * ring.shape[1], -1)
        places = [sum(splits[:i]) for i in range(len(splits))]
        return [whole[:, at : at + width] for at, width in zip(places, splits)]

    def ring_of(own):
        return Gather(own) if ringed else own

    def step(rings, transfers=(), work=()):
        return phase((list(rings) if ringed else []) + list(transfers), work)

    norms = jnp.pad(jnp.concatenate([norm_gains, norm_shifts]), (0, cut * LANES - 2 * norm_gains.size))
    norms = norms.reshape(cut, LANES)
    self_shards = Trade(
        jnp.concatenate([block_of(causal_project, 3 * D), block_of(causal_output, D), norms], 1),
        jnp.concatenate([block_of(window_project, 3 * D), block_of(window_output, D), norms], 1),
    )
    cross_shards = Trade(
        cross_squares(reader_query, reader_pair, reader_output),
        cross_squares(viewer_query, viewer_pair, viewer_output),
    )
    cross_shards.kept, cross_shards.away = phase([self_shards], (cross_shards.kept, cross_shards.away))
    self_ring = ring_of(self_shards.found)
    mlp_shards = Trade(mlp_squares(question_up, question_down), mlp_squares(visual_up, visual_down))
    mlp_shards.kept, mlp_shards.away = step(
        [self_ring], [cross_shards], (mlp_shards.kept, mlp_shards.away)
    )
    row_shards = Trade(
        pad_rows(lax.dynamic_slice_in_dim(question_in, first, reach, 0), span),
        pad_rows(visual_in, span),
    )
    marks = Trade(segment_ids[0], jnp.pad(regions, (0, Q_LEN - rows)))
    cot = Trade(
        pad_rows(lax.dynamic_slice_in_dim(question_cot, turn * share, share, 0), rows), visual_cot
    )
    row_shards.away, later = step([self_ring], [mlp_shards], (row_shards.away, cross_shards.found))
    row_shards.begin()
    later = jnp.concatenate([later, mlp_shards.found], 1)
    later = later.transpose(1, 0, 2, 3).reshape(-1, cut, D)
    later = lax.all_gather(later, ("core", "blk"), axis=1, tiled=True).reshape(-1, D, D)
    row_shards.away = step([self_ring], [marks], row_shards.away)
    bias = window_bias(role, rel_table, rel_index, 0, 1)
    bias = step([self_ring], [row_shards], bias)[:, :HEADS].transpose(1, 0, 2)
    slots, marks = row_shards.found, marks.found

    def of_slots(values, starts, size):
        return jnp.stack(
            [lax.dynamic_slice_in_dim(values[i], start, size, 0) for i, start in enumerate(starts)]
        )

    key_marks = own_of(
        jnp.pad(
            of_slots(marks, firsts, reach), ((0, 0), (0, span - reach)), constant_values=-2
        ),
        marks[:, :span],
    )[:, None, :]
    row_marks = own_of(
        jnp.pad(
            of_slots(marks, [turn * share for turn in turns], share),
            ((0, 0), (0, rows - share)),
            constant_values=-1,
        ),
        marks[:, :rows],
    )[:, :, None]
    self_weights = matrices(self_ring, (D, D, D, D, LANES))
    self_query_weight, self_key_weight, self_value_weight, self_exit, norm_rows = self_weights
    norm_flat = norm_rows.reshape(4 * blocks, -1)[:, : 2 * norm_gains.size].astype(jnp.float32)
    gains = norm_flat[:, : norm_gains.size].reshape(6, D)
    shifts = norm_flat[:, norm_gains.size :].reshape(6, D)

    own = of_slots(slots, insets, rows).astype(jnp.float32)
    self_gain, self_shift = own_of(gains[1], gains[0]), own_of(shifts[1], shifts[0])
    self_norm, self_pull = jax.vjp(normalize, own, self_gain, self_shift)
    self_low = low(self_norm).reshape(2 * rows, D)
    every_low = low(normalize(slots.astype(jnp.float32), self_gain, self_shift))
    every_low = every_low.reshape(2 * span, D)
    self_query = low(product(self_low, self_query_weight)).reshape(2, rows, D)
    self_keys = low(product(every_low, self_key_weight)).reshape(2, span, D)
    self_values = low(product(every_low, self_value_weight)).reshape(2, span, D)
    self_attn, self_logs = self_forward(
        role, self_query, self_keys, self_values, bias, row_marks, key_marks
    )
    self_attn = self_attn.reshape(2 * rows, D)
    rows_one = own + product(self_attn, self_exit).reshape(2, rows, D)

    cross_gain, cross_shift = own_of(gains[2], gains[3]), own_of(shifts[2], shifts[3])
    cross_norm, cross_pull = jax.vjp(normalize, rows_one, cross_gain, cross_shift)
    cross_low = low(cross_norm)
    sent = Once(lambda: swap_far(cross_low))
    phase([sent])
    cross_weights = lax.optimization_barrier([later[i] for i in range(4)])
    cross_query_weight, cross_key_weight, cross_value_weight, cross_exit = cross_weights
    cross_query = low(product(cross_low.reshape(2 * rows, D), cross_query_weight))
    cross_query = cross_query.reshape(2, rows, D)
    source_ring = ring_of(sent.found)
    if ringed:
        for number in range(4):
            phase([source_ring] + ([cot] if number == 0 else []))
        pieces = [source_ring.pieces[k] for k in OFFSETS[:-1]]
        pieces.append(jnp.concatenate([source_ring.pieces["first"], source_ring.pieces["second"]]))
        sources = jnp.concatenate(pieces, axis=1)
    else:
        phase([cot])
        sources = lax.all_gather(sent.found, "blk", axis=1, tiled=True)
    sources = sources.reshape(-1, D)
    cot = cot.found
    column = jnp.arange(blocks * rows) % rows
    cross_extra = own_of(0.0, jnp.where(column < share, 0.0, NEG))[None]
    cross_keys = low(product(sources, cross_key_weight)).reshape(2, -1, D)
    cross_values = low(product(sources, cross_value_weight)).reshape(2, -1, D)
    cross_attn, cross_logs = cross_forward(cross_query, cross_keys, cross_values, cross_extra)
    cross_attn = cross_attn.reshape(2 * rows, D)
    rows_two = rows_one + product(cross_attn, cross_exit).reshape(2, rows, D)

    mlp_gain, mlp_shift = own_of(gains[5], gains[4]), own_of(shifts[5], shifts[4])
    mlp_norm, mlp_pull = jax.vjp(normalize, rows_two, mlp_gain, mlp_shift)
    mlp_low = low(mlp_norm).reshape(2 * rows, D)
    mlp_out, back_mlp, mlp_delta = mlp(mlp_low, cot.reshape(2 * rows, D), later, blocks)
    rows_three = rows_two + mlp_out.reshape(2, rows, D)
    back_mlp_in, gain_mlp, shift_mlp = mlp_pull(back_mlp.reshape(2, rows, D))
    back_two = cot.astype(jnp.float32) + back_mlp_in
    mlp_delta = mlp_delta.reshape(2, blocks, -1, D)

    class Shares:
        def __init__(self, delta):
            self.delta = delta
            self.swap = Once(
                lambda: swap_core(lax.dynamic_index_in_dim(delta, 1 - core, 0, keepdims=False))
            )

        def start(self):
            if ringed:
                self.ring = Sum(self.chunk)
            else:
                kept = lax.dynamic_index_in_dim(self.delta, core, 0, keepdims=False)
                kept = kept.astype(jnp.float32) + self.swap.found.astype(jnp.float32)
                self.sum = lax.psum_scatter(kept, "blk", scatter_dimension=0, tiled=True)[0]

        def chunk(self, k):
            place = ring_place(seat + k, blocks)
            mine = lax.dynamic_slice(self.delta, (core, place, 0, 0), (1, 1) + self.delta.shape[2:])
            theirs = lax.dynamic_index_in_dim(self.swap.found, place, 0, keepdims=False)
            mine = mine.reshape(theirs.shape)
            return mine.astype(jnp.float32) + theirs.astype(jnp.float32)

        def rings(self):
            return [self.ring] if ringed else []

        def total(self):
            found = self.ring.total if ringed else self.sum
            return found.reshape(-1, 2, cut, D).transpose(1, 0, 2, 3)

    mlp_shares = Shares(mlp_delta)
    class Owners(Once):
        def __init__(self, total):
            self.total = total

        def send(self):
            return swap_far(low(own_of(self.total[1], self.total[0])))

        def receive(self, came):
            mine = own_of(self.total[0], self.total[1]).astype(jnp.float32)
            came = came.astype(jnp.float32)
            self.found = own_of(mine, came), own_of(came, mine)

    class Home(Once):
        def __init__(self, values):
            self.values = values

        def send(self):
            return swap_far(own_of(self.values[1], self.values[0]))

        def receive(self, got):
            kept = own_of(self.values[0], self.values[1])
            self.found = own_of(kept, got)[:share], own_of(got, kept)

    home_out = Home(low(rows_three))

    cross_branch = low(back_two).reshape(2 * rows, D)
    back_attn = low(times_transposed(cross_branch, cross_exit)).reshape(2, rows, D)
    back_attn = phase([mlp_shares.swap], back_attn)
    mlp_shares.start()
    back_query, back_keys, back_values = phase(
        mlp_shares.rings(),
        cross_backward(cross_query, cross_keys, cross_values, cross_extra, cross_logs, back_attn),
    )
    back_query = back_query.reshape(2 * rows, D)
    back_keys, back_values = back_keys.reshape(-1, D), back_values.reshape(-1, D)
    back_sources = times_transposed(back_keys, cross_key_weight)
    back_sources = back_sources + times_transposed(back_values, cross_value_weight)
    back_sources = phase(mlp_shares.rings(), back_sources.reshape(2, -1, D))

    def owned(delta):
        delta = delta.reshape(2 * blocks, -1, D)
        return lax.psum_scatter(delta, ("core", "blk"), scatter_dimension=0, tiled=True)

    cross_pairs = [
        (cross_low.reshape(2 * rows, D), back_query),
        (sources, back_keys),
        (sources, back_values),
        (cross_attn, cross_branch),
    ]
    if ringed:

        def source_chunk(k):
            at = OFFSETS.index(k) * rows
            return back_sources[:, at : at + rows].reshape(2 * rows, D)

        back_sent = Sum(source_chunk)
        cross_delta = weight_gradients(cross_pairs, blocks)
        back_cross = times_transposed(back_query, cross_query_weight).reshape(2, rows, D)
        ready = mlp_shares.ring
        works = [back_cross, cross_delta, ready.state, ()]
        extra = [[home_out], [], [], []]
        works = [phase([back_sent] + more, work) for work, more in zip(works, extra)]
        back_cross, cross_delta, ready.state = works[:3]
        cross_delta = owned(cross_delta)
        back_sent = back_sent.total.reshape(2, rows, D)
    else:
        back_sent = lax.psum_scatter(back_sources, "blk", scatter_dimension=1, tiled=True)
        phase([home_out])
        cross_delta = owned(weight_gradients(cross_pairs, blocks))
        back_cross = times_transposed(back_query, cross_query_weight).reshape(2, rows, D)
    returned = Once(lambda: swap_far(low(back_sent)))
    phase([returned] + mlp_shares.rings())
    back_cross = back_cross + returned.found.astype(jnp.float32)
    back_cross_in, gain_cross, shift_cross = cross_pull(back_cross)
    back_one = back_two + back_cross_in

    self_branch = low(back_one).reshape(2 * rows, D)
    back_attn = low(times_transposed(self_branch, self_exit)).reshape(2, rows, D)
    back_query, back_keys, back_values, back_scores = phase(
        mlp_shares.rings(),
        self_backward(
            role,
            self_query,
            self_keys,
            self_values,
            bias,
            row_marks,
            key_marks,
            self_logs,
            back_attn,
        ),
    )
    back_query = back_query.reshape(2 * rows, D)
    back_keys, back_values = back_keys.reshape(2 * span, D), back_values.reshape(2 * span, D)
    back_every = times_transposed(back_keys, self_key_weight)
    back_every = back_every + times_transposed(back_values, self_value_weight)
    back_every = back_every.reshape(2, span, D)
    back_self = times_transposed(back_query, self_query_weight).reshape(2, rows, D)

    def for_earlier(j):
        parts = []
        for slot in (0, 1):
            at = jnp.maximum(insets[slot] - j * share, 0)
            found = lax.dynamic_slice_in_dim(back_every[slot], at, share, 0)
            parts.append(jnp.where(asks & (turns[slot] >= j), found, 0.0))
        return parts

    class Chain(Ring):
        def __init__(self):
            self.left = early
            self.set(for_earlier(early))

        def set(self, total):
            self.total = total
            self.state = low(total[1]), low(total[0])

        def receive(self, found):
            self.left -= 1
            own = for_earlier(self.left)
            self.set([found[1].astype(jnp.float32) + own[0], found[0].astype(jnp.float32) + own[1]])

    chain = Chain()
    chain.state, back_query, back_keys, back_values = lax.optimization_barrier(
        (chain.state, back_query, back_keys, back_values)
    )
    self_pairs = [
        (self_low, back_query),
        (every_low, back_keys),
        (every_low, back_values),
        (self_attn, self_branch),
    ]
    self_delta = weight_gradients(self_pairs, blocks).reshape(2, blocks, 8 * cut, D)
    question_rows, visual_out = home_out.found
    outs = [Gather(question_rows)] if ringed else []
    score_rows = back_scores.reshape(2 * HEADS, WIN, WIN).transpose(1, 0, 2)
    table_parts = [table_sums(role, score_rows, rel_index, part, 4) for part in range(4)]
    self_delta, table_parts[0] = phase([chain] + outs, (self_delta, table_parts[0]))
    self_shares = Shares(self_delta)
    table_parts[1], cross_delta = phase(
        [chain, self_shares.swap] + outs, (table_parts[1], cross_delta)
    )
    self_shares.start()
    sums = self_shares.rings()
    for number in range(early - 2):
        work = table_parts[2 + number] if number < 2 else ()
        work = phase([chain] + (outs + sums if number < 2 else []), work)
        if number < 2:
            table_parts[2 + number] = work
    table_part = sum(table_parts).reshape(HEADS, 2, RELS_PAD)
    table_part = jnp.sum(table_part, axis=1)[:, :RELS]
    back_self = back_self + own_of(
        jnp.pad(jnp.stack(chain.total), ((0, 0), (0, rows - share), (0, 0))), back_every[:, :rows]
    )
    back_self_in, gain_self, shift_self = self_pull(back_self)
    back_in = back_one + back_self_in

    blank = jnp.zeros((D,), jnp.float32)
    gain_delta = [
        own_of(blank, gain_self),
        own_of(gain_self, blank),
        own_of(gain_cross, blank),
        own_of(blank, gain_cross),
        own_of(blank, gain_mlp),
        own_of(gain_mlp, blank),
    ]
    shift_delta = [
        own_of(blank, shift_self),
        own_of(shift_self, blank),
        own_of(shift_cross, blank),
        own_of(blank, shift_cross),
        own_of(blank, shift_mlp),
        own_of(shift_mlp, blank),
    ]
    small = jnp.concatenate(gain_delta + shift_delta + [table_part.reshape(-1)])
    size = small.size
    small = jnp.pad(small, (0, LANES * LANES - size)).reshape(LANES, LANES)

    class Everywhere:
        def __init__(self, total):
            self.total, self.bit = total, 0
            self.bits = [("far", 1, 2)]
            self.bits += [("blk", 1 << i, blocks) for i in range(blocks.bit_length() - 1)]
            self.bits += [("core", 1, 2)]

        def send(self):
            axis, bit, count = self.bits[self.bit]
            return lax.ppermute(self.total, axis, [(i, i ^ bit) for i in range(count)])

        def receive(self, found):
            self.total, self.bit = self.total + found, self.bit + 1

    small = Everywhere(small)
    home_back = Home(low(back_in))
    mlp_sums = Owners(mlp_shares.total())
    phase([home_back, mlp_sums, small] + sums)
    cross_sums = Owners(cross_delta.reshape(4, 2, cut, D).transpose(1, 0, 2, 3))
    question_back, visual_back = home_back.found
    if ringed:
        back_ring = Gather(question_back)
        phase([back_ring, small] + sums)
    self_sums = Owners(self_shares.total())
    if ringed:
        for number in range(3):
            phase([back_ring, small] + [[], [cross_sums], [self_sums]][number])
        question_delta = seats_in_order(back_ring, far, seat, blocks, jnp.float32)
        question_out = seats_in_order(outs[0], far, seat, blocks, jnp.bfloat16)
    else:
        both = jnp.stack([question_rows, question_back])
        both = lax.all_gather(both, "blk", axis=0)
        order = ring_order(blocks)
        both = own_of(
            jnp.concatenate([both[i] for i in order], 1),
            jnp.concatenate([both[i] for i in order[::-1]], 1),
        )
        question_out, question_delta = both[0], both[1].astype(jnp.float32)
        phase([cross_sums, self_sums])
    while small.bit < len(small.bits):
        phase([small])
    small = small.total.reshape(-1)
    at = ((2 * far + core) * blocks + blk) * norm_gains.size
    delta_gains = lax.dynamic_slice_in_dim(small, at, norm_gains.size, 0)
    delta_shifts = lax.dynamic_slice_in_dim(small, 6 * D + at, norm_gains.size, 0)
    table_delta = small[12 * D : size].reshape(HEADS, RELS)
    question_shift = small[11 * D : 12 * D]

    def joined(side, start, stop):
        return side[start:stop].transpose(1, 0, 2).reshape(-1)

    causal, window = [[joined(side, 0, 3), joined(side, 3, 4)] for side in self_sums.found]
    reader, viewer = [
        [joined(side, 0, 1), joined(side, 1, 3), joined(side, 3, 4)] for side in cross_sums.found
    ]
    question_mlp, visual_mlp = [
        [joined(side, 0, TILES), side[TILES:].reshape(-1)] for side in mlp_sums.found
    ]
    return (
        visual_out,
        question_out,
        visual_back.astype(jnp.float32),
        question_delta,
        table_delta,
        window[0],
        window[1],
        causal[0],
        causal[1],
        reader[0],
        reader[1],
        reader[2],
        viewer[0],
        viewer[1],
        viewer[2],
        visual_mlp[0],
        visual_mlp[1],
        question_mlp[0],
        question_mlp[1],
        delta_gains,
        delta_shifts,
        question_shift,
    )


def solution(mesh):
    pages, blocks = mesh.devices.shape
    cut = jax.sharding.Mesh(
        mesh.devices.reshape(2, pages // 2, blocks), ("far", "core", "blk")
    )
    flat, whole, by_page = P(("far", "core", "blk")), P(), P(("far", "core"), None)
    split = P(("far", "core", "blk"), None)
    in_specs = (split, by_page, by_page, flat, whole, whole) + (flat,) * 16 + (split, by_page)
    out_specs = (split, by_page, split, by_page, whole) + (flat,) * 16 + (whole,)
    return jax.shard_map(body, mesh=cut, in_specs=in_specs, out_specs=out_specs, check_vma=False)
```

```python
import functools

import jax
import jax.numpy as jnp
from jax import lax
from jax.experimental import pallas as pl
from jax.experimental.pallas import tpu as pltpu
from jax.sharding import PartitionSpec as P

D = 768
HEADS = 12
HEAD_DIM = 64
FF = 3072
Q_LEN = 1024
WIN = 144
RELS = 529
LONGEST = Q_LEN // 2
LANES = 128
PAIRS = D // LANES
RELS_PAD = 544

EPS = 1e-05
NEG = -1000000000.0
SCALE = HEAD_DIM ** (-0.5)
MIB = 1 << 20


def product(left, right):
    return jnp.dot(left, right, preferred_element_type=jnp.float32)


def times_transposed(left, right):
    return lax.dot_general(
        left, right, (((1,), (1,)), ((), ())), preferred_element_type=jnp.float32
    )


def transposed_times(left, right):
    return lax.dot_general(
        left, right, (((0,), (0,)), ((), ())), preferred_element_type=jnp.float32
    )


def low(values):
    return values.astype(jnp.bfloat16)


def normalize(rows, gain, shift):
    mean = jnp.mean(rows, axis=-1, keepdims=True)
    centred = rows - mean
    spread = jnp.mean(centred * centred, axis=-1, keepdims=True)
    return centred * lax.rsqrt(spread + EPS) * gain + shift


def smooth(values):
    return jax.nn.gelu(values, approximate=False)


def ring_order(blocks):
    return tuple(range(0, blocks, 2)) + tuple(range(blocks - 1, 0, -2))


def ring_seat(blk, blocks):
    return jnp.where(blk % 2 == 0, blk // 2, blocks - 1 - blk // 2)


def ring_place(seat, blocks):
    seat = lax.rem(seat + 2 * blocks, blocks)
    return jnp.where(seat < blocks // 2, 2 * seat, 2 * (blocks - 1 - seat) + 1)


def forward_hop(blocks):
    order = ring_order(blocks)
    return [(order[i], order[(i + 1) % blocks]) for i in range(blocks)]


def backward_hop(blocks):
    return [(there, here) for here, there in forward_hop(blocks)]


def swap_far(values):
    return lax.ppermute(values, "far", [(0, 1), (1, 0)])


def swap_core(values):
    return lax.ppermute(values, "core", [(0, 1), (1, 0)])


OFFSETS = (0, -1, 1, -2, 2, -3, 3, 4)


class Ring:
    state = None
    within = None


class Gather(Ring):
    def __init__(self, own):
        self.half = own.shape[0] // 2
        self.pieces, self.step, self.state = {0: own}, 0, (own, own)
        self.places = {0: (own, 0)}

    def receive(self, found):
        self.step += 1
        if self.step == 4:
            self.pieces["first"], self.pieces["second"] = found
            self.places["first"], self.places["second"] = self.within
        else:
            self.pieces[-self.step], self.pieces[self.step] = found
            self.places[-self.step], self.places[self.step] = self.within
            one, two = found
            self.state = (one[: self.half], two[self.half :]) if self.step == 3 else found


class Sum(Ring):
    def __init__(self, chunk):
        self.chunk, self.step = chunk, 0
        most = chunk(4)
        half = most.shape[0] // 2
        self.state = low(most[:half]), low(most[half:])

    def receive(self, found):
        one, two = [item.astype(jnp.float32) for item in found]
        if self.step == 0:
            blank = jnp.zeros(one.shape, jnp.float32)
            one, two = jnp.concatenate([one, blank]), jnp.concatenate([blank, two])
        self.step += 1
        left = 4 - self.step
        if left == 0:
            self.total = self.chunk(0) + one + two
        else:
            self.state = low(self.chunk(left) + one), low(self.chunk(-left) + two)


class Once:
    def __init__(self, send):
        self.send = send

    def receive(self, found):
        self.found = found


def phase(transfers, work=()):
    rings = [item for item in transfers if isinstance(item, Ring)]
    others = [item for item in transfers if not isinstance(item, Ring)]
    states = lax.optimization_barrier([item.state for item in rings])
    both = []
    if rings:
        blocks = lax.axis_size("blk")
        for side, hop in ((0, forward_hop(blocks)), (1, backward_hop(blocks))):
            parts = [state[side] for state in states]
            both.append(
                lax.ppermute(parts[0] if len(parts) == 1 else jnp.concatenate(parts), "blk", hop)
            )
    found = [item.send() for item in others]
    both, found, work = lax.optimization_barrier((both, found, work))
    for item, one in zip(others, found):
        item.receive(one)
    starts = [0, 0]
    for item, state in zip(rings, states):
        pieces = []
        item.within = [(both[side], starts[side]) for side in (0, 1)]
        for side in (0, 1):
            size = state[side].shape[0]
            pieces.append(both[side][starts[side] : starts[side] + size])
            starts[side] += size
        item.receive(tuple(pieces) if len(rings) > 1 else tuple(both))
    return work


def whole_block(array):
    blank = (0,) * len(array.shape)
    return pl.BlockSpec(array.shape, lambda i, where: blank)


def assemble_kernel(plan, count, where_ref, *refs):
    pieces, outs = refs[:count], refs[count:]
    for piece, (index, first, core) in zip(pieces, plan):
        start = 0
        for out in outs:
            width = out.shape[-1]
            for number in range(piece.shape[0]):
                target = (first + number, where_ref[core], where_ref[index])
                out[target] = piece[number, :, start : start + width]
            start += width


def assemble(own, other, splits, core, seat, blocks):
    rows = own[0].shape[1]
    places = [ring_place(seat + k, blocks) for k in OFFSETS]
    where = jnp.stack([core, 1 - core] + places).astype(jnp.int32)
    pieces, plan = [], []
    for side, group in ((0, own), (1, other)):
        for number, offset in enumerate(OFFSETS):
            if offset == 4:
                pieces += [group["first"], group["second"]]
                plan += [(2 + number, 0, side), (2 + number, 1, side)]
            else:
                pieces.append(group[offset])
                plan.append((2 + number, 0, side))
    outs = [jax.ShapeDtypeStruct((2, 2, blocks, rows, width), jnp.bfloat16) for width in splits]
    found = pl.pallas_call(
        functools.partial(assemble_kernel, plan, len(pieces)),
        out_shape=outs,
        grid_spec=pltpu.PrefetchScalarGridSpec(
            num_scalar_prefetch=1,
            grid=(1,),
            in_specs=[whole_block(item) for item in pieces],
            out_specs=[whole_block(item) for item in outs],
        ),
        compiler_params=pltpu.CompilerParams(vmem_limit_bytes=32 * MIB),
        cost_estimate=pl.CostEstimate(
            flops=0, bytes_accessed=16 * blocks * rows * sum(splits), transcendentals=0
        ),
    )(where, *pieces)
    return [item.reshape(4 * blocks * rows, -1) for item in found]


def place_kernel(plan, where_ref, *refs):
    pieces, out = refs[:-1], refs[-1]
    for piece, (index, start, first, last) in zip(pieces, plan):
        found = piece[start : start + last - first]
        out[where_ref[index], first:last] = found.astype(out.dtype)


def seats_in_order(ring, far, seat, blocks, dtype):
    rows, columns = ring.pieces[0].shape
    found = [(k, ring.places[k], 0, rows) for k in OFFSETS[:-1]]
    found += [(4, ring.places["first"], 0, rows // 2), (4, ring.places["second"], rows // 2, rows)]
    where = [lax.rem(seat + item[0] + blocks, blocks) for item in found]
    where = [jnp.where(far == 0, item, blocks - 1 - item) for item in where]
    where = jnp.stack(where).astype(jnp.int32)
    pieces = [item[1][0] for item in found]
    plan = [(i, item[1][1], item[2], item[3]) for i, item in enumerate(found)]
    out = jax.ShapeDtypeStruct((blocks, rows, columns), dtype)
    placed = pl.pallas_call(
        functools.partial(place_kernel, plan),
        out_shape=out,
        grid_spec=pltpu.PrefetchScalarGridSpec(
            num_scalar_prefetch=1,
            grid=(1,),
            in_specs=[whole_block(item) for item in pieces],
            out_specs=whole_block(out),
        ),
        compiler_params=pltpu.CompilerParams(vmem_limit_bytes=24 * MIB),
        cost_estimate=pl.CostEstimate(
            flops=0, bytes_accessed=6 * blocks * rows * columns, transcendentals=0
        ),
    )(where, *pieces)
    return placed.reshape(blocks * rows, columns)


def bias_kernel(part, role_ref, table_ref, index_ref, out_ref):
    count = out_ref.shape[0]

    def one(i, carry):
        row = index_ref[pl.ds(part * count + i, 1), :]
        marks = lax.broadcasted_iota(jnp.int32, (RELS_PAD, WIN), 0) == row
        hot = low(jnp.where(marks, 1.0, 0.0))
        both = jnp.dot(table_ref[...], hot, preferred_element_type=jnp.float32)
        out_ref[i] = both[:16] + both[16:]
        return carry

    @pl.when(role_ref[0] != 0)
    def visual():
        lax.fori_loop(0, count, one, 0, unroll=4)


def window_bias(role, rel_table, rel_index, part, parts):
    table = jnp.pad(rel_table, ((0, 16 - HEADS), (0, RELS_PAD - RELS)))
    coarse = lax.reduce_precision(table, 8, 7)
    both = low(jnp.concatenate([coarse, table - coarse]))
    return pl.pallas_call(
        functools.partial(bias_kernel, part),
        out_shape=jax.ShapeDtypeStruct((WIN // parts, 16, WIN), jnp.float32),
        in_specs=[pl.BlockSpec(memory_space=pltpu.SMEM)] + [pl.BlockSpec()] * 2,
        cost_estimate=pl.CostEstimate(
            flops=64 * RELS_PAD * WIN * WIN // parts,
            bytes_accessed=4 * 17 * WIN * WIN // parts,
            transcendentals=0,
        ),
    )(role, both, rel_index)


def table_kernel(part, role_ref, scores_ref, index_ref, out_ref):
    count = scores_ref.shape[0]

    def one(i, total):
        row = index_ref[pl.ds(part * count + i, 1), :]
        marks = lax.broadcasted_iota(jnp.int32, (RELS_PAD, WIN), 0) == row
        hot = low(jnp.where(marks, 1.0, 0.0))
        return total + times_transposed(scores_ref[i], hot)

    blank = jnp.zeros((2 * HEADS, RELS_PAD), jnp.float32)

    @pl.when(role_ref[0] != 0)
    def visual():
        out_ref[...] = lax.fori_loop(0, count, one, blank, unroll=4)

    @pl.when(role_ref[0] == 0)
    def question():
        out_ref[...] = blank


def table_sums(role, rows, rel_index, part, parts):
    count = WIN // parts
    return pl.pallas_call(
        functools.partial(table_kernel, part),
        out_shape=jax.ShapeDtypeStruct((2 * HEADS, RELS_PAD), jnp.float32),
        grid=(1,),
        in_specs=[
            pl.BlockSpec(memory_space=pltpu.SMEM),
            pl.BlockSpec((count, 2 * HEADS, WIN), lambda i: (part, 0, 0)),
            pl.BlockSpec((WIN, WIN), lambda i: (0, 0)),
        ],
        out_specs=pl.BlockSpec((2 * HEADS, RELS_PAD), lambda i: (0, 0)),
        cost_estimate=pl.CostEstimate(
            flops=48 * RELS_PAD * WIN * count, bytes_accessed=52 * WIN * count, transcendentals=0
        ),
    )(role, rows, rel_index)


def both_heads(rows):
    first = lax.broadcasted_iota(jnp.int32, (1, LANES), 1) < HEAD_DIM
    blank = jnp.zeros_like(rows)
    return jnp.concatenate([jnp.where(first, rows, blank), jnp.where(first, blank, rows)])


def own_lanes(stacked):
    rows = stacked.shape[0] // 2
    first = lax.broadcasted_iota(jnp.int32, (1, LANES), 1) < HEAD_DIM
    return jnp.where(first, stacked[:rows], stacked[rows:])


def attend_pair(query, keys, values, extra):
    scores = times_transposed(both_heads(query * SCALE), keys) + extra
    top = jnp.max(scores, axis=-1, keepdims=True)
    expo = jnp.exp(scores - top)
    total = jnp.sum(expo, axis=-1, keepdims=True)
    found = product(low(expo), values) / total
    return low(own_lanes(found)), own_lanes(jnp.broadcast_to(top + jnp.log(total), found.shape))


def pair_backward(query, keys, values, extra, logs, back_out):
    query, back_out = both_heads(query * SCALE), both_heads(back_out)
    logs = jnp.concatenate([logs[:, :1], logs[:, HEAD_DIM : HEAD_DIM + 1]])
    shares = jnp.exp(times_transposed(query, keys) + extra - logs)
    back_shares = times_transposed(back_out, values)
    inner = jnp.sum(shares * back_shares, axis=-1, keepdims=True)
    back_scores = low(shares * (back_shares - inner))
    back_query = own_lanes(product(back_scores, keys) * SCALE)
    back_keys = transposed_times(back_scores, query)
    back_values = transposed_times(low(shares), back_out)
    return low(back_query), low(back_keys), low(back_values), back_scores


def question_extra(slot, role_ref, qid, kid):
    shape = (qid.shape[0], kid.shape[1])
    row = lax.broadcasted_iota(jnp.int32, shape, 0) + role_ref[1 + slot]
    column = lax.broadcasted_iota(jnp.int32, shape, 1)
    extra = jnp.where((qid == kid) & (column <= row), 0.0, NEG)
    return jnp.concatenate([extra, extra])


def window_extra(bias_ref, qid, kid):
    same = jnp.where(qid == kid, 0.0, NEG)
    return jnp.concatenate([bias_ref[0] + same, bias_ref[1] + same])


def self_forward_kernel(
    role_ref, q_ref, k_ref, v_ref, bias_ref, qid_ref, kid_ref, o_ref, log_ref
):
    rows = q_ref.shape[1]

    @pl.when(role_ref[0] == 0)
    def question():
        for s in (0, 1):
            extra = question_extra(s, role_ref, qid_ref[s], kid_ref[s])
            o_ref[s], log_ref[s] = attend_pair(q_ref[s], k_ref[s], v_ref[s], extra)

    @pl.when(role_ref[0] != 0)
    def visual():
        for s in (0, 1):
            extra = window_extra(bias_ref, qid_ref[s], kid_ref[s, :, :rows])
            o_ref[s], log_ref[s] = attend_pair(
                q_ref[s], k_ref[s, :rows], v_ref[s, :rows], extra
            )


def self_backward_kernel(
    role_ref,
    q_ref,
    k_ref,
    v_ref,
    bias_ref,
    qid_ref,
    kid_ref,
    log_ref,
    back_ref,
    dq_ref,
    dk_ref,
    dv_ref,
    ds_ref,
):
    rows = q_ref.shape[1]

    @pl.when(role_ref[0] == 0)
    def question():
        ds_ref[...] = jnp.zeros_like(ds_ref)
        for s in (0, 1):
            extra = question_extra(s, role_ref, qid_ref[s], kid_ref[s])
            dq_ref[s], dk_ref[s], dv_ref[s], unused = pair_backward(
                q_ref[s], k_ref[s], v_ref[s], extra, log_ref[s], back_ref[s]
            )

    @pl.when(role_ref[0] != 0)
    def visual():
        dk_ref[...] = jnp.zeros_like(dk_ref)
        dv_ref[...] = jnp.zeros_like(dv_ref)
        for s in (0, 1):
            extra = window_extra(bias_ref, qid_ref[s], kid_ref[s, :, :rows])
            dq_ref[s], found_keys, found_values, kept = pair_backward(
                q_ref[s], k_ref[s, :rows], v_ref[s, :rows], extra, log_ref[s], back_ref[s]
            )
            dk_ref[s, :rows] = found_keys
            dv_ref[s, :rows] = found_values
            ds_ref[0, s] = kept[:rows]
            ds_ref[1, s] = kept[rows:]


def self_specs(rows, span):
    query = pl.BlockSpec((2, rows, LANES), lambda h, role: (0, 0, h))
    keys = pl.BlockSpec((2, span, LANES), lambda h, role: (0, 0, h))
    bias = pl.BlockSpec((2, rows, rows), lambda h, role: (h, 0, 0))
    qid = pl.BlockSpec((2, rows, 1), lambda h, role: (0, 0, 0))
    kid = pl.BlockSpec((2, 1, span), lambda h, role: (0, 0, 0))
    return query, keys, keys, bias, qid, kid


def self_forward(role, query, keys, values, bias, qid, kid):
    rows, span = query.shape[1], keys.shape[1]
    specs = self_specs(rows, span)
    return pl.pallas_call(
        self_forward_kernel,
        out_shape=[
            jax.ShapeDtypeStruct((2, rows, D), jnp.bfloat16),
            jax.ShapeDtypeStruct((2, rows, D), jnp.float32),
        ],
        grid_spec=pltpu.PrefetchScalarGridSpec(
            num_scalar_prefetch=1, grid=(PAIRS,), in_specs=list(specs), out_specs=[specs[0]] * 2
        ),
        compiler_params=pltpu.CompilerParams(vmem_limit_bytes=24 * MIB),
        cost_estimate=pl.CostEstimate(
            flops=16 * rows * span * D, bytes_accessed=12 * span * D, transcendentals=0
        ),
    )(role, query, keys, values, bias, qid, kid)


def self_backward(role, query, keys, values, bias, qid, kid, logs, back_out):
    rows, span = query.shape[1], keys.shape[1]
    specs = self_specs(rows, span)
    return pl.pallas_call(
        self_backward_kernel,
        out_shape=[
            jax.ShapeDtypeStruct((2, rows, D), jnp.bfloat16),
            jax.ShapeDtypeStruct((2, span, D), jnp.bfloat16),
            jax.ShapeDtypeStruct((2, span, D), jnp.bfloat16),
            jax.ShapeDtypeStruct((HEADS, 2, rows, rows), jnp.bfloat16),
        ],
        grid_spec=pltpu.PrefetchScalarGridSpec(
            num_scalar_prefetch=1,
            grid=(PAIRS,),
            in_specs=list(specs) + [specs[0]] * 2,
            out_specs=[
                specs[0],
                specs[1],
                specs[1],
                pl.BlockSpec((2, 2, rows, rows), lambda h, role: (h, 0, 0, 0)),
            ],
        ),
        compiler_params=pltpu.CompilerParams(vmem_limit_bytes=24 * MIB),
        cost_estimate=pl.CostEstimate(
            flops=40 * rows * span * D, bytes_accessed=16 * span * D, transcendentals=0
        ),
    )(role, query, keys, values, bias, qid, kid, logs, back_out)


def cross_forward_kernel(q_ref, k_ref, v_ref, extra_ref, o_ref, log_ref):
    extra = extra_ref[...]
    o_ref[0], log_ref[0] = attend_pair(q_ref[0], k_ref[0], v_ref[0], extra)


def cross_backward_kernel(
    q_ref, k_ref, v_ref, extra_ref, log_ref, back_ref, dq_ref, dk_ref, dv_ref
):
    extra = extra_ref[...]
    dq_ref[0], dk_ref[0], dv_ref[0], unused = pair_backward(
        q_ref[0], k_ref[0], v_ref[0], extra, log_ref[0], back_ref[0]
    )


def cross_specs(rows, span):
    query = pl.BlockSpec((1, rows, LANES), lambda s, h: (s, 0, h))
    keys = pl.BlockSpec((1, span, LANES), lambda s, h: (s, 0, h))
    extra = pl.BlockSpec((1, span), lambda s, h: (0, 0))
    return query, keys, keys, extra


def cross_limit(span):
    return (24 if span <= 2048 else 60) * MIB


def cross_forward(query, keys, values, extra):
    rows, span = query.shape[1], keys.shape[1]
    specs = cross_specs(rows, span)
    return pl.pallas_call(
        cross_forward_kernel,
        out_shape=[
            jax.ShapeDtypeStruct((2, rows, D), jnp.bfloat16),
            jax.ShapeDtypeStruct((2, rows, D), jnp.float32),
        ],
        grid=(2, PAIRS),
        in_specs=list(specs),
        out_specs=[specs[0]] * 2,
        compiler_params=pltpu.CompilerParams(vmem_limit_bytes=cross_limit(span)),
        cost_estimate=pl.CostEstimate(
            flops=32 * rows * span * D, bytes_accessed=8 * span * D, transcendentals=0
        ),
    )(query, keys, values, extra)


def cross_backward(query, keys, values, extra, logs, back_out):
    rows, span = query.shape[1], keys.shape[1]
    specs = cross_specs(rows, span)
    return pl.pallas_call(
        cross_backward_kernel,
        out_shape=[
            jax.ShapeDtypeStruct((2, rows, D), jnp.bfloat16),
            jax.ShapeDtypeStruct((2, span, D), jnp.bfloat16),
            jax.ShapeDtypeStruct((2, span, D), jnp.bfloat16),
        ],
        grid=(2, PAIRS),
        in_specs=list(specs) + [specs[0]] * 2,
        out_specs=[specs[0], specs[1], specs[1]],
        compiler_params=pltpu.CompilerParams(vmem_limit_bytes=cross_limit(span)),
        cost_estimate=pl.CostEstimate(
            flops=80 * rows * span * D, bytes_accessed=16 * span * D, transcendentals=0
        ),
    )(query, keys, values, extra, logs, back_out)


TILES = FF // D
HALF_ROOT = 0.5**0.5
BELL = (0.5 / 3.141592653589793) ** 0.5


def mlp_kernel(places, h_ref, g_ref, up_ref, down_ref, out_ref, back_ref, delta_ref, tile_ref):
    step = pl.program_id(0)
    far, core = step // 2, step % 2
    cut = delta_ref.shape[3]

    for place in range(places):
        for part in range(TILES):
            row = (place * TILES + part) * cut
            tile_ref[row : row + cut] = down_ref[part, place * cut : (place + 1) * cut]
    rows, branch, up, down = h_ref[...], g_ref[...], up_ref[0], tile_ref[...]
    upward = product(rows, up)
    lift = times_transposed(branch, down)
    chance = 0.5 * (1.0 + lax.erf(upward * HALF_ROOT))
    active = low(upward * chance)
    slope = chance + upward * jnp.exp(-0.5 * upward * upward) * BELL
    back_up = low(slope * lift)
    out, back = product(active, down), times_transposed(back_up, up)

    @pl.when(step == 0)
    def start():
        out_ref[...] = out
        back_ref[...] = back

    @pl.when(step > 0)
    def add():
        out_ref[...] += out
        back_ref[...] += back

    delta_up = low(transposed_times(rows, back_up))
    for side in range(2):
        for place in range(2 * places):
            row = (side * 2 * places + place) * cut
            delta_ref[place, step, side] = delta_up[row : row + cut]
    delta_down = low(transposed_times(active, branch))
    for place in range(places):
        for part in range(TILES):
            row = (place * TILES + part) * cut
            delta_ref[core * places + place, TILES + part, far] = delta_down[row : row + cut]


def mlp(rows, branch, weights, blocks):
    count = rows.shape[0]
    cut = D // (4 * blocks)
    resident = pl.BlockSpec((count, D), lambda i: (0, 0))
    shape = (2 * blocks, 2 * TILES, 2, cut, D)
    return pl.pallas_call(
        functools.partial(mlp_kernel, blocks),
        out_shape=[
            jax.ShapeDtypeStruct((count, D), jnp.float32),
            jax.ShapeDtypeStruct((count, D), jnp.float32),
            jax.ShapeDtypeStruct(shape, jnp.bfloat16),
        ],
        grid=(TILES,),
        in_specs=[
            resident,
            resident,
            pl.BlockSpec((1, D, D), lambda i: (4 + i, 0, 0)),
            pl.BlockSpec((TILES, D // TILES, D), lambda i: (2, i, 0)),
        ],
        out_specs=[resident, resident, pl.BlockSpec(shape, lambda i: (0, 0, 0, 0, 0))],
        scratch_shapes=[pltpu.VMEM((D, D), jnp.bfloat16)],
        compiler_params=pltpu.CompilerParams(vmem_limit_bytes=48 * MIB),
        cost_estimate=pl.CostEstimate(
            flops=12 * count * D * FF, bytes_accessed=8 * D * FF, transcendentals=0
        ),
    )(rows, branch, weights, weights)


def weight_kernel(places, *refs):
    delta_ref = refs[-1]
    cut = delta_ref.shape[3]
    for number in range(len(refs) // 2):
        delta = low(transposed_times(refs[2 * number][...], refs[2 * number + 1][...]))
        for place in range(places):
            delta_ref[place, number, 0] = delta[place * cut : (place + 1) * cut]


def weight_gradients(pairs, blocks):
    cut = D // (4 * blocks)
    total = sum(rows.shape[0] for rows, unused in pairs)
    if total > 8 * D:
        parts = [low(transposed_times(rows, back)) for rows, back in pairs]
        parts = jnp.stack([part.reshape(2, 2 * blocks, cut, D) for part in parts])
        return parts.transpose(2, 0, 1, 3, 4)
    specs, arrays = [], []
    for rows, back in pairs:
        specs.append(pl.BlockSpec((rows.shape[0], D // 2), lambda i: (0, i)))
        specs.append(pl.BlockSpec(back.shape, lambda i: (0, 0)))
        arrays += [rows, back]
    return pl.pallas_call(
        functools.partial(weight_kernel, 2 * blocks),
        out_shape=jax.ShapeDtypeStruct((2 * blocks, len(pairs), 2, cut, D), jnp.bfloat16),
        grid=(2,),
        in_specs=specs,
        out_specs=pl.BlockSpec(
            (2 * blocks, len(pairs), 1, cut, D), lambda i: (0, 0, i, 0, 0)
        ),
        compiler_params=pltpu.CompilerParams(vmem_limit_bytes=32 * MIB),
        cost_estimate=pl.CostEstimate(
            flops=2 * total * D * D, bytes_accessed=4 * total * D, transcendentals=0
        ),
    )(*arrays)


def body(
    visual_in,
    question_in,
    segment_ids,
    regions,
    rel_index,
    rel_table,
    window_project,
    window_output,
    causal_project,
    causal_output,
    reader_query,
    reader_pair,
    reader_output,
    viewer_query,
    viewer_pair,
    viewer_output,
    visual_up,
    visual_down,
    question_up,
    question_down,
    norm_gains,
    norm_shifts,
    visual_cot,
    question_cot,
):
    blocks = lax.axis_size("blk")
    ringed = blocks == 8
    share = Q_LEN // blocks
    rows = visual_in.shape[0]
    far, core, blk = lax.axis_index("far"), lax.axis_index("core"), lax.axis_index("blk")
    asks = far == 0
    seat = ring_seat(blk, blocks)
    early = -(-(LONGEST - 1) // share)
    reach = min(Q_LEN, share * (early + 1))
    span = reach + rows - share
    turns = (seat, blocks - 1 - seat)
    firsts = [jnp.clip((turn - early) * share, 0, Q_LEN - reach) for turn in turns]
    insets = [jnp.where(far == 0, turn * share - at, 0) for turn, at in zip(turns, firsts)]
    turn = jnp.where(far == 0, turns[0], turns[1])
    first = jnp.where(far == 0, firsts[0], firsts[1])
    role = jnp.stack([far] + insets).astype(jnp.int32)
    cut = D // (4 * blocks)

    def own_of(question_side, visual_side):
        return jnp.where(asks, question_side, visual_side)

    class Trade(Once):
        def __init__(self, question_side, visual_side):
            self.kept = own_of(question_side, visual_side)
            self.away = own_of(visual_side, question_side)

        def begin(self):
            self.coming = swap_far(self.away)

        def send(self):
            return self.coming if hasattr(self, "coming") else swap_far(self.away)

        def receive(self, got):
            self.found = jnp.stack([own_of(self.kept, got), own_of(got, self.kept)])

    def pad_rows(values, total):
        return jnp.pad(values, ((0, total - values.shape[0]),) + ((0, 0),) * (values.ndim - 1))

    def block_of(flat, columns):
        return flat.reshape(-1, columns)

    def cross_squares(query, pair, out):
        pair = pair.reshape(cut, 2, D).transpose(1, 0, 2)
        return jnp.concatenate([query.reshape(1, cut, D), pair, out.reshape(1, cut, D)])

    def mlp_squares(up, down):
        up = up.reshape(cut, TILES, D).transpose(1, 0, 2)
        return jnp.concatenate([up, down.reshape(TILES, cut, D)])

    def matrices(ring, splits):
        if ringed:
            other = {key: swap_core(item) for key, item in ring.pieces.items()}
            return assemble(ring.pieces, other, splits, core, seat, blocks)
        here = lax.all_gather(ring, "blk", axis=0)
        there = swap_core(here)
        pair = jnp.where(core == 0, jnp.stack([here, there]), jnp.stack([there, here]))
        whole = pair.transpose(2, 0, 1, 3, 4).reshape(4 * blocks * ring.shape[1], -1)
        places = [sum(splits[:i]) for i in range(len(splits))]
        return [whole[:, at : at + width] for at, width in zip(places, splits)]

    def ring_of(own):
        return Gather(own) if ringed else own

    def step(rings, transfers=(), work=()):
        return phase((list(rings) if ringed else []) + list(transfers), work)

    norms = jnp.pad(jnp.concatenate([norm_gains, norm_shifts]), (0, cut * LANES - 2 * norm_gains.size))
    norms = norms.reshape(cut, LANES)
    self_shards = Trade(
        jnp.concatenate([block_of(causal_project, 3 * D), block_of(causal_output, D), norms], 1),
        jnp.concatenate([block_of(window_project, 3 * D), block_of(window_output, D), norms], 1),
    )
    cross_shards = Trade(
        cross_squares(reader_query, reader_pair, reader_output),
        cross_squares(viewer_query, viewer_pair, viewer_output),
    )
    cross_shards.kept, cross_shards.away = phase([self_shards], (cross_shards.kept, cross_shards.away))
    self_ring = ring_of(self_shards.found)
    mlp_shards = Trade(mlp_squares(question_up, question_down), mlp_squares(visual_up, visual_down))
    mlp_shards.kept, mlp_shards.away = step(
        [self_ring], [cross_shards], (mlp_shards.kept, mlp_shards.away)
    )
    row_shards = Trade(
        pad_rows(lax.dynamic_slice_in_dim(question_in, first, reach, 0), span),
        pad_rows(visual_in, span),
    )
    marks = Trade(segment_ids[0], jnp.pad(regions, (0, Q_LEN - rows)))
    cot = Trade(
        pad_rows(lax.dynamic_slice_in_dim(question_cot, turn * share, share, 0), rows), visual_cot
    )
    row_shards.away, later = step([self_ring], [mlp_shards], (row_shards.away, cross_shards.found))
    row_shards.begin()
    later = jnp.concatenate([later, mlp_shards.found], 1)
    later = later.transpose(1, 0, 2, 3).reshape(-1, cut, D)
    later = lax.all_gather(later, ("core", "blk"), axis=1, tiled=True).reshape(-1, D, D)
    row_shards.away = step([self_ring], [marks], row_shards.away)
    bias = window_bias(role, rel_table, rel_index, 0, 1)
    bias = step([self_ring], [row_shards], bias)[:, :HEADS].transpose(1, 0, 2)
    slots, marks = row_shards.found, marks.found

    def of_slots(values, starts, size):
        return jnp.stack(
            [lax.dynamic_slice_in_dim(values[i], start, size, 0) for i, start in enumerate(starts)]
        )

    key_marks = own_of(
        jnp.pad(
            of_slots(marks, firsts, reach), ((0, 0), (0, span - reach)), constant_values=-2
        ),
        marks[:, :span],
    )[:, None, :]
    row_marks = own_of(
        jnp.pad(
            of_slots(marks, [turn * share for turn in turns], share),
            ((0, 0), (0, rows - share)),
            constant_values=-1,
        ),
        marks[:, :rows],
    )[:, :, None]
    self_weights = matrices(self_ring, (D, D, D, D, LANES))
    self_query_weight, self_key_weight, self_value_weight, self_exit, norm_rows = self_weights
    norm_flat = norm_rows.reshape(4 * blocks, -1)[:, : 2 * norm_gains.size].astype(jnp.float32)
    gains = norm_flat[:, : norm_gains.size].reshape(6, D)
    shifts = norm_flat[:, norm_gains.size :].reshape(6, D)

    own = of_slots(slots, insets, rows).astype(jnp.float32)
    self_gain, self_shift = own_of(gains[1], gains[0]), own_of(shifts[1], shifts[0])
    self_norm, self_pull = jax.vjp(normalize, own, self_gain, self_shift)
    self_low = low(self_norm).reshape(2 * rows, D)
    every_low = low(normalize(slots.astype(jnp.float32), self_gain, self_shift))
    every_low = every_low.reshape(2 * span, D)
    self_query = low(product(self_low, self_query_weight)).reshape(2, rows, D)
    self_keys = low(product(every_low, self_key_weight)).reshape(2, span, D)
    self_values = low(product(every_low, self_value_weight)).reshape(2, span, D)
    self_attn, self_logs = self_forward(
        role, self_query, self_keys, self_values, bias, row_marks, key_marks
    )
    self_attn = self_attn.reshape(2 * rows, D)
    rows_one = own + product(self_attn, self_exit).reshape(2, rows, D)

    cross_gain, cross_shift = own_of(gains[2], gains[3]), own_of(shifts[2], shifts[3])
    cross_norm, cross_pull = jax.vjp(normalize, rows_one, cross_gain, cross_shift)
    cross_low = low(cross_norm)
    sent = Once(lambda: swap_far(cross_low))
    phase([sent])
    cross_weights = lax.optimization_barrier([later[i] for i in range(4)])
    cross_query_weight, cross_key_weight, cross_value_weight, cross_exit = cross_weights
    cross_query = low(product(cross_low.reshape(2 * rows, D), cross_query_weight))
    cross_query = cross_query.reshape(2, rows, D)
    source_ring = ring_of(sent.found)
    if ringed:
        for number in range(4):
            phase([source_ring] + ([cot] if number == 0 else []))
        pieces = [source_ring.pieces[k] for k in OFFSETS[:-1]]
        pieces.append(jnp.concatenate([source_ring.pieces["first"], source_ring.pieces["second"]]))
        sources = jnp.concatenate(pieces, axis=1)
    else:
        phase([cot])
        sources = lax.all_gather(sent.found, "blk", axis=1, tiled=True)
    sources = sources.reshape(-1, D)
    cot = cot.found
    column = jnp.arange(blocks * rows) % rows
    cross_extra = own_of(0.0, jnp.where(column < share, 0.0, NEG))[None]
    cross_keys = low(product(sources, cross_key_weight)).reshape(2, -1, D)
    cross_values = low(product(sources, cross_value_weight)).reshape(2, -1, D)
    cross_attn, cross_logs = cross_forward(cross_query, cross_keys, cross_values, cross_extra)
    cross_attn = cross_attn.reshape(2 * rows, D)
    rows_two = rows_one + product(cross_attn, cross_exit).reshape(2, rows, D)

    mlp_gain, mlp_shift = own_of(gains[5], gains[4]), own_of(shifts[5], shifts[4])
    mlp_norm, mlp_pull = jax.vjp(normalize, rows_two, mlp_gain, mlp_shift)
    mlp_low = low(mlp_norm).reshape(2 * rows, D)
    mlp_out, back_mlp, mlp_delta = mlp(mlp_low, cot.reshape(2 * rows, D), later, blocks)
    rows_three = rows_two + mlp_out.reshape(2, rows, D)
    back_mlp_in, gain_mlp, shift_mlp = mlp_pull(back_mlp.reshape(2, rows, D))
    back_two = cot.astype(jnp.float32) + back_mlp_in
    mlp_delta = mlp_delta.reshape(2, blocks, -1, D)

    class Shares:
        def __init__(self, delta):
            self.delta = delta
            self.swap = Once(
                lambda: swap_core(lax.dynamic_index_in_dim(delta, 1 - core, 0, keepdims=False))
            )

        def start(self):
            if ringed:
                self.ring = Sum(self.chunk)
            else:
                kept = lax.dynamic_index_in_dim(self.delta, core, 0, keepdims=False)
                kept = kept.astype(jnp.float32) + self.swap.found.astype(jnp.float32)
                self.sum = lax.psum_scatter(kept, "blk", scatter_dimension=0, tiled=True)[0]

        def chunk(self, k):
            place = ring_place(seat + k, blocks)
            mine = lax.dynamic_slice(self.delta, (core, place, 0, 0), (1, 1) + self.delta.shape[2:])
            theirs = lax.dynamic_index_in_dim(self.swap.found, place, 0, keepdims=False)
            mine = mine.reshape(theirs.shape)
            return mine.astype(jnp.float32) + theirs.astype(jnp.float32)

        def rings(self):
            return [self.ring] if ringed else []

        def total(self):
            found = self.ring.total if ringed else self.sum
            return found.reshape(-1, 2, cut, D).transpose(1, 0, 2, 3)

    mlp_shares = Shares(mlp_delta)
    class Owners(Once):
        def __init__(self, total):
            self.total = total

        def send(self):
            return swap_far(low(own_of(self.total[1], self.total[0])))

        def receive(self, came):
            mine = own_of(self.total[0], self.total[1]).astype(jnp.float32)
            came = came.astype(jnp.float32)
            self.found = own_of(mine, came), own_of(came, mine)

    class Home(Once):
        def __init__(self, values):
            self.values = values

        def send(self):
            return swap_far(own_of(self.values[1], self.values[0]))

        def receive(self, got):
            kept = own_of(self.values[0], self.values[1])
            self.found = own_of(kept, got)[:share], own_of(got, kept)

    home_out = Home(low(rows_three))

    cross_branch = low(back_two).reshape(2 * rows, D)
    back_attn = low(times_transposed(cross_branch, cross_exit)).reshape(2, rows, D)
    back_attn = phase([mlp_shares.swap], back_attn)
    mlp_shares.start()
    back_query, back_keys, back_values = phase(
        mlp_shares.rings(),
        cross_backward(cross_query, cross_keys, cross_values, cross_extra, cross_logs, back_attn),
    )
    back_query = back_query.reshape(2 * rows, D)
    back_keys, back_values = back_keys.reshape(-1, D), back_values.reshape(-1, D)
    back_sources = times_transposed(back_keys, cross_key_weight)
    back_sources = back_sources + times_transposed(back_values, cross_value_weight)
    back_sources = phase(mlp_shares.rings(), back_sources.reshape(2, -1, D))

    def owned(delta):
        delta = delta.reshape(2 * blocks, -1, D)
        return lax.psum_scatter(delta, ("core", "blk"), scatter_dimension=0, tiled=True)

    cross_pairs = [
        (cross_low.reshape(2 * rows, D), back_query),
        (sources, back_keys),
        (sources, back_values),
        (cross_attn, cross_branch),
    ]
    if ringed:

        def source_chunk(k):
            at = OFFSETS.index(k) * rows
            return back_sources[:, at : at + rows].reshape(2 * rows, D)

        back_sent = Sum(source_chunk)
        cross_delta = weight_gradients(cross_pairs, blocks)
        back_cross = times_transposed(back_query, cross_query_weight).reshape(2, rows, D)
        ready = mlp_shares.ring
        works = [back_cross, cross_delta, ready.state, ()]
        extra = [[home_out], [], [], []]
        works = [phase([back_sent] + more, work) for work, more in zip(works, extra)]
        back_cross, cross_delta, ready.state = works[:3]
        cross_delta = owned(cross_delta)
        back_sent = back_sent.total.reshape(2, rows, D)
    else:
        back_sent = lax.psum_scatter(back_sources, "blk", scatter_dimension=1, tiled=True)
        phase([home_out])
        cross_delta = owned(weight_gradients(cross_pairs, blocks))
        back_cross = times_transposed(back_query, cross_query_weight).reshape(2, rows, D)
    returned = Once(lambda: swap_far(low(back_sent)))
    phase([returned] + mlp_shares.rings())
    back_cross = back_cross + returned.found.astype(jnp.float32)
    back_cross_in, gain_cross, shift_cross = cross_pull(back_cross)
    back_one = back_two + back_cross_in

    self_branch = low(back_one).reshape(2 * rows, D)
    back_attn = low(times_transposed(self_branch, self_exit)).reshape(2, rows, D)
    back_query, back_keys, back_values, back_scores = phase(
        mlp_shares.rings(),
        self_backward(
            role,
            self_query,
            self_keys,
            self_values,
            bias,
            row_marks,
            key_marks,
            self_logs,
            back_attn,
        ),
    )
    back_query = back_query.reshape(2 * rows, D)
    back_keys, back_values = back_keys.reshape(2 * span, D), back_values.reshape(2 * span, D)
    back_every = times_transposed(back_keys, self_key_weight)
    back_every = back_every + times_transposed(back_values, self_value_weight)
    back_every = back_every.reshape(2, span, D)
    back_self = times_transposed(back_query, self_query_weight).reshape(2, rows, D)

    def for_earlier(j):
        parts = []
        for slot in (0, 1):
            at = jnp.maximum(insets[slot] - j * share, 0)
            found = lax.dynamic_slice_in_dim(back_every[slot], at, share, 0)
            parts.append(jnp.where(asks & (turns[slot] >= j), found, 0.0))
        return parts

    class Chain(Ring):
        def __init__(self):
            self.left = early
            self.set(for_earlier(early))

        def set(self, total):
            self.total = total
            self.state = low(total[1]), low(total[0])

        def receive(self, found):
            self.left -= 1
            own = for_earlier(self.left)
            self.set([found[1].astype(jnp.float32) + own[0], found[0].astype(jnp.float32) + own[1]])

    chain = Chain()
    chain.state, back_query, back_keys, back_values = lax.optimization_barrier(
        (chain.state, back_query, back_keys, back_values)
    )
    self_pairs = [
        (self_low, back_query),
        (every_low, back_keys),
        (every_low, back_values),
        (self_attn, self_branch),
    ]
    self_delta = weight_gradients(self_pairs, blocks).reshape(2, blocks, 8 * cut, D)
    question_rows, visual_out = home_out.found
    outs = [Gather(question_rows)] if ringed else []
    score_rows = back_scores.reshape(2 * HEADS, WIN, WIN).transpose(1, 0, 2)
    table_parts = [table_sums(role, score_rows, rel_index, part, 4) for part in range(4)]
    self_delta, table_parts[0] = phase([chain] + outs, (self_delta, table_parts[0]))
    self_shares = Shares(self_delta)
    table_parts[1] = phase([chain, self_shares.swap] + outs, table_parts[1])
    self_shares.start()
    sums = self_shares.rings()
    for number in range(early - 2):
        work = table_parts[2 + number] if number < 2 else ()
        if number == 0:
            work, cross_delta = lax.optimization_barrier((work, cross_delta))
        work = phase([chain] + (outs + sums if number < 2 else []), work)
        if number < 2:
            table_parts[2 + number] = work
    table_part = sum(table_parts).reshape(HEADS, 2, RELS_PAD)
    table_part = jnp.sum(table_part, axis=1)[:, :RELS]
    back_self = back_self + own_of(
        jnp.pad(jnp.stack(chain.total), ((0, 0), (0, rows - share), (0, 0))), back_every[:, :rows]
    )
    back_self_in, gain_self, shift_self = self_pull(back_self)
    back_in = back_one + back_self_in

    blank = jnp.zeros((D,), jnp.float32)
    gain_delta = [
        own_of(blank, gain_self),
        own_of(gain_self, blank),
        own_of(gain_cross, blank),
        own_of(blank, gain_cross),
        own_of(blank, gain_mlp),
        own_of(gain_mlp, blank),
    ]
    shift_delta = [
        own_of(blank, shift_self),
        own_of(shift_self, blank),
        own_of(shift_cross, blank),
        own_of(blank, shift_cross),
        own_of(blank, shift_mlp),
        own_of(shift_mlp, blank),
    ]
    small = jnp.concatenate(gain_delta + shift_delta + [table_part.reshape(-1)])
    size = small.size
    small = jnp.pad(small, (0, LANES * LANES - size)).reshape(LANES, LANES)

    class Everywhere:
        def __init__(self, total):
            self.total, self.bit = total, 0
            self.bits = [("far", 1, 2)]
            self.bits += [("blk", 1 << i, blocks) for i in range(blocks.bit_length() - 1)]
            self.bits += [("core", 1, 2)]

        def send(self):
            axis, bit, count = self.bits[self.bit]
            return lax.ppermute(self.total, axis, [(i, i ^ bit) for i in range(count)])

        def receive(self, found):
            self.total, self.bit = self.total + found, self.bit + 1

    small = Everywhere(small)
    home_back = Home(low(back_in))
    mlp_sums = Owners(mlp_shares.total())
    phase([home_back, mlp_sums, small] + sums)
    cross_sums = Owners(cross_delta.reshape(4, 2, cut, D).transpose(1, 0, 2, 3))
    question_back, visual_back = home_back.found
    if ringed:
        back_ring = Gather(question_back)
        phase([back_ring, small] + sums)
    self_sums = Owners(self_shares.total())
    if ringed:
        for number in range(3):
            phase([back_ring, small] + [[], [cross_sums], [self_sums]][number])
        question_delta = seats_in_order(back_ring, far, seat, blocks, jnp.float32)
        question_out = seats_in_order(outs[0], far, seat, blocks, jnp.bfloat16)
    else:
        both = jnp.stack([question_rows, question_back])
        both = lax.all_gather(both, "blk", axis=0)
        order = ring_order(blocks)
        both = own_of(
            jnp.concatenate([both[i] for i in order], 1),
            jnp.concatenate([both[i] for i in order[::-1]], 1),
        )
        question_out, question_delta = both[0], both[1].astype(jnp.float32)
        phase([cross_sums, self_sums])
    while small.bit < len(small.bits):
        phase([small])
    small = small.total.reshape(-1)
    at = ((2 * far + core) * blocks + blk) * norm_gains.size
    delta_gains = lax.dynamic_slice_in_dim(small, at, norm_gains.size, 0)
    delta_shifts = lax.dynamic_slice_in_dim(small, 6 * D + at, norm_gains.size, 0)
    table_delta = small[12 * D : size].reshape(HEADS, RELS)
    question_shift = small[11 * D : 12 * D]

    def joined(side, start, stop):
        return side[start:stop].transpose(1, 0, 2).reshape(-1)

    causal, window = [[joined(side, 0, 3), joined(side, 3, 4)] for side in self_sums.found]
    reader, viewer = [
        [joined(side, 0, 1), joined(side, 1, 3), joined(side, 3, 4)] for side in cross_sums.found
    ]
    question_mlp, visual_mlp = [
        [joined(side, 0, TILES), side[TILES:].reshape(-1)] for side in mlp_sums.found
    ]
    return (
        visual_out,
        question_out,
        visual_back.astype(jnp.float32),
        question_delta,
        table_delta,
        window[0],
        window[1],
        causal[0],
        causal[1],
        reader[0],
        reader[1],
        reader[2],
        viewer[0],
        viewer[1],
        viewer[2],
        visual_mlp[0],
        visual_mlp[1],
        question_mlp[0],
        question_mlp[1],
        delta_gains,
        delta_shifts,
        question_shift,
    )


def solution(mesh):
    pages, blocks = mesh.devices.shape
    cut = jax.sharding.Mesh(
        mesh.devices.reshape(2, pages // 2, blocks), ("far", "core", "blk")
    )
    flat, whole, by_page = P(("far", "core", "blk")), P(), P(("far", "core"), None)
    split = P(("far", "core", "blk"), None)
    in_specs = (split, by_page, by_page, flat, whole, whole) + (flat,) * 16 + (split, by_page)
    out_specs = (split, by_page, split, by_page, whole) + (flat,) * 16 + (whole,)
    return jax.shard_map(body, mesh=cut, in_specs=in_specs, out_specs=out_specs, check_vma=False)
```
